32 devices in a mesh: row: 4 (over x, core), col: 8 (over z, y).
Axes of the slice: x: 2, y: 2, z: 4, core: 2. Of those that a mesh axis runs over, the one named last changes fastest.
Arguments:
- embeddings: float32 [16384, 1024], P(('row', 'col')), may hold values from -6 to 6
- dest_pos: int32 [16384], P(('row', 'col')), may hold values from 0 to 16383, as said below
- cluster_ids: int32 [4, 4096], P('row', 'col'), may hold values from 0 to 7, as said below
Outputs:
- best_match: float32 [4, 4096], P('row', 'col')
The draws below stay inside these ranges and needn't reach their ends.
Inputs may be any that keep to these rules, and one draw needn't show every extreme that they name: dest_pos is a permutation; of the 512 rows stored on one device at most 32 have positions in one device's block of 512 positions, and exactly 32 for some pairs of devices. In each group cluster_ids never falls along the positions; every cluster holds 102 to 2560 positions, and one cluster of each group exactly 2560.
All inputs are finite; a program needn't handle non-finite values.
Results may differ from the reference program's by a relative error of at most 0.0013.
Values may be sent and summed in bfloat16 or wider, within the bound.
No kernel may reach another device: no remote copies, remote signals or barrier semaphores. Data moves between devices by JAX's collectives and lax.ppermute only.
A program may use at most 64 MiB of HBM per device.

```python
import jax
import jax.numpy as jnp
from jax import lax

E = 1024
ROWS_DEV = 512
CAP = 32
GROUP = 4096
MEMBERS = 16384
CLUSTERS = 8
MOST = 2560
SMALLEST = 102
N_ROW = 4
N_COL = 8


def draw_dest_pos(key, part):
    key = jax.random.fold_in(key, 7)
    devs = N_ROW * N_COL
    key_order, key_source, key_target = jax.random.split(key, 3)
    slots = devs * CAP
    first = devs // 2
    order = jax.random.permutation(key_order, slots)
    slot_offset = jnp.arange(slots, dtype=jnp.int32) // CAP
    ranking = jnp.where(slot_offset == first, order - slots, order)
    chosen = jnp.argsort(ranking)[:ROWS_DEV]
    offsets = slot_offset[chosen]
    source_perm = jax.vmap(lambda k: jax.random.permutation(k, ROWS_DEV))(jax.random.split(key_source, devs))
    target_perm = jax.vmap(lambda k: jax.random.permutation(k, ROWS_DEV))(jax.random.split(key_target, devs))
    sources = jnp.arange(devs, dtype=jnp.int32)[:, None]
    target = (sources + offsets[source_perm]) % devs
    places = target_perm[target, source_perm]
    return (target * ROWS_DEV + places).reshape(-1).astype(jnp.int32)


def one_group_ids(key):
    key_weight, key_order = jax.random.split(key, 2)
    others = CLUSTERS - 1
    extra = GROUP - MOST - others * SMALLEST
    powers = jax.random.randint(key_weight, (others,), 0, 8)
    weights = jnp.left_shift(jnp.ones((others,), jnp.int32), powers)
    shares = extra * weights // jnp.sum(weights)
    shares = shares.at[0].add(extra - jnp.sum(shares))
    sizes = jnp.concatenate([jnp.full((1,), MOST, jnp.int32), SMALLEST + shares]).astype(jnp.int32)
    sizes = sizes[jax.random.permutation(key_order, CLUSTERS)]
    ends = jnp.cumsum(sizes)[:-1]
    positions = jnp.arange(GROUP, dtype=jnp.int32)
    return jnp.sum((positions[:, None] >= ends[None, :]).astype(jnp.int32), axis=1).astype(jnp.int32)


def draw_cluster_ids(key, part):
    key = jax.random.fold_in(key, 11)
    return jax.vmap(one_group_ids)(jax.random.split(key, N_ROW)).astype(jnp.int32)


def block_scale(rng, dims, cuts, smallest, high):
    loudness = 1.0
    for dim, blocks in cuts:
        draws = jax.random.uniform(jax.random.fold_in(jax.random.fold_in(rng, 6), dim), (blocks,), jnp.float32, smallest / len(cuts), high / len(cuts))
        loudness = loudness * jnp.repeat(jnp.exp(draws), dims[dim] // blocks).reshape((-1,) + (1,) * (len(dims) - 1 - dim))
    return loudness


def centred(rng, dims, spread, limit, shards=(), held_as=jnp.bfloat16):
    array = spread * jax.random.normal(rng, dims, jnp.float32)
    if shards:
        array = array * block_scale(rng, dims, shards, -0.22, 0.18)
    return jnp.clip(array, -limit, limit).astype(held_as)


def setup_inputs(seed: int = 0) -> dict:
    key_list = jax.random.split(jax.random.key(seed), 4)
    embeddings = centred(key_list[0], (MEMBERS, E), 1.0, 6.0, ((0, 32),), jnp.float32)
    dest_pos = draw_dest_pos(jax.random.fold_in(key_list[3], 71), 0)
    cluster_ids = draw_cluster_ids(jax.random.fold_in(key_list[3], 71), 0)
    return {"embeddings": embeddings, "dest_pos": dest_pos, "cluster_ids": cluster_ids}


def normalize(rows):
    scale = lax.rsqrt(lax.optimization_barrier(jnp.sum(rows * rows, axis=1, keepdims=True)) + 1e-06)
    return (rows * scale).astype(jnp.bfloat16)

def group_best(rows, labels):
    block = min(512, GROUP)
    count = GROUP // block
    blocks = rows.reshape(count, block, E)
    block_labels = labels.reshape(count, block)
    places = jnp.arange(GROUP, dtype=jnp.int32).reshape(count, block)
    columns = jnp.arange(GROUP, dtype=jnp.int32)

    def one_block(item):
        left, left_labels, left_places = item
        sims = jnp.dot(left, rows.T, preferred_element_type=jnp.float32)
        keep = (left_labels[:, None] == labels[None, :]) & (left_places[:, None] != columns[None, :])
        return lax.optimization_barrier(jnp.max(jnp.where(keep, sims, jnp.float32(-1.0)), axis=1))
    return lax.map(one_block, (blocks, block_labels, places)).reshape(GROUP)

def reference(embeddings, dest_pos, cluster_ids):
    unit = normalize(embeddings)
    sorted_units = jnp.zeros((MEMBERS, E), jnp.bfloat16).at[dest_pos].set(unit)
    sorted_units = sorted_units.reshape(N_ROW, GROUP, E)
    results = [group_best(sorted_units[g], cluster_ids[g]) for g in range(N_ROW)]
    return jnp.stack(results)
```

```python
import functools
import itertools

import jax
import jax.numpy as jnp
import numpy as np
from jax import lax
from jax.experimental import pallas as pl
from jax.experimental.pallas import tpu as pltpu
from jax.sharding import PartitionSpec as P

AXES = ("row", "col")
LEVELS = 16
NT = (((1,), (1,)), ((), ()))
VMEM = pl.BlockSpec(memory_space=pltpu.VMEM)


def kernel_params(mebibytes):
    return pltpu.CompilerParams(vmem_limit_bytes=mebibytes * 2**20)


def plane_plan(n_row, wide):
    n = n_row * wide
    if n_row == 4 and wide == 2:
        chips = [(0, 0), (0, 1), (1, 1), (1, 0)]

        def dev(chip, core):
            x, y = chips[chip % 4]
            return (x * 2 + core) * wide + y

        held = np.zeros((4, n), np.int64)
        for chip, core in itertools.product(range(4), range(2)):
            i = dev(chip, core)
            crossed = 1 - core if chip in (1, 2) else core
            held[:, i] = i, dev(chip, 1 - core), dev(chip + 1, core), dev(chip + 3, crossed)
        pairs = [(0, 0), (0, 1), (0, 2), (1, 2), (2, 3)]
    else:
        def covered(cover):
            return {(b - a) % n for a in cover for b in cover}

        size = 1
        while True:
            found = [c for c in itertools.combinations(range(n), size) if c[0] == 0 and len(covered(c)) == n]
            if found:
                break
            size += 1
        cover = found[0]
        held = (np.arange(n)[None, :] + np.array(cover)[:, None]) % n
        pairs, seen = [], set()
        for j, k in itertools.combinations_with_replacement(range(size), 2):
            delta = (cover[k] - cover[j]) % n
            if delta not in seen:
                seen |= {delta, (n - delta) % n}
                pairs.append((j, k))
    met = set()
    for j, k in pairs:
        for i in range(n):
            met |= {(held[j, i], held[k, i]), (held[k, i], held[j, i])}
    assert len(met) == n * n
    return held, pairs


def write_chunks(slot, unit, cap, chunk_refs, numbers):
    for ref, k in zip(chunk_refs, numbers):
        index = lax.broadcasted_iota(jnp.int32, (cap, unit.shape[0]), 0) + k * cap
        pick = (index == slot).astype(jnp.bfloat16)
        ref[...] = jnp.dot(pick, unit, preferred_element_type=jnp.float32).astype(jnp.bfloat16)


def unit_kernel(groups, cap, group_size, numbers, plane_ref, dest_ref, emb_ref, unit_ref, slot_ref, *chunk_refs):
    rows_dev = emb_ref.shape[0]
    dest = dest_ref[...]
    group = jnp.zeros_like(dest)
    for g in range(1, groups):
        group += (dest >= g * group_size).astype(jnp.int32)
    group = jnp.bitwise_xor(group, plane_ref[0])
    pad = -(-groups // 16) * 16
    member = lax.broadcasted_iota(jnp.int32, (pad, rows_dev), 0) == group
    earlier = lax.broadcasted_iota(jnp.int32, (rows_dev, rows_dev), 0) < lax.broadcasted_iota(
        jnp.int32, (rows_dev, rows_dev), 1
    )
    before = jnp.dot(member.astype(jnp.bfloat16), earlier.astype(jnp.bfloat16), preferred_element_type=jnp.float32)
    rank = jnp.sum(jnp.where(member, before, 0.0), axis=0, keepdims=True).astype(jnp.int32)
    slot = jnp.where(rank < cap, group * cap + rank, groups * cap)
    slot_ref[...] = slot
    x = emb_ref[...]
    unit = (x * lax.rsqrt(jnp.sum(x * x, axis=1, keepdims=True) + 1e-06)).astype(jnp.bfloat16)
    unit_ref[...] = unit
    write_chunks(slot, unit, cap, chunk_refs, numbers)


def rest_kernel(groups, cap, group_size, numbers, dest_ref, slot_ref, unit_ref, place_ref, *chunk_refs):
    rows_dev = unit_ref.shape[0]
    slot = slot_ref[...]
    write_chunks(slot, unit_ref[...], cap, chunk_refs, numbers)
    dest = dest_ref[...]
    place = dest
    for g in range(1, groups):
        place -= jnp.where(dest >= g * group_size, group_size, 0)
    high = lax.shift_right_logical(place, 7)
    low = jnp.bitwise_and(place, 127)
    kind = lax.broadcasted_iota(jnp.int32, (16, rows_dev), 0)
    facts = jnp.where(kind == 0, high, jnp.where(kind == 1, low, jnp.where(kind == 2, 1, 0)))
    facts = facts.astype(jnp.float32).astype(jnp.bfloat16)
    pick = (lax.broadcasted_iota(jnp.int32, (groups * cap, rows_dev), 0) == slot).astype(jnp.bfloat16)
    got = lax.dot_general(facts, pick, NT, preferred_element_type=jnp.float32).astype(jnp.int32)
    there = got[2:3, :] > 0
    place_ref[...] = jnp.where(there, got[0:1, :] * 128 + got[1:2, :], group_size)


class Best:
    def __init__(self, start):
        self.row, self.column = start, None

    def add_row(self, row):
        self.row = jnp.maximum(self.row, row)

    def add_column(self, column):
        self.column = column if self.column is None else jnp.maximum(self.column, column)

    def as_row(self):
        if self.column is None:
            return self.row
        n = self.column.shape[0]
        eye = lax.broadcasted_iota(jnp.int32, (n, n), 0) == lax.broadcasted_iota(jnp.int32, (n, n), 1)
        return jnp.maximum(self.row, jnp.max(jnp.where(eye, self.column, -1.0), axis=0, keepdims=True))


def similar(left, right, left_label, right_label, shift=None):
    sims = lax.dot_general(left, right, NT, preferred_element_type=jnp.float32)
    keep = left_label == right_label
    if shift is not None:
        keep &= lax.broadcasted_iota(jnp.int32, sims.shape, 0) != lax.broadcasted_iota(jnp.int32, sims.shape, 1) + shift
    return jnp.where(keep, sims, -1.0)


def row_max(sims):
    return jnp.max(sims, axis=1, keepdims=True)


def column_max(sims):
    return jnp.max(sims, axis=0, keepdims=True)


def loader(chunks, count, blocks, sems):
    number = len(chunks) // count
    cap = chunks[0].shape[0]

    def copy(j, k):
        return pltpu.make_async_copy(chunks[j * number + k], blocks.at[j, pl.ds(k * cap, cap)], sems.at[j, k])

    for j, k in itertools.product(range(count), range(number)):
        copy(j, k).start()
    here = set()

    def need(*wanted):
        for j in sorted(set(wanted) - here):
            for k in range(number):
                copy(j, k).wait()
            here.add(j)

    return need


def early_kernel(pairs, count, *refs):
    *chunks, label_ref, label_col_ref, out_ref, blocks, sems = refs
    need = loader(chunks, count, blocks, sems)
    best = [Best(jnp.full((1, blocks.shape[1]), -1.0, jnp.float32)) for _ in range(count)]
    for j, k in pairs:
        need(j, k)
        sims = similar(
            blocks[j], blocks[k], label_col_ref[:, j : j + 1], label_ref[k : k + 1, :], 0 if j == k else None
        )
        best[k].add_row(column_max(sims))
        if j != k:
            best[j].add_column(row_max(sims))
    for j in range(count):
        out_ref[j : j + 1, :] = best[j].as_row()


def late_kernel(pairs, count, group_size, *refs):
    plane_ref, *chunks, best_ref, place_ref, last_place_ref, label_ref, last_label_ref, label_col_ref, out_ref, blocks, sems = refs
    need = loader(chunks, count, blocks, sems)
    cap = chunks[0].shape[0]
    first = blocks.shape[1] - cap
    early = [Best(best_ref[j : j + 1, :]) for j in range(count)]
    late = [Best(jnp.full((1, cap), -1.0, jnp.float32)) for _ in range(count)]
    for j, k in pairs:
        need(j, k)
        sims = similar(
            blocks[j],
            blocks[k, first:],
            label_col_ref[:, j : j + 1],
            last_label_ref[k : k + 1, :],
            first if j == k else None,
        )
        column = row_max(sims)
        early[j].add_column(column[:first])
        late[k].add_row(column_max(sims))
        if j != k:
            late[j].add_column(column[first:])
            sims = similar(
                blocks[j, first:], blocks[k, :first], label_col_ref[first:, j : j + 1], label_ref[k : k + 1, :]
            )
            early[k].add_row(column_max(sims))
            late[j].add_column(row_max(sims))
    tall = group_size // 128
    pieces = [(early[j], place_ref[j : j + 1, :]) for j in range(count)]
    pieces += [(late[j], last_place_ref[j : j + 1, :]) for j in range(count)]
    spread = jnp.zeros((4 * tall, 128), jnp.float32)
    for best, place in pieces:
        best = best.as_row()
        slots = best.shape[1]
        high = lax.broadcasted_iota(jnp.int32, (tall, slots), 0) == lax.shift_right_logical(place, 7)
        low = lax.broadcasted_iota(jnp.int32, (128, slots), 0) == jnp.bitwise_and(place, 127)
        parts, rest = [], best
        for _ in range(3):
            part = rest.astype(jnp.bfloat16).astype(jnp.float32)
            rest = rest - part
            parts.append(part)
        parts.append(jnp.ones_like(best))
        stack = jnp.concatenate([jnp.where(high, part, 0.0) for part in parts], axis=0).astype(jnp.bfloat16)
        spread += lax.dot_general(stack, low.astype(jnp.bfloat16), NT, preferred_element_type=jnp.float32)
    value = spread[:tall] + spread[tall : 2 * tall] + spread[2 * tall : 3 * tall]
    value = jnp.where(spread[3 * tall :] > 0.5, value, -1.0)
    n_row, n_col, lines, _ = out_ref.shape
    for r in range(n_row):
        here = jnp.where(plane_ref[0] == r, value, -1.0)
        for c in range(n_col):
            out_ref[r, c] = here[c * lines : (c + 1) * lines]


def best_matches(cap, embeddings, dest_pos, cluster_ids):
    n_row, n_col = lax.axis_size("row"), lax.axis_size("col")
    devs = n_row * n_col
    groups, wide = n_row, n_col // n_row
    rows_dev, width = embeddings.shape
    group_size = rows_dev * n_col
    slots = groups * cap
    held, pairs = plane_plan(n_row, wide)
    count = len(held)

    assert groups & (groups - 1) == 0
    row, col = lax.axis_index("row"), lax.axis_index("col")
    plane, index = col // wide, row * wide + col % wide

    def device(i, h):
        return (i // wide) * n_col + h * wide + i % wide

    planes = [(i, h) for h in range(groups) for i in range(n_row * wide)]
    numbers = tuple(range(1, min(3, groups)))
    others = tuple(k for k in range(groups) if k not in numbers)
    chunk_shape = jax.ShapeDtypeStruct((cap, width), jnp.bfloat16)
    dest_row = dest_pos.reshape(1, rows_dev)
    plane_ref = plane.astype(jnp.int32).reshape(1)
    unit, slot, *made = pl.pallas_call(
        functools.partial(unit_kernel, groups, cap, group_size, numbers),
        out_shape=[
            jax.ShapeDtypeStruct((rows_dev, width), jnp.bfloat16),
            jax.ShapeDtypeStruct((1, rows_dev), jnp.int32),
            *[chunk_shape] * len(numbers),
        ],
        in_specs=[pl.BlockSpec(memory_space=pltpu.SMEM), VMEM, VMEM],
        out_specs=[VMEM] * (2 + len(numbers)),
        compiler_params=kernel_params(20),
    )(plane_ref, dest_row, embeddings)
    place, *more = pl.pallas_call(
        functools.partial(rest_kernel, groups, cap, group_size, others),
        out_shape=[jax.ShapeDtypeStruct((1, slots), jnp.int32), *[chunk_shape] * len(others)],
        in_specs=[VMEM] * 3,
        out_specs=[VMEM] * (1 + len(others)),
        compiler_params=kernel_params(20),
    )(dest_row, slot, unit)
    parts = dict(zip(numbers + others, made + more))

    def across(part, k):
        return lax.ppermute(part, AXES, [(device(i, h ^ k), device(i, h)) for i, h in planes])

    def inside(part, j):
        return lax.ppermute(part, AXES, [(device(int(held[j, i]), h), device(i, h)) for i, h in planes])

    def after(values, *done):
        return lax.optimization_barrier((values, done))[0]

    own = [parts[0]] + [across(parts[k], k) for k in numbers]
    rounds = [[inside(own[0], j) for j in range(1, count)]]
    place, rest = after((place, [parts[k] for k in others[1:]]), *rounds[0])
    own += [across(part, k) for k, part in zip(others[1:], rest)]
    for k in range(1, groups):
        part = own[k] if k == 1 else after(own[k], *rounds[-1])
        rounds.append([inside(part, j) for j in range(1, count)])
    blocks = [own] + [[moved[j - 1] for moved in rounds] for j in range(1, count)]

    planes_i = jnp.arange(groups, dtype=jnp.int32)
    swap = (planes_i[:, None] ^ planes_i[None, :]) == plane

    def by_plane(array):
        return jnp.sum(jnp.where(swap[:, :, None], array[None, :, :], 0), axis=1)

    levels = jnp.arange(LEVELS, dtype=jnp.int32)
    counts = jnp.sum((cluster_ids.reshape(1, rows_dev) <= levels[:, None]).astype(jnp.int32), axis=1)
    target_group = dest_pos // group_size
    most = jnp.max(jnp.sum((target_group[None, :] == jnp.arange(groups)[:, None]).astype(jnp.int32), axis=1))
    tail = jnp.concatenate([counts, (most > cap).astype(jnp.int32).reshape(1)])
    length = -(-(cap + LEVELS + 1) // 128) * 128
    facts = jnp.concatenate(
        [
            by_plane(place.reshape(groups, cap)),
            jnp.broadcast_to(tail[None, :], (groups, LEVELS + 1)),
            jnp.zeros((groups, length - cap - LEVELS - 1), jnp.int32),
        ],
        axis=1,
    )
    facts = jnp.broadcast_to(facts[None, :, None, :], (n_row, groups, wide, length)).reshape(devs, length)
    facts = lax.all_to_all(facts, AXES, split_axis=0, concat_axis=0, tiled=True)
    over = jnp.max(facts[:, cap + LEVELS]) > 0
    facts = facts.reshape(n_row, groups, wide, length)

    in_plane = (jnp.arange(n_row, dtype=jnp.int32) == plane).astype(jnp.int32)
    ends = jnp.sum(facts[..., cap : cap + LEVELS] * in_plane[:, None, None, None], axis=(0, 1, 2))
    places = by_plane(facts[..., :cap].transpose(1, 0, 2, 3).reshape(groups, n_row * wide * cap))
    places = places.reshape(groups, n_row * wide, cap).transpose(1, 0, 2).reshape(n_row * wide, slots)
    mine = jnp.sum(
        jnp.where(jnp.arange(n_row * wide)[None, :] == index, jnp.asarray(held, jnp.int32), 0), axis=1
    )
    mine = (mine[:, None] == jnp.arange(n_row * wide)[None, :]).astype(jnp.int32)
    places = jnp.sum(mine[:, :, None] * places[None, :, :], axis=1)
    labels = jnp.sum((places[:, None, :] >= ends[None, :, None]).astype(jnp.int32), axis=1)
    labels = jnp.where(places < group_size, labels, -1)

    early = slots - cap
    any_space = pl.BlockSpec(memory_space=pl.ANY)
    label_cols = labels.T
    area = 4 * slots * slots

    def scratch(number):
        return [
            pltpu.VMEM((count, number * cap, width), jnp.bfloat16),
            pltpu.SemaphoreType.DMA((count, number)),
        ]

    limit = 8 + (2 * count * slots * width + 5 * area) // 2**20
    first_best = pl.pallas_call(
        functools.partial(early_kernel, pairs, count),
        out_shape=jax.ShapeDtypeStruct((count, early), jnp.float32),
        in_specs=[any_space] * (count * (groups - 1)) + [VMEM] * 2,
        out_specs=VMEM,
        scratch_shapes=scratch(groups - 1),
        compiler_params=kernel_params(limit),
        cost_estimate=pl.CostEstimate(
            flops=2 * len(pairs) * early * early * width, bytes_accessed=2 * count * early * width, transcendentals=0
        ),
    )(*[part for block in blocks for part in block[:-1]], labels[:, :early], label_cols[:early])
    best = pl.pallas_call(
        functools.partial(late_kernel, pairs, count, group_size),
        out_shape=jax.ShapeDtypeStruct((n_row, n_col, rows_dev // 128, 128), jnp.float32),
        in_specs=[pl.BlockSpec(memory_space=pltpu.SMEM)] + [any_space] * (count * groups) + [VMEM] * 6,
        out_specs=VMEM,
        scratch_shapes=scratch(groups),
        compiler_params=kernel_params(limit),
    )(
        plane_ref,
        *itertools.chain(*blocks),
        first_best,
        places[:, :early],
        places[:, early:],
        labels[:, :early],
        labels[:, early:],
        label_cols,
    )

    best = lax.all_to_all(best.reshape(devs, -1, 128), AXES, split_axis=0, concat_axis=0, tiled=True)
    return jnp.max(best, axis=0).reshape(1, rows_dev), over


def shards(embeddings, dest_pos, cluster_ids):
    n_row, n_col = lax.axis_size("row"), lax.axis_size("col")
    rows_dev = embeddings.shape[0]
    devs = n_row * n_col
    most = min(rows_dev, n_col * max(4, 2 * rows_dev // devs))
    usual = min(most, -(-(rows_dev // n_row) * 11 // 8 // 16) * 16)
    args = (embeddings, dest_pos, cluster_ids)
    best, over = best_matches(usual, *args)
    if usual == most:
        return best
    return lax.cond(over, lambda: best_matches(most, *args)[0], lambda: best)


def solution(mesh):
    return jax.shard_map(
        shards,
        mesh=mesh,
        in_specs=(P(("row", "col"), None), P(("row", "col")), P("row", "col")),
        out_specs=P("row", "col"),
        check_vma=False,
    )
```

```python
import functools
import itertools

import jax
import jax.numpy as jnp
import numpy as np
from jax import lax
from jax.experimental import pallas as pl
from jax.experimental.pallas import tpu as pltpu
from jax.sharding import PartitionSpec as P

AXES = ("row", "col")
LEVELS = 16
NT = (((1,), (1,)), ((), ()))
VMEM = pl.BlockSpec(memory_space=pltpu.VMEM)


def kernel_params(mebibytes):
    return pltpu.CompilerParams(vmem_limit_bytes=mebibytes * 2**20)


def plane_plan(n_row, wide):
    n = n_row * wide
    if n_row == 4 and wide == 2:
        chips = [(0, 0), (0, 1), (1, 1), (1, 0)]

        def dev(chip, core):
            x, y = chips[chip % 4]
            return (x * 2 + core) * wide + y

        held = np.zeros((4, n), np.int64)
        for chip, core in itertools.product(range(4), range(2)):
            i = dev(chip, core)
            crossed = 1 - core if chip in (1, 2) else core
            held[:, i] = i, dev(chip, 1 - core), dev(chip + 1, core), dev(chip + 3, crossed)
        pairs = [(0, 0), (0, 1), (0, 2), (1, 2), (2, 3)]
    else:
        def covered(cover):
            return {(b - a) % n for a in cover for b in cover}

        size = 1
        while True:
            found = [c for c in itertools.combinations(range(n), size) if c[0] == 0 and len(covered(c)) == n]
            if found:
                break
            size += 1
        cover = found[0]
        held = (np.arange(n)[None, :] + np.array(cover)[:, None]) % n
        pairs, seen = [], set()
        for j, k in itertools.combinations_with_replacement(range(size), 2):
            delta = (cover[k] - cover[j]) % n
            if delta not in seen:
                seen |= {delta, (n - delta) % n}
                pairs.append((j, k))
    met = set()
    for j, k in pairs:
        for i in range(n):
            met |= {(held[j, i], held[k, i]), (held[k, i], held[j, i])}
    assert len(met) == n * n
    return held, pairs


def write_chunks(slot, unit, cap, chunk_refs, numbers):
    for ref, k in zip(chunk_refs, numbers):
        index = lax.broadcasted_iota(jnp.int32, (cap, unit.shape[0]), 0) + k * cap
        pick = (index == slot).astype(jnp.bfloat16)
        ref[...] = jnp.dot(pick, unit, preferred_element_type=jnp.float32).astype(jnp.bfloat16)


def unit_kernel(groups, cap, group_size, numbers, plane_ref, dest_ref, emb_ref, unit_ref, slot_ref, *chunk_refs):
    rows_dev = emb_ref.shape[0]
    dest = dest_ref[...]
    group = jnp.zeros_like(dest)
    for g in range(1, groups):
        group += (dest >= g * group_size).astype(jnp.int32)
    group = jnp.bitwise_xor(group, plane_ref[0])
    pad = -(-groups // 16) * 16
    member = lax.broadcasted_iota(jnp.int32, (pad, rows_dev), 0) == group
    earlier = lax.broadcasted_iota(jnp.int32, (rows_dev, rows_dev), 0) < lax.broadcasted_iota(
        jnp.int32, (rows_dev, rows_dev), 1
    )
    before = jnp.dot(member.astype(jnp.bfloat16), earlier.astype(jnp.bfloat16), preferred_element_type=jnp.float32)
    rank = jnp.sum(jnp.where(member, before, 0.0), axis=0, keepdims=True).astype(jnp.int32)
    slot = jnp.where(rank < cap, group * cap + rank, groups * cap)
    slot_ref[...] = slot
    x = emb_ref[...]
    unit = (x * lax.rsqrt(jnp.sum(x * x, axis=1, keepdims=True) + 1e-06)).astype(jnp.bfloat16)
    unit_ref[...] = unit
    write_chunks(slot, unit, cap, chunk_refs, numbers)


def rest_kernel(groups, cap, group_size, numbers, dest_ref, slot_ref, unit_ref, place_ref, *chunk_refs):
    rows_dev = unit_ref.shape[0]
    slot = slot_ref[...]
    write_chunks(slot, unit_ref[...], cap, chunk_refs, numbers)
    dest = dest_ref[...]
    place = dest
    for g in range(1, groups):
        place -= jnp.where(dest >= g * group_size, group_size, 0)
    high = lax.shift_right_logical(place, 7)
    low = jnp.bitwise_and(place, 127)
    kind = lax.broadcasted_iota(jnp.int32, (16, rows_dev), 0)
    facts = jnp.where(kind == 0, high, jnp.where(kind == 1, low, jnp.where(kind == 2, 1, 0)))
    facts = facts.astype(jnp.float32).astype(jnp.bfloat16)
    pick = (lax.broadcasted_iota(jnp.int32, (groups * cap, rows_dev), 0) == slot).astype(jnp.bfloat16)
    got = lax.dot_general(facts, pick, NT, preferred_element_type=jnp.float32).astype(jnp.int32)
    there = got[2:3, :] > 0
    place_ref[...] = jnp.where(there, got[0:1, :] * 128 + got[1:2, :], group_size)


class Best:
    def __init__(self, start):
        self.row, self.column = start, None

    def add_row(self, row):
        self.row = jnp.maximum(self.row, row)

    def add_column(self, column):
        self.column = column if self.column is None else jnp.maximum(self.column, column)

    def as_row(self):
        if self.column is None:
            return self.row
        n = self.column.shape[0]
        eye = lax.broadcasted_iota(jnp.int32, (n, n), 0) == lax.broadcasted_iota(jnp.int32, (n, n), 1)
        return jnp.maximum(self.row, jnp.max(jnp.where(eye, self.column, -1.0), axis=0, keepdims=True))


def similar(left, right, left_label, right_label, shift=None):
    sims = lax.dot_general(left, right, NT, preferred_element_type=jnp.float32)
    keep = left_label == right_label
    if shift is not None:
        keep &= lax.broadcasted_iota(jnp.int32, sims.shape, 0) != lax.broadcasted_iota(jnp.int32, sims.shape, 1) + shift
    return jnp.where(keep, sims, -1.0)


def row_max(sims):
    return jnp.max(sims, axis=1, keepdims=True)


def column_max(sims):
    return jnp.max(sims, axis=0, keepdims=True)


def loader(chunks, count, blocks, sems):
    number = len(chunks) // count
    cap = chunks[0].shape[0]

    def copy(j, k):
        return pltpu.make_async_copy(chunks[j * number + k], blocks.at[j, pl.ds(k * cap, cap)], sems.at[j, k])

    for j, k in itertools.product(range(count), range(number)):
        copy(j, k).start()
    here = set()

    def need(*wanted):
        for j in sorted(set(wanted) - here):
            for k in range(number):
                copy(j, k).wait()
            here.add(j)

    return need


def early_kernel(pairs, count, *refs):
    *chunks, label_ref, label_col_ref, out_ref, blocks, sems = refs
    need = loader(chunks, count, blocks, sems)
    best = [Best(jnp.full((1, blocks.shape[1]), -1.0, jnp.float32)) for _ in range(count)]
    for j, k in pairs:
        need(j, k)
        sims = similar(
            blocks[j], blocks[k], label_col_ref[:, j : j + 1], label_ref[k : k + 1, :], 0 if j == k else None
        )
        best[k].add_row(column_max(sims))
        if j != k:
            best[j].add_column(row_max(sims))
    for j in range(count):
        out_ref[j : j + 1, :] = best[j].as_row()


def late_kernel(pairs, count, group_size, *refs):
    plane_ref, *chunks, best_ref, place_ref, last_place_ref, label_ref, last_label_ref, label_col_ref, out_ref, blocks, sems = refs
    need = loader(chunks, count, blocks, sems)
    cap = chunks[0].shape[0]
    first = blocks.shape[1] - cap
    early = [Best(best_ref[j : j + 1, :]) for j in range(count)]
    late = [Best(jnp.full((1, cap), -1.0, jnp.float32)) for _ in range(count)]
    for j, k in pairs:
        need(j, k)
        sims = similar(
            blocks[j],
            blocks[k, first:],
            label_col_ref[:, j : j + 1],
            last_label_ref[k : k + 1, :],
            first if j == k else None,
        )
        column = row_max(sims)
        early[j].add_column(column[:first])
        late[k].add_row(column_max(sims))
        if j != k:
            late[j].add_column(column[first:])
            sims = similar(
                blocks[j, first:], blocks[k, :first], label_col_ref[first:, j : j + 1], label_ref[k : k + 1, :]
            )
            early[k].add_row(column_max(sims))
            late[j].add_column(row_max(sims))
    tall = group_size // 128
    pieces = [(early[j], place_ref[j : j + 1, :]) for j in range(count)]
    pieces += [(late[j], last_place_ref[j : j + 1, :]) for j in range(count)]
    spread = jnp.zeros((4 * tall, 128), jnp.float32)
    for best, place in pieces:
        best = best.as_row()
        slots = best.shape[1]
        high = lax.broadcasted_iota(jnp.int32, (tall, slots), 0) == lax.shift_right_logical(place, 7)
        low = lax.broadcasted_iota(jnp.int32, (128, slots), 0) == jnp.bitwise_and(place, 127)
        parts, rest = [], best
        for _ in range(3):
            part = rest.astype(jnp.bfloat16).astype(jnp.float32)
            rest = rest - part
            parts.append(part)
        parts.append(jnp.ones_like(best))
        stack = jnp.concatenate([jnp.where(high, part, 0.0) for part in parts], axis=0).astype(jnp.bfloat16)
        spread += lax.dot_general(stack, low.astype(jnp.bfloat16), NT, preferred_element_type=jnp.float32)
    value = spread[:tall] + spread[tall : 2 * tall] + spread[2 * tall : 3 * tall]
    value = jnp.where(spread[3 * tall :] > 0.5, value, -1.0)
    n_row, n_col, lines, _ = out_ref.shape
    for r in range(n_row):
        here = jnp.where(plane_ref[0] == r, value, -1.0)
        for c in range(n_col):
            out_ref[r, c] = here[c * lines : (c + 1) * lines]


def best_matches(cap, embeddings, dest_pos, cluster_ids):
    n_row, n_col = lax.axis_size("row"), lax.axis_size("col")
    devs = n_row * n_col
    groups, wide = n_row, n_col // n_row
    rows_dev, width = embeddings.shape
    group_size = rows_dev * n_col
    slots = groups * cap
    held, pairs = plane_plan(n_row, wide)
    count = len(held)

    assert groups & (groups - 1) == 0
    row, col = lax.axis_index("row"), lax.axis_index("col")
    plane, index = col // wide, row * wide + col % wide

    def device(i, h):
        return (i // wide) * n_col + h * wide + i % wide

    planes = [(i, h) for h in range(groups) for i in range(n_row * wide)]
    numbers, others = (0,), tuple(range(1, groups))
    chunk_shape = jax.ShapeDtypeStruct((cap, width), jnp.bfloat16)
    dest_row = dest_pos.reshape(1, rows_dev)
    plane_ref = plane.astype(jnp.int32).reshape(1)
    unit, slot, *made = pl.pallas_call(
        functools.partial(unit_kernel, groups, cap, group_size, numbers),
        out_shape=[
            jax.ShapeDtypeStruct((rows_dev, width), jnp.bfloat16),
            jax.ShapeDtypeStruct((1, rows_dev), jnp.int32),
            *[chunk_shape] * len(numbers),
        ],
        in_specs=[pl.BlockSpec(memory_space=pltpu.SMEM), VMEM, VMEM],
        out_specs=[VMEM] * (2 + len(numbers)),
        compiler_params=kernel_params(20),
    )(plane_ref, dest_row, embeddings)
    place, *more = pl.pallas_call(
        functools.partial(rest_kernel, groups, cap, group_size, others),
        out_shape=[jax.ShapeDtypeStruct((1, slots), jnp.int32), *[chunk_shape] * len(others)],
        in_specs=[VMEM] * 3,
        out_specs=[VMEM] * (1 + len(others)),
        compiler_params=kernel_params(20),
    )(dest_row, slot, unit)
    parts = dict(zip(numbers + others, made + more))

    def across(part, k):
        return lax.ppermute(part, AXES, [(device(i, h ^ k), device(i, h)) for i, h in planes])

    def inside(part, j):
        return lax.ppermute(part, AXES, [(device(int(held[j, i]), h), device(i, h)) for i, h in planes])

    def after(values, *done):
        return lax.optimization_barrier((values, done))[0]

    own = [parts[0]] + [across(parts[k], k) for k in range(1, min(3, groups))]
    rounds = [[inside(own[0], j) for j in range(1, count)]]
    place = after(place, rounds[0][0])
    rest = after([parts[k] for k in range(3, groups)], own[1])
    own += [across(part, k) for k, part in zip(range(3, groups), rest)]
    for k in range(1, groups - 1):
        near, *far = rounds[-1]
        part = after(own[k], near, *([] if k > 1 else far))
        rounds.append([inside(after(part, *far), 1), *[inside(part, j) for j in range(2, count)]])

    planes_i = jnp.arange(groups, dtype=jnp.int32)
    swap = (planes_i[:, None] ^ planes_i[None, :]) == plane

    def by_plane(array):
        return jnp.sum(jnp.where(swap[:, :, None], array[None, :, :], 0), axis=1)

    levels = jnp.arange(LEVELS, dtype=jnp.int32)
    counts = jnp.sum((cluster_ids.reshape(1, rows_dev) <= levels[:, None]).astype(jnp.int32), axis=1)
    target_group = dest_pos // group_size
    most = jnp.max(jnp.sum((target_group[None, :] == jnp.arange(groups)[:, None]).astype(jnp.int32), axis=1))
    tail = jnp.concatenate([counts, (most > cap).astype(jnp.int32).reshape(1)])
    length = -(-(cap + LEVELS + 1) // 128) * 128
    facts = jnp.concatenate(
        [
            by_plane(place.reshape(groups, cap)),
            jnp.broadcast_to(tail[None, :], (groups, LEVELS + 1)),
            jnp.zeros((groups, length - cap - LEVELS - 1), jnp.int32),
        ],
        axis=1,
    )
    facts = jnp.broadcast_to(facts[None, :, None, :], (n_row, groups, wide, length)).reshape(devs, length)
    facts = lax.all_to_all(facts, AXES, split_axis=0, concat_axis=0, tiled=True)
    facts = after(facts, *rounds[1])
    over = jnp.max(facts[:, cap + LEVELS]) > 0
    facts = facts.reshape(n_row, groups, wide, length)

    in_plane = (jnp.arange(n_row, dtype=jnp.int32) == plane).astype(jnp.int32)
    ends = jnp.sum(facts[..., cap : cap + LEVELS] * in_plane[:, None, None, None], axis=(0, 1, 2))
    places = by_plane(facts[..., :cap].transpose(1, 0, 2, 3).reshape(groups, n_row * wide * cap))
    places = places.reshape(groups, n_row * wide, cap).transpose(1, 0, 2).reshape(n_row * wide, slots)
    mine = jnp.sum(
        jnp.where(jnp.arange(n_row * wide)[None, :] == index, jnp.asarray(held, jnp.int32), 0), axis=1
    )
    mine = (mine[:, None] == jnp.arange(n_row * wide)[None, :]).astype(jnp.int32)
    places = jnp.sum(mine[:, :, None] * places[None, :, :], axis=1)
    labels = jnp.sum((places[:, None, :] >= ends[None, :, None]).astype(jnp.int32), axis=1)
    labels = jnp.where(places < group_size, labels, -1)

    early = slots - cap
    label_cols = labels.T
    facts = places[:, :early], places[:, early:], labels[:, :early], labels[:, early:], label_cols[:early], label_cols
    facts, last = lax.optimization_barrier((facts, after(own[-1], *rounds[-1][:1], *rounds[-2])))
    rounds.append([inside(last, j) for j in range(1, count)])
    place, last_place, label, last_label, label_col, label_cols = facts
    blocks = [own] + [[moved[j - 1] for moved in rounds] for j in range(1, count)]
    any_space = pl.BlockSpec(memory_space=pl.ANY)
    area = 4 * slots * slots

    def scratch(number):
        return [
            pltpu.VMEM((count, number * cap, width), jnp.bfloat16),
            pltpu.SemaphoreType.DMA((count, number)),
        ]

    limit = 8 + (2 * count * slots * width + 5 * area) // 2**20
    first_best = pl.pallas_call(
        functools.partial(early_kernel, pairs, count),
        out_shape=jax.ShapeDtypeStruct((count, early), jnp.float32),
        in_specs=[any_space] * (count * (groups - 1)) + [VMEM] * 2,
        out_specs=VMEM,
        scratch_shapes=scratch(groups - 1),
        compiler_params=kernel_params(limit),
        cost_estimate=pl.CostEstimate(
            flops=2 * len(pairs) * early * early * width, bytes_accessed=2 * count * early * width, transcendentals=0
        ),
    )(*[part for block in blocks for part in block[:-1]], label, label_col)
    best = pl.pallas_call(
        functools.partial(late_kernel, pairs, count, group_size),
        out_shape=jax.ShapeDtypeStruct((n_row, n_col, rows_dev // 128, 128), jnp.float32),
        in_specs=[pl.BlockSpec(memory_space=pltpu.SMEM)] + [any_space] * (count * groups) + [VMEM] * 6,
        out_specs=VMEM,
        scratch_shapes=scratch(groups),
        compiler_params=kernel_params(limit),
    )(
        plane_ref,
        *itertools.chain(*blocks),
        first_best,
        place,
        last_place,
        label,
        last_label,
        label_cols,
    )

    best = lax.all_to_all(best.reshape(devs, -1, 128), AXES, split_axis=0, concat_axis=0, tiled=True)
    return jnp.max(best, axis=0).reshape(1, rows_dev), over


def shards(embeddings, dest_pos, cluster_ids):
    n_row, n_col = lax.axis_size("row"), lax.axis_size("col")
    rows_dev = embeddings.shape[0]
    devs = n_row * n_col
    most = min(rows_dev, n_col * max(4, 2 * rows_dev // devs))
    usual = min(most, -(-(rows_dev // n_row) * 11 // 8 // 16) * 16)
    args = (embeddings, dest_pos, cluster_ids)
    best, over = best_matches(usual, *args)
    if usual == most:
        return best
    return lax.cond(over, lambda: best_matches(most, *args)[0], lambda: best)


def solution(mesh):
    return jax.shard_map(
        shards,
        mesh=mesh,
        in_specs=(P(("row", "col"), None), P(("row", "col")), P("row", "col")),
        out_specs=P("row", "col"),
        check_vma=False,
    )
```

```python
import functools
import itertools

import jax
import jax.numpy as jnp
import numpy as np
from jax import lax
from jax.experimental import pallas as pl
from jax.experimental.pallas import tpu as pltpu
from jax.sharding import PartitionSpec as P

AXES = ("row", "col")
LEVELS = 16
NT = (((1,), (1,)), ((), ()))
VMEM = pl.BlockSpec(memory_space=pltpu.VMEM)


def kernel_params(mebibytes):
    return pltpu.CompilerParams(vmem_limit_bytes=mebibytes * 2**20)


def plane_plan(n_row, wide):
    n = n_row * wide
    if n_row == 4 and wide == 2:
        chips = [(0, 0), (0, 1), (1, 1), (1, 0)]

        def dev(chip, core):
            x, y = chips[chip % 4]
            return (x * 2 + core) * wide + y

        held = np.zeros((4, n), np.int64)
        for chip, core in itertools.product(range(4), range(2)):
            i = dev(chip, core)
            crossed = 1 - core if chip in (1, 2) else core
            held[:, i] = i, dev(chip, 1 - core), dev(chip + 1, core), dev(chip + 3, crossed)
        pairs = [(0, 0), (0, 1), (0, 2), (1, 2), (2, 3)]
    else:
        def covered(cover):
            return {(b - a) % n for a in cover for b in cover}

        size = 1
        while True:
            found = [c for c in itertools.combinations(range(n), size) if c[0] == 0 and len(covered(c)) == n]
            if found:
                break
            size += 1
        cover = found[0]
        held = (np.arange(n)[None, :] + np.array(cover)[:, None]) % n
        pairs, seen = [], set()
        for j, k in itertools.combinations_with_replacement(range(size), 2):
            delta = (cover[k] - cover[j]) % n
            if delta not in seen:
                seen |= {delta, (n - delta) % n}
                pairs.append((j, k))
    met = set()
    for j, k in pairs:
        for i in range(n):
            met |= {(held[j, i], held[k, i]), (held[k, i], held[j, i])}
    assert len(met) == n * n
    return held, pairs


def write_chunks(slot, unit, cap, chunk_refs, numbers):
    for ref, k in zip(chunk_refs, numbers):
        index = lax.broadcasted_iota(jnp.int32, (cap, unit.shape[0]), 0) + k * cap
        pick = (index == slot).astype(jnp.bfloat16)
        ref[...] = jnp.dot(pick, unit, preferred_element_type=jnp.float32).astype(jnp.bfloat16)


def unit_kernel(groups, cap, group_size, numbers, plane_ref, dest_ref, emb_ref, unit_ref, slot_ref, *chunk_refs):
    rows_dev = emb_ref.shape[0]
    dest = dest_ref[...]
    group = jnp.zeros_like(dest)
    for g in range(1, groups):
        group += (dest >= g * group_size).astype(jnp.int32)
    group = jnp.bitwise_xor(group, plane_ref[0])
    pad = -(-groups // 16) * 16
    member = lax.broadcasted_iota(jnp.int32, (pad, rows_dev), 0) == group
    earlier = lax.broadcasted_iota(jnp.int32, (rows_dev, rows_dev), 0) < lax.broadcasted_iota(
        jnp.int32, (rows_dev, rows_dev), 1
    )
    before = jnp.dot(member.astype(jnp.bfloat16), earlier.astype(jnp.bfloat16), preferred_element_type=jnp.float32)
    rank = jnp.sum(jnp.where(member, before, 0.0), axis=0, keepdims=True).astype(jnp.int32)
    slot = jnp.where(rank < cap, group * cap + rank, groups * cap)
    slot_ref[...] = slot
    x = emb_ref[...]
    unit = (x * lax.rsqrt(jnp.sum(x * x, axis=1, keepdims=True) + 1e-06)).astype(jnp.bfloat16)
    unit_ref[...] = unit
    write_chunks(slot, unit, cap, chunk_refs, numbers)


def rest_kernel(groups, cap, group_size, numbers, dest_ref, slot_ref, unit_ref, place_ref, *chunk_refs):
    rows_dev = unit_ref.shape[0]
    slot = slot_ref[...]
    write_chunks(slot, unit_ref[...], cap, chunk_refs, numbers)
    dest = dest_ref[...]
    place = dest
    for g in range(1, groups):
        place -= jnp.where(dest >= g * group_size, group_size, 0)
    high = lax.shift_right_logical(place, 7)
    low = jnp.bitwise_and(place, 127)
    kind = lax.broadcasted_iota(jnp.int32, (16, rows_dev), 0)
    facts = jnp.where(kind == 0, high, jnp.where(kind == 1, low, jnp.where(kind == 2, 1, 0)))
    facts = facts.astype(jnp.float32).astype(jnp.bfloat16)
    pick = (lax.broadcasted_iota(jnp.int32, (groups * cap, rows_dev), 0) == slot).astype(jnp.bfloat16)
    got = lax.dot_general(facts, pick, NT, preferred_element_type=jnp.float32).astype(jnp.int32)
    there = got[2:3, :] > 0
    place_ref[...] = jnp.where(there, got[0:1, :] * 128 + got[1:2, :], group_size)


class Best:
    def __init__(self, start):
        self.row, self.column = start, None

    def add_row(self, row):
        self.row = jnp.maximum(self.row, row)

    def add_column(self, column):
        self.column = column if self.column is None else jnp.maximum(self.column, column)

    def as_row(self):
        if self.column is None:
            return self.row
        n = self.column.shape[0]
        eye = lax.broadcasted_iota(jnp.int32, (n, n), 0) == lax.broadcasted_iota(jnp.int32, (n, n), 1)
        return jnp.maximum(self.row, jnp.max(jnp.where(eye, self.column, -1.0), axis=0, keepdims=True))


def similar(left, right, left_label, right_label, shift=None):
    sims = lax.dot_general(left, right, NT, preferred_element_type=jnp.float32)
    keep = left_label == right_label
    if shift is not None:
        keep &= lax.broadcasted_iota(jnp.int32, sims.shape, 0) != lax.broadcasted_iota(jnp.int32, sims.shape, 1) + shift
    return jnp.where(keep, sims, -1.0)


def row_max(sims):
    return jnp.max(sims, axis=1, keepdims=True)


def column_max(sims):
    return jnp.max(sims, axis=0, keepdims=True)


def loader(chunks, count, blocks, sems):
    number = len(chunks) // count
    cap = chunks[0].shape[0]

    def copy(j, k):
        return pltpu.make_async_copy(chunks[j * number + k], blocks.at[j, pl.ds(k * cap, cap)], sems.at[j, k])

    for j, k in itertools.product(range(count), range(number)):
        copy(j, k).start()
    here = set()

    def need(*wanted):
        for j in sorted(set(wanted) - here):
            for k in range(number):
                copy(j, k).wait()
            here.add(j)

    return need


def early_kernel(pairs, count, *refs):
    *chunks, label_ref, label_col_ref, out_ref, blocks, sems = refs
    need = loader(chunks, count, blocks, sems)
    best = [Best(jnp.full((1, blocks.shape[1]), -1.0, jnp.float32)) for _ in range(count)]
    for j, k in pairs:
        need(j, k)
        sims = similar(
            blocks[j], blocks[k], label_col_ref[:, j : j + 1], label_ref[k : k + 1, :], 0 if j == k else None
        )
        best[k].add_row(column_max(sims))
        if j != k:
            best[j].add_column(row_max(sims))
    for j in range(count):
        out_ref[j : j + 1, :] = best[j].as_row()


def late_kernel(pairs, count, group_size, *refs):
    plane_ref, *chunks, best_ref, place_ref, last_place_ref, label_ref, last_label_ref, label_col_ref, out_ref, blocks, sems = refs
    need = loader(chunks, count, blocks, sems)
    cap = chunks[0].shape[0]
    first = blocks.shape[1] - cap
    early = [Best(best_ref[j : j + 1, :]) for j in range(count)]
    late = [Best(jnp.full((1, cap), -1.0, jnp.float32)) for _ in range(count)]
    for j, k in pairs:
        need(j, k)
        sims = similar(
            blocks[j],
            blocks[k, first:],
            label_col_ref[:, j : j + 1],
            last_label_ref[k : k + 1, :],
            first if j == k else None,
        )
        column = row_max(sims)
        early[j].add_column(column[:first])
        late[k].add_row(column_max(sims))
        if j != k:
            late[j].add_column(column[first:])
            sims = similar(
                blocks[j, first:], blocks[k, :first], label_col_ref[first:, j : j + 1], label_ref[k : k + 1, :]
            )
            early[k].add_row(column_max(sims))
            late[j].add_column(row_max(sims))
    tall = group_size // 128
    pieces = [(early[j], place_ref[j : j + 1, :]) for j in range(count)]
    pieces += [(late[j], last_place_ref[j : j + 1, :]) for j in range(count)]
    spread = jnp.zeros((4 * tall, 128), jnp.float32)
    for best, place in pieces:
        best = best.as_row()
        slots = best.shape[1]
        high = lax.broadcasted_iota(jnp.int32, (tall, slots), 0) == lax.shift_right_logical(place, 7)
        low = lax.broadcasted_iota(jnp.int32, (128, slots), 0) == jnp.bitwise_and(place, 127)
        parts, rest = [], best
        for _ in range(3):
            part = rest.astype(jnp.bfloat16).astype(jnp.float32)
            rest = rest - part
            parts.append(part)
        parts.append(jnp.ones_like(best))
        stack = jnp.concatenate([jnp.where(high, part, 0.0) for part in parts], axis=0).astype(jnp.bfloat16)
        spread += lax.dot_general(stack, low.astype(jnp.bfloat16), NT, preferred_element_type=jnp.float32)
    value = spread[:tall] + spread[tall : 2 * tall] + spread[2 * tall : 3 * tall]
    value = jnp.where(spread[3 * tall :] > 0.5, value, -1.0)
    n_row, n_col, lines, _ = out_ref.shape
    for r in range(n_row):
        here = jnp.where(plane_ref[0] == r, value, -1.0)
        for c in range(n_col):
            out_ref[r, c] = here[c * lines : (c + 1) * lines]


def best_matches(cap, embeddings, dest_pos, cluster_ids):
    n_row, n_col = lax.axis_size("row"), lax.axis_size("col")
    devs = n_row * n_col
    groups, wide = n_row, n_col // n_row
    rows_dev, width = embeddings.shape
    group_size = rows_dev * n_col
    slots = groups * cap
    held, pairs = plane_plan(n_row, wide)
    count = len(held)

    assert groups & (groups - 1) == 0
    row, col = lax.axis_index("row"), lax.axis_index("col")
    plane, index = col // wide, row * wide + col % wide

    def device(i, h):
        return (i // wide) * n_col + h * wide + i % wide

    planes = [(i, h) for h in range(groups) for i in range(n_row * wide)]
    numbers, others = tuple(range(min(3, groups))), tuple(range(3, groups))
    chunk_shape = jax.ShapeDtypeStruct((cap, width), jnp.bfloat16)
    dest_row = dest_pos.reshape(1, rows_dev)
    plane_ref = plane.astype(jnp.int32).reshape(1)
    unit, slot, *made = pl.pallas_call(
        functools.partial(unit_kernel, groups, cap, group_size, numbers),
        out_shape=[
            jax.ShapeDtypeStruct((rows_dev, width), jnp.bfloat16),
            jax.ShapeDtypeStruct((1, rows_dev), jnp.int32),
            *[chunk_shape] * len(numbers),
        ],
        in_specs=[pl.BlockSpec(memory_space=pltpu.SMEM), VMEM, VMEM],
        out_specs=[VMEM] * (2 + len(numbers)),
        compiler_params=kernel_params(20),
    )(plane_ref, dest_row, embeddings)
    place, *more = pl.pallas_call(
        functools.partial(rest_kernel, groups, cap, group_size, others),
        out_shape=[jax.ShapeDtypeStruct((1, slots), jnp.int32), *[chunk_shape] * len(others)],
        in_specs=[VMEM] * 3,
        out_specs=[VMEM] * (1 + len(others)),
        compiler_params=kernel_params(20),
    )(dest_row, slot, unit)
    parts = dict(zip(numbers + others, made + more))

    def across(part, k):
        return lax.ppermute(part, AXES, [(device(i, h ^ k), device(i, h)) for i, h in planes])

    def inside(part, j):
        return lax.ppermute(part, AXES, [(device(int(held[j, i]), h), device(i, h)) for i, h in planes])

    def after(values, *done):
        return lax.optimization_barrier((values, done))[0]

    own = [parts[0]] + [across(parts[k], k) for k in range(1, min(3, groups))]
    near = inside(own[0], 1)
    rounds = [[near] + [inside(after(own[0], near), j) for j in range(2, count)]]
    place, rest = after((place, [parts[k] for k in range(3, groups)]), near)

    planes_i = jnp.arange(groups, dtype=jnp.int32)
    swap = (planes_i[:, None] ^ planes_i[None, :]) == plane

    def by_plane(array):
        return jnp.sum(jnp.where(swap[:, :, None], array[None, :, :], 0), axis=1)

    levels = jnp.arange(LEVELS, dtype=jnp.int32)
    counts = jnp.sum((cluster_ids.reshape(1, rows_dev) <= levels[:, None]).astype(jnp.int32), axis=1)
    target_group = dest_pos // group_size
    most = jnp.max(jnp.sum((target_group[None, :] == jnp.arange(groups)[:, None]).astype(jnp.int32), axis=1))
    tail = jnp.concatenate([counts, (most > cap).astype(jnp.int32).reshape(1)])
    length = -(-(cap + LEVELS + 1) // 128) * 128
    facts = jnp.concatenate(
        [
            by_plane(place.reshape(groups, cap)),
            jnp.broadcast_to(tail[None, :], (groups, LEVELS + 1)),
            jnp.zeros((groups, length - cap - LEVELS - 1), jnp.int32),
        ],
        axis=1,
    )
    facts = jnp.broadcast_to(facts[None, :, None, :], (n_row, groups, wide, length)).reshape(devs, length)
    facts = lax.all_to_all(facts, AXES, split_axis=0, concat_axis=0, tiled=True)
    rest = after(rest, near)
    own += [across(part, k) for k, part in zip(range(3, groups), rest)]
    for k in range(1, groups - 1):
        part = after(own[k], facts, *rounds[0]) if k == 1 else after(own[k], rounds[-1][0], *rounds[-2])
        near = after(part, own[k + 1]) if k > 1 else part
        rounds.append([inside(near, 1), *[inside(part, j) for j in range(2, count)]])

    over = jnp.max(facts[:, cap + LEVELS]) > 0
    facts = facts.reshape(n_row, groups, wide, length)

    in_plane = (jnp.arange(n_row, dtype=jnp.int32) == plane).astype(jnp.int32)
    ends = jnp.sum(facts[..., cap : cap + LEVELS] * in_plane[:, None, None, None], axis=(0, 1, 2))
    places = by_plane(facts[..., :cap].transpose(1, 0, 2, 3).reshape(groups, n_row * wide * cap))
    places = places.reshape(groups, n_row * wide, cap).transpose(1, 0, 2).reshape(n_row * wide, slots)
    mine = jnp.sum(
        jnp.where(jnp.arange(n_row * wide)[None, :] == index, jnp.asarray(held, jnp.int32), 0), axis=1
    )
    mine = (mine[:, None] == jnp.arange(n_row * wide)[None, :]).astype(jnp.int32)
    places = jnp.sum(mine[:, :, None] * places[None, :, :], axis=1)
    labels = jnp.sum((places[:, None, :] >= ends[None, :, None]).astype(jnp.int32), axis=1)
    labels = jnp.where(places < group_size, labels, -1)

    early = slots - cap
    label_cols = labels.T
    facts = places[:, :early], places[:, early:], labels[:, :early], labels[:, early:], label_cols[:early], label_cols
    facts, last = lax.optimization_barrier((facts, after(own[-1], *rounds[-2])))
    rounds.append([inside(after(last, rounds[-1][0]), 1), *[inside(last, j) for j in range(2, count)]])
    place, last_place, label, last_label, label_col, label_cols = facts
    blocks = [own] + [[moved[j - 1] for moved in rounds] for j in range(1, count)]
    any_space = pl.BlockSpec(memory_space=pltpu.HBM)
    area = 4 * slots * slots

    def scratch(number):
        return [
            pltpu.VMEM((count, number * cap, width), jnp.bfloat16),
            pltpu.SemaphoreType.DMA((count, number)),
        ]

    limit = 8 + (2 * count * slots * width + 5 * area) // 2**20
    first_best = pl.pallas_call(
        functools.partial(early_kernel, pairs, count),
        out_shape=jax.ShapeDtypeStruct((count, early), jnp.float32),
        in_specs=[any_space] * (count * (groups - 1)) + [VMEM] * 2,
        out_specs=VMEM,
        scratch_shapes=scratch(groups - 1),
        compiler_params=kernel_params(limit),
        cost_estimate=pl.CostEstimate(
            flops=2 * len(pairs) * early * early * width, bytes_accessed=2 * count * early * width, transcendentals=0
        ),
    )(*[part for block in blocks for part in block[:-1]], label, label_col)
    best = pl.pallas_call(
        functools.partial(late_kernel, pairs, count, group_size),
        out_shape=jax.ShapeDtypeStruct((n_row, n_col, rows_dev // 128, 128), jnp.float32),
        in_specs=[pl.BlockSpec(memory_space=pltpu.SMEM)] + [any_space] * (count * groups) + [VMEM] * 6,
        out_specs=VMEM,
        scratch_shapes=scratch(groups),
        compiler_params=kernel_params(limit),
    )(
        plane_ref,
        *itertools.chain(*blocks),
        first_best,
        place,
        last_place,
        label,
        last_label,
        label_cols,
    )

    best = lax.all_to_all(best.reshape(devs, -1, 128), AXES, split_axis=0, concat_axis=0, tiled=True)
    return jnp.max(best, axis=0).reshape(1, rows_dev), over


def shards(embeddings, dest_pos, cluster_ids):
    n_row, n_col = lax.axis_size("row"), lax.axis_size("col")
    rows_dev = embeddings.shape[0]
    devs = n_row * n_col
    most = min(rows_dev, n_col * max(4, 2 * rows_dev // devs))
    usual = min(most, -(-(rows_dev // n_row) * 11 // 8 // 16) * 16)
    args = (embeddings, dest_pos, cluster_ids)
    best, over = best_matches(usual, *args)
    if usual == most:
        return best
    return lax.cond(over, lambda: best_matches(most, *args)[0], lambda: best)


def solution(mesh):
    return jax.shard_map(
        shards,
        mesh=mesh,
        in_specs=(P(("row", "col"), None), P(("row", "col")), P("row", "col")),
        out_specs=P("row", "col"),
        check_vma=False,
    )
```

```python
import functools
import itertools

import jax
import jax.numpy as jnp
import numpy as np
from jax import lax
from jax.experimental import pallas as pl
from jax.experimental.pallas import tpu as pltpu
from jax.sharding import PartitionSpec as P

AXES = ("row", "col")
LEVELS = 16
NT = (((1,), (1,)), ((), ()))
VMEM = pl.BlockSpec(memory_space=pltpu.VMEM)


def kernel_params(mebibytes):
    return pltpu.CompilerParams(vmem_limit_bytes=mebibytes * 2**20)


def plane_plan(n_row, wide):
    n = n_row * wide
    if n_row == 4 and wide == 2:
        chips = [(0, 0), (0, 1), (1, 1), (1, 0)]

        def dev(chip, core):
            x, y = chips[chip % 4]
            return (x * 2 + core) * wide + y

        held = np.zeros((4, n), np.int64)
        for chip, core in itertools.product(range(4), range(2)):
            i = dev(chip, core)
            crossed = 1 - core if chip in (1, 2) else core
            held[:, i] = i, dev(chip, 1 - core), dev(chip + 1, core), dev(chip + 3, crossed)
        pairs = [(0, 0), (0, 1), (0, 2), (1, 2), (2, 3)]
    else:
        def covered(cover):
            return {(b - a) % n for a in cover for b in cover}

        size = 1
        while True:
            found = [c for c in itertools.combinations(range(n), size) if c[0] == 0 and len(covered(c)) == n]
            if found:
                break
            size += 1
        cover = found[0]
        held = (np.arange(n)[None, :] + np.array(cover)[:, None]) % n
        pairs, seen = [], set()
        for j, k in itertools.combinations_with_replacement(range(size), 2):
            delta = (cover[k] - cover[j]) % n
            if delta not in seen:
                seen |= {delta, (n - delta) % n}
                pairs.append((j, k))
    met = set()
    for j, k in pairs:
        for i in range(n):
            met |= {(held[j, i], held[k, i]), (held[k, i], held[j, i])}
    assert len(met) == n * n
    return held, pairs


def write_chunks(slot, unit, cap, chunk_refs, numbers):
    for ref, k in zip(chunk_refs, numbers):
        index = lax.broadcasted_iota(jnp.int32, (cap, unit.shape[0]), 0) + k * cap
        pick = (index == slot).astype(jnp.bfloat16)
        ref[...] = jnp.dot(pick, unit, preferred_element_type=jnp.float32).astype(jnp.bfloat16)


def unit_kernel(groups, cap, group_size, numbers, plane_ref, dest_ref, emb_ref, unit_ref, slot_ref, *chunk_refs):
    rows_dev = emb_ref.shape[0]
    dest = dest_ref[...]
    group = jnp.zeros_like(dest)
    for g in range(1, groups):
        group += (dest >= g * group_size).astype(jnp.int32)
    group = jnp.bitwise_xor(group, plane_ref[0])
    pad = -(-groups // 16) * 16
    member = lax.broadcasted_iota(jnp.int32, (pad, rows_dev), 0) == group
    earlier = lax.broadcasted_iota(jnp.int32, (rows_dev, rows_dev), 0) < lax.broadcasted_iota(
        jnp.int32, (rows_dev, rows_dev), 1
    )
    before = jnp.dot(member.astype(jnp.bfloat16), earlier.astype(jnp.bfloat16), preferred_element_type=jnp.float32)
    rank = jnp.sum(jnp.where(member, before, 0.0), axis=0, keepdims=True).astype(jnp.int32)
    slot = jnp.where(rank < cap, group * cap + rank, groups * cap)
    slot_ref[...] = slot
    x = emb_ref[...]
    unit = (x * lax.rsqrt(jnp.sum(x * x, axis=1, keepdims=True) + 1e-06)).astype(jnp.bfloat16)
    unit_ref[...] = unit
    write_chunks(slot, unit, cap, chunk_refs, numbers)


def rest_kernel(groups, cap, group_size, numbers, dest_ref, slot_ref, unit_ref, place_ref, *chunk_refs):
    rows_dev = unit_ref.shape[0]
    slot = slot_ref[...]
    write_chunks(slot, unit_ref[...], cap, chunk_refs, numbers)
    dest = dest_ref[...]
    place = dest
    for g in range(1, groups):
        place -= jnp.where(dest >= g * group_size, group_size, 0)
    high = lax.shift_right_logical(place, 7)
    low = jnp.bitwise_and(place, 127)
    kind = lax.broadcasted_iota(jnp.int32, (16, rows_dev), 0)
    facts = jnp.where(kind == 0, high, jnp.where(kind == 1, low, jnp.where(kind == 2, 1, 0)))
    facts = facts.astype(jnp.float32).astype(jnp.bfloat16)
    pick = (lax.broadcasted_iota(jnp.int32, (groups * cap, rows_dev), 0) == slot).astype(jnp.bfloat16)
    got = lax.dot_general(facts, pick, NT, preferred_element_type=jnp.float32).astype(jnp.int32)
    there = got[2:3, :] > 0
    place_ref[...] = jnp.where(there, got[0:1, :] * 128 + got[1:2, :], group_size)


class Best:
    def __init__(self, start):
        self.row, self.column = start, None

    def add_row(self, row):
        self.row = jnp.maximum(self.row, row)

    def add_column(self, column):
        self.column = column if self.column is None else jnp.maximum(self.column, column)

    def as_row(self):
        if self.column is None:
            return self.row
        n = self.column.shape[0]
        eye = lax.broadcasted_iota(jnp.int32, (n, n), 0) == lax.broadcasted_iota(jnp.int32, (n, n), 1)
        return jnp.maximum(self.row, jnp.max(jnp.where(eye, self.column, -1.0), axis=0, keepdims=True))


def similar(left, right, left_label, right_label, shift=None):
    sims = lax.dot_general(left, right, NT, preferred_element_type=jnp.float32)
    keep = left_label == right_label
    if shift is not None:
        keep &= lax.broadcasted_iota(jnp.int32, sims.shape, 0) != lax.broadcasted_iota(jnp.int32, sims.shape, 1) + shift
    return jnp.where(keep, sims, -1.0)


def row_max(sims):
    return jnp.max(sims, axis=1, keepdims=True)


def column_max(sims):
    return jnp.max(sims, axis=0, keepdims=True)


def loader(chunks, count, blocks, sems):
    number = len(chunks) // count
    cap = chunks[0].shape[0]

    def copy(j, k):
        return pltpu.make_async_copy(chunks[j * number + k], blocks.at[j, pl.ds(k * cap, cap)], sems.at[j, k])

    for j, k in itertools.product(range(count), range(number)):
        copy(j, k).start()
    here = set()

    def need(*wanted):
        for j in sorted(set(wanted) - here):
            for k in range(number):
                copy(j, k).wait()
            here.add(j)

    return need


def early_kernel(pairs, count, *refs):
    *chunks, label_ref, label_col_ref, out_ref, blocks, sems = refs
    need = loader(chunks, count, blocks, sems)
    best = [Best(jnp.full((1, blocks.shape[1]), -1.0, jnp.float32)) for _ in range(count)]
    for j, k in pairs:
        need(j, k)
        sims = similar(
            blocks[j], blocks[k], label_col_ref[:, j : j + 1], label_ref[k : k + 1, :], 0 if j == k else None
        )
        best[k].add_row(column_max(sims))
        if j != k:
            best[j].add_column(row_max(sims))
    for j in range(count):
        out_ref[j : j + 1, :] = best[j].as_row()


def late_kernel(pairs, count, group_size, *refs):
    plane_ref, *chunks, best_ref, place_ref, last_place_ref, label_ref, last_label_ref, label_col_ref, out_ref, blocks, sems = refs
    need = loader(chunks, count, blocks, sems)
    cap = chunks[0].shape[0]
    first = blocks.shape[1] - cap
    early = [Best(best_ref[j : j + 1, :]) for j in range(count)]
    late = [Best(jnp.full((1, cap), -1.0, jnp.float32)) for _ in range(count)]
    for j, k in pairs:
        need(j, k)
        sims = similar(
            blocks[j],
            blocks[k, first:],
            label_col_ref[:, j : j + 1],
            last_label_ref[k : k + 1, :],
            first if j == k else None,
        )
        column = row_max(sims)
        early[j].add_column(column[:first])
        late[k].add_row(column_max(sims))
        if j != k:
            late[j].add_column(column[first:])
            sims = similar(
                blocks[j, first:], blocks[k, :first], label_col_ref[first:, j : j + 1], label_ref[k : k + 1, :]
            )
            early[k].add_row(column_max(sims))
            late[j].add_column(row_max(sims))
    tall = group_size // 128
    pieces = [(early[j], place_ref[j : j + 1, :]) for j in range(count)]
    pieces += [(late[j], last_place_ref[j : j + 1, :]) for j in range(count)]
    spread = jnp.zeros((4 * tall, 128), jnp.float32)
    for best, place in pieces:
        best = best.as_row()
        slots = best.shape[1]
        high = lax.broadcasted_iota(jnp.int32, (tall, slots), 0) == lax.shift_right_logical(place, 7)
        low = lax.broadcasted_iota(jnp.int32, (128, slots), 0) == jnp.bitwise_and(place, 127)
        parts, rest = [], best
        for _ in range(3):
            part = rest.astype(jnp.bfloat16).astype(jnp.float32)
            rest = rest - part
            parts.append(part)
        parts.append(jnp.ones_like(best))
        stack = jnp.concatenate([jnp.where(high, part, 0.0) for part in parts], axis=0).astype(jnp.bfloat16)
        spread += lax.dot_general(stack, low.astype(jnp.bfloat16), NT, preferred_element_type=jnp.float32)
    value = spread[:tall] + spread[tall : 2 * tall] + spread[2 * tall : 3 * tall]
    value = jnp.where(spread[3 * tall :] > 0.5, value, -1.0)
    n_row, n_col, lines, _ = out_ref.shape
    for r in range(n_row):
        here = jnp.where(plane_ref[0] == r, value, -1.0)
        for c in range(n_col):
            out_ref[r, c] = here[c * lines : (c + 1) * lines]


def best_matches(cap, embeddings, dest_pos, cluster_ids):
    n_row, n_col = lax.axis_size("row"), lax.axis_size("col")
    devs = n_row * n_col
    groups, wide = n_row, n_col // n_row
    rows_dev, width = embeddings.shape
    group_size = rows_dev * n_col
    slots = groups * cap
    held, pairs = plane_plan(n_row, wide)
    count = len(held)

    assert groups & (groups - 1) == 0
    row, col = lax.axis_index("row"), lax.axis_index("col")
    plane, index = col // wide, row * wide + col % wide

    def device(i, h):
        return (i // wide) * n_col + h * wide + i % wide

    planes = [(i, h) for h in range(groups) for i in range(n_row * wide)]
    numbers, others = tuple(range(min(3, groups))), tuple(range(3, groups))
    chunk_shape = jax.ShapeDtypeStruct((cap, width), jnp.bfloat16)
    dest_row = dest_pos.reshape(1, rows_dev)
    plane_ref = plane.astype(jnp.int32).reshape(1)
    unit, slot, *made = pl.pallas_call(
        functools.partial(unit_kernel, groups, cap, group_size, numbers),
        out_shape=[
            jax.ShapeDtypeStruct((rows_dev, width), jnp.bfloat16),
            jax.ShapeDtypeStruct((1, rows_dev), jnp.int32),
            *[chunk_shape] * len(numbers),
        ],
        in_specs=[pl.BlockSpec(memory_space=pltpu.SMEM), VMEM, VMEM],
        out_specs=[VMEM] * (2 + len(numbers)),
        compiler_params=kernel_params(20),
    )(plane_ref, dest_row, embeddings)
    place, *more = pl.pallas_call(
        functools.partial(rest_kernel, groups, cap, group_size, others),
        out_shape=[jax.ShapeDtypeStruct((1, slots), jnp.int32), *[chunk_shape] * len(others)],
        in_specs=[VMEM] * 3,
        out_specs=[VMEM] * (1 + len(others)),
        compiler_params=kernel_params(20),
    )(dest_row, slot, unit)
    parts = dict(zip(numbers + others, made + more))

    def across(part, k):
        return lax.ppermute(part, AXES, [(device(i, h ^ k), device(i, h)) for i, h in planes])

    def inside(part, j):
        return lax.ppermute(part, AXES, [(device(int(held[j, i]), h), device(i, h)) for i, h in planes])

    def after(values, *done):
        return lax.optimization_barrier((values, done))[0]

    own = [parts[0]] + [across(parts[k], k) for k in range(1, min(3, groups))]
    near = inside(own[0], 1)
    rounds = [[near] + [inside(after(own[0], near), j) for j in range(2, count)]]
    rest = after([parts[k] for k in range(3, groups)], near)

    own += [across(part, k) for k, part in zip(range(3, groups), rest)]
    for k in range(1, groups - 1):
        part = after(own[k], *rounds[0]) if k == 1 else after(own[k], rounds[-1][0], *rounds[-2])
        near = after(part, own[k + 1]) if k > 1 else part
        rounds.append([inside(near, 1), *[inside(part, j) for j in range(2, count)]])

    last = after(own[-1], *rounds[-2])
    rounds.append([inside(after(last, rounds[-1][0]), 1), *[inside(last, j) for j in range(2, count)]])
    place = after(place, rounds[1][0])

    planes_i = jnp.arange(groups, dtype=jnp.int32)
    swap = (planes_i[:, None] ^ planes_i[None, :]) == plane

    def by_plane(array):
        return jnp.sum(jnp.where(swap[:, :, None], array[None, :, :], 0), axis=1)

    levels = jnp.arange(LEVELS, dtype=jnp.int32)
    counts = jnp.sum((cluster_ids.reshape(1, rows_dev) <= levels[:, None]).astype(jnp.int32), axis=1)
    target_group = dest_pos // group_size
    most = jnp.max(jnp.sum((target_group[None, :] == jnp.arange(groups)[:, None]).astype(jnp.int32), axis=1))
    tail = jnp.concatenate([counts, (most > cap).astype(jnp.int32).reshape(1)])
    length = -(-(cap + LEVELS + 1) // 128) * 128
    facts = jnp.concatenate(
        [
            by_plane(place.reshape(groups, cap)),
            jnp.broadcast_to(tail[None, :], (groups, LEVELS + 1)),
            jnp.zeros((groups, length - cap - LEVELS - 1), jnp.int32),
        ],
        axis=1,
    )
    facts = jnp.broadcast_to(facts[None, :, None, :], (n_row, groups, wide, length)).reshape(devs, length)
    facts = lax.all_to_all(facts, AXES, split_axis=0, concat_axis=0, tiled=True)
    over = jnp.max(facts[:, cap + LEVELS]) > 0
    facts = facts.reshape(n_row, groups, wide, length)

    in_plane = (jnp.arange(n_row, dtype=jnp.int32) == plane).astype(jnp.int32)
    ends = jnp.sum(facts[..., cap : cap + LEVELS] * in_plane[:, None, None, None], axis=(0, 1, 2))
    places = by_plane(facts[..., :cap].transpose(1, 0, 2, 3).reshape(groups, n_row * wide * cap))
    places = places.reshape(groups, n_row * wide, cap).transpose(1, 0, 2).reshape(n_row * wide, slots)
    mine = jnp.sum(
        jnp.where(jnp.arange(n_row * wide)[None, :] == index, jnp.asarray(held, jnp.int32), 0), axis=1
    )
    mine = (mine[:, None] == jnp.arange(n_row * wide)[None, :]).astype(jnp.int32)
    places = jnp.sum(mine[:, :, None] * places[None, :, :], axis=1)
    labels = jnp.sum((places[:, None, :] >= ends[None, :, None]).astype(jnp.int32), axis=1)
    labels = jnp.where(places < group_size, labels, -1)

    early = slots - cap
    label_cols = labels.T
    facts = places[:, :early], places[:, early:], labels[:, :early], labels[:, early:], label_cols[:early], label_cols
    place, last_place, label, last_label, label_col, label_cols = facts
    blocks = [own] + [[moved[j - 1] for moved in rounds] for j in range(1, count)]
    any_space = pl.BlockSpec(memory_space=pltpu.HBM)
    area = 4 * slots * slots

    def scratch(number):
        return [
            pltpu.VMEM((count, number * cap, width), jnp.bfloat16),
            pltpu.SemaphoreType.DMA((count, number)),
        ]

    limit = 8 + (2 * count * slots * width + 5 * area) // 2**20
    first_best = pl.pallas_call(
        functools.partial(early_kernel, pairs, count),
        out_shape=jax.ShapeDtypeStruct((count, early), jnp.float32),
        in_specs=[any_space] * (count * (groups - 1)) + [VMEM] * 2,
        out_specs=VMEM,
        scratch_shapes=scratch(groups - 1),
        compiler_params=kernel_params(limit),
        cost_estimate=pl.CostEstimate(
            flops=2 * len(pairs) * early * early * width, bytes_accessed=2 * count * early * width, transcendentals=0
        ),
    )(*[part for block in blocks for part in block[:-1]], label, label_col)
    best = pl.pallas_call(
        functools.partial(late_kernel, pairs, count, group_size),
        out_shape=jax.ShapeDtypeStruct((n_row, n_col, rows_dev // 128, 128), jnp.float32),
        in_specs=[pl.BlockSpec(memory_space=pltpu.SMEM)] + [any_space] * (count * groups) + [VMEM] * 6,
        out_specs=VMEM,
        scratch_shapes=scratch(groups),
        compiler_params=kernel_params(limit),
    )(
        plane_ref,
        *itertools.chain(*blocks),
        first_best,
        place,
        last_place,
        label,
        last_label,
        label_cols,
    )

    best = lax.all_to_all(best.reshape(devs, -1, 128), AXES, split_axis=0, concat_axis=0, tiled=True)
    return jnp.max(best, axis=0).reshape(1, rows_dev), over


def shards(embeddings, dest_pos, cluster_ids):
    n_row, n_col = lax.axis_size("row"), lax.axis_size("col")
    rows_dev = embeddings.shape[0]
    devs = n_row * n_col
    most = min(rows_dev, n_col * max(4, 2 * rows_dev // devs))
    usual = min(most, -(-(rows_dev // n_row) * 11 // 8 // 16) * 16)
    args = (embeddings, dest_pos, cluster_ids)
    best, over = best_matches(usual, *args)
    if usual == most:
        return best
    return lax.cond(over, lambda: best_matches(most, *args)[0], lambda: best)


def solution(mesh):
    return jax.shard_map(
        shards,
        mesh=mesh,
        in_specs=(P(("row", "col"), None), P(("row", "col")), P("row", "col")),
        out_specs=P("row", "col"),
        check_vma=False,
    )
```

```python
import functools
import itertools

import jax
import jax.numpy as jnp
import numpy as np
from jax import lax
from jax.experimental import pallas as pl
from jax.experimental.pallas import tpu as pltpu
from jax.sharding import PartitionSpec as P

AXES = ("row", "col")
LEVELS = 16
NT = (((1,), (1,)), ((), ()))
VMEM = pl.BlockSpec(memory_space=pltpu.VMEM)


def kernel_params(mebibytes):
    return pltpu.CompilerParams(vmem_limit_bytes=mebibytes * 2**20)


def plane_plan(n_row, wide):
    n = n_row * wide
    if n_row == 4 and wide == 2:
        chips = [(0, 0), (0, 1), (1, 1), (1, 0)]

        def dev(chip, core):
            x, y = chips[chip % 4]
            return (x * 2 + core) * wide + y

        held = np.zeros((4, n), np.int64)
        for chip, core in itertools.product(range(4), range(2)):
            i = dev(chip, core)
            crossed = 1 - core if chip in (1, 2) else core
            held[:, i] = i, dev(chip, 1 - core), dev(chip + 1, core), dev(chip + 3, crossed)
        pairs = [(0, 0), (0, 1), (0, 2), (1, 2), (2, 3)]
    else:
        def covered(cover):
            return {(b - a) % n for a in cover for b in cover}

        size = 1
        while True:
            found = [c for c in itertools.combinations(range(n), size) if c[0] == 0 and len(covered(c)) == n]
            if found:
                break
            size += 1
        cover = found[0]
        held = (np.arange(n)[None, :] + np.array(cover)[:, None]) % n
        pairs, seen = [], set()
        for j, k in itertools.combinations_with_replacement(range(size), 2):
            delta = (cover[k] - cover[j]) % n
            if delta not in seen:
                seen |= {delta, (n - delta) % n}
                pairs.append((j, k))
    met = set()
    for j, k in pairs:
        for i in range(n):
            met |= {(held[j, i], held[k, i]), (held[k, i], held[j, i])}
    assert len(met) == n * n
    return held, pairs


def write_chunks(slot, unit, cap, chunk_refs, numbers):
    for ref, k in zip(chunk_refs, numbers):
        index = lax.broadcasted_iota(jnp.int32, (cap, unit.shape[0]), 0) + k * cap
        pick = (index == slot).astype(jnp.bfloat16)
        ref[...] = jnp.dot(pick, unit, preferred_element_type=jnp.float32).astype(jnp.bfloat16)


def unit_kernel(groups, cap, group_size, numbers, plane_ref, dest_ref, emb_ref, unit_ref, slot_ref, *chunk_refs):
    rows_dev = emb_ref.shape[0]
    dest = dest_ref[...]
    group = jnp.zeros_like(dest)
    for g in range(1, groups):
        group += (dest >= g * group_size).astype(jnp.int32)
    group = jnp.bitwise_xor(group, plane_ref[0])
    pad = -(-groups // 16) * 16
    member = lax.broadcasted_iota(jnp.int32, (pad, rows_dev), 0) == group
    earlier = lax.broadcasted_iota(jnp.int32, (rows_dev, rows_dev), 0) < lax.broadcasted_iota(
        jnp.int32, (rows_dev, rows_dev), 1
    )
    before = jnp.dot(member.astype(jnp.bfloat16), earlier.astype(jnp.bfloat16), preferred_element_type=jnp.float32)
    rank = jnp.sum(jnp.where(member, before, 0.0), axis=0, keepdims=True).astype(jnp.int32)
    slot = jnp.where(rank < cap, group * cap + rank, groups * cap)
    slot_ref[...] = slot
    x = emb_ref[...]
    unit = (x * lax.rsqrt(jnp.sum(x * x, axis=1, keepdims=True) + 1e-06)).astype(jnp.bfloat16)
    unit_ref[...] = unit
    write_chunks(slot, unit, cap, chunk_refs, numbers)


def rest_kernel(groups, cap, group_size, numbers, dest_ref, slot_ref, unit_ref, place_ref, *chunk_refs):
    rows_dev = unit_ref.shape[0]
    slot = slot_ref[...]
    write_chunks(slot, unit_ref[...], cap, chunk_refs, numbers)
    dest = dest_ref[...]
    place = dest
    for g in range(1, groups):
        place -= jnp.where(dest >= g * group_size, group_size, 0)
    high = lax.shift_right_logical(place, 7)
    low = jnp.bitwise_and(place, 127)
    kind = lax.broadcasted_iota(jnp.int32, (16, rows_dev), 0)
    facts = jnp.where(kind == 0, high, jnp.where(kind == 1, low, jnp.where(kind == 2, 1, 0)))
    facts = facts.astype(jnp.float32).astype(jnp.bfloat16)
    pick = (lax.broadcasted_iota(jnp.int32, (groups * cap, rows_dev), 0) == slot).astype(jnp.bfloat16)
    got = lax.dot_general(facts, pick, NT, preferred_element_type=jnp.float32).astype(jnp.int32)
    there = got[2:3, :] > 0
    place_ref[...] = jnp.where(there, got[0:1, :] * 128 + got[1:2, :], group_size)


class Best:
    def __init__(self, start):
        self.row, self.column = start, None

    def add_row(self, row):
        self.row = jnp.maximum(self.row, row)

    def add_column(self, column):
        self.column = column if self.column is None else jnp.maximum(self.column, column)

    def as_row(self):
        if self.column is None:
            return self.row
        n = self.column.shape[0]
        eye = lax.broadcasted_iota(jnp.int32, (n, n), 0) == lax.broadcasted_iota(jnp.int32, (n, n), 1)
        return jnp.maximum(self.row, jnp.max(jnp.where(eye, self.column, -1.0), axis=0, keepdims=True))


def similar(left, right, left_label, right_label, shift=None):
    sims = lax.dot_general(left, right, NT, preferred_element_type=jnp.float32)
    keep = left_label == right_label
    if shift is not None:
        keep &= lax.broadcasted_iota(jnp.int32, sims.shape, 0) != lax.broadcasted_iota(jnp.int32, sims.shape, 1) + shift
    return jnp.where(keep, sims, -1.0)


def row_max(sims):
    return jnp.max(sims, axis=1, keepdims=True)


def column_max(sims):
    return jnp.max(sims, axis=0, keepdims=True)


def loader(chunks, count, blocks, sems):
    number = len(chunks) // count
    cap = chunks[0].shape[0]

    def copy(j, k):
        return pltpu.make_async_copy(chunks[j * number + k], blocks.at[j, pl.ds(k * cap, cap)], sems.at[j, k])

    for j, k in itertools.product(range(count), range(number)):
        copy(j, k).start()
    here = set()

    def need(*wanted):
        for j in sorted(set(wanted) - here):
            for k in range(number):
                copy(j, k).wait()
            here.add(j)

    return need


def early_kernel(pairs, count, early, *refs):
    *chunks, label_ref, label_col_ref, out_ref, blocks, sems = refs
    need = loader(chunks, count, blocks, sems)
    best = [Best(jnp.full((1, early), -1.0, jnp.float32)) for _ in range(count)]
    for j, k in pairs:
        need(j, k)
        sims = similar(
            blocks[j, :early],
            blocks[k, :early],
            label_col_ref[:, j : j + 1],
            label_ref[k : k + 1, :],
            0 if j == k else None,
        )
        best[k].add_row(column_max(sims))
        if j != k:
            best[j].add_column(row_max(sims))
    for j in range(count):
        out_ref[j : j + 1, :] = best[j].as_row()


def late_kernel(pairs, count, number, group_size, *refs):
    index_ref, *chunks = refs[: 1 + number]
    best_ref, place_ref, last_place_ref, label_ref, last_label_ref, label_col_ref, *out_refs = refs[1 + number : -3]
    whole, blocks, sems = refs[-3:]
    need = loader(chunks, count, blocks, sems)
    first = best_ref.shape[1]
    rest = blocks.shape[1] - first
    early = [Best(best_ref[j : j + 1, :]) for j in range(count)]
    late = [Best(jnp.full((1, rest), -1.0, jnp.float32)) for _ in range(count)]
    for j, k in pairs:
        need(j, k)
        sims = similar(
            blocks[j],
            blocks[k, first:],
            label_col_ref[:, j : j + 1],
            last_label_ref[k : k + 1, :],
            first if j == k else None,
        )
        column = row_max(sims)
        early[j].add_column(column[:first])
        late[k].add_row(column_max(sims))
        if j != k:
            late[j].add_column(column[first:])
            sims = similar(
                blocks[j, first:], blocks[k, :first], label_col_ref[first:, j : j + 1], label_ref[k : k + 1, :]
            )
            early[k].add_row(column_max(sims))
            late[j].add_column(row_max(sims))
    tall = group_size // 128
    pieces = [(early[j], place_ref[j : j + 1, :]) for j in range(count)]
    pieces += [(late[j], last_place_ref[j : j + 1, :]) for j in range(count)]
    spread = jnp.zeros((4 * tall, 128), jnp.float32)
    for best, place in pieces:
        best = best.as_row()
        slots = best.shape[1]
        high = lax.broadcasted_iota(jnp.int32, (tall, slots), 0) == lax.shift_right_logical(place, 7)
        low = lax.broadcasted_iota(jnp.int32, (128, slots), 0) == jnp.bitwise_and(place, 127)
        parts, rest = [], best
        for _ in range(3):
            part = rest.astype(jnp.bfloat16).astype(jnp.float32)
            rest = rest - part
            parts.append(part)
        parts.append(jnp.ones_like(best))
        stack = jnp.concatenate([jnp.where(high, part, 0.0) for part in parts], axis=0).astype(jnp.bfloat16)
        spread += lax.dot_general(stack, low.astype(jnp.bfloat16), NT, preferred_element_type=jnp.float32)
    value = spread[:tall] + spread[tall : 2 * tall] + spread[2 * tall : 3 * tall]
    value = jnp.where(spread[3 * tall :] > 0.5, value, -1.0)
    parts_of, lines = len(out_refs), value.shape[0] // len(out_refs)
    for c in range(parts_of):
        whole[c] = value[c * lines : (c + 1) * lines]
    for k, ref in enumerate(out_refs):
        ref[...] = whole[lax.rem(index_ref[0] + k, parts_of)]


def best_matches(cap, embeddings, dest_pos, cluster_ids):
    n_row, n_col = lax.axis_size("row"), lax.axis_size("col")
    devs = n_row * n_col
    groups, wide = n_row, n_col // n_row
    rows_dev, width = embeddings.shape
    group_size = rows_dev * n_col
    slots = groups * cap
    held, pairs = plane_plan(n_row, wide)
    count = len(held)

    assert groups & (groups - 1) == 0
    row, col = lax.axis_index("row"), lax.axis_index("col")
    plane, index = col // wide, row * wide + col % wide

    def device(i, h):
        return (i // wide) * n_col + h * wide + i % wide

    planes = [(i, h) for h in range(groups) for i in range(n_row * wide)]
    numbers, others = tuple(range(min(3, groups))), tuple(range(3, groups))
    chunk_shape = jax.ShapeDtypeStruct((cap, width), jnp.bfloat16)
    dest_row = dest_pos.reshape(1, rows_dev)
    plane_ref = plane.astype(jnp.int32).reshape(1)
    unit, slot, *made = pl.pallas_call(
        functools.partial(unit_kernel, groups, cap, group_size, numbers),
        out_shape=[
            jax.ShapeDtypeStruct((rows_dev, width), jnp.bfloat16),
            jax.ShapeDtypeStruct((1, rows_dev), jnp.int32),
            *[chunk_shape] * len(numbers),
        ],
        in_specs=[pl.BlockSpec(memory_space=pltpu.SMEM), VMEM, VMEM],
        out_specs=[VMEM] * (2 + len(numbers)),
        compiler_params=kernel_params(20),
    )(plane_ref, dest_row, embeddings)
    place, *more = pl.pallas_call(
        functools.partial(rest_kernel, groups, cap, group_size, others),
        out_shape=[jax.ShapeDtypeStruct((1, slots), jnp.int32), *[chunk_shape] * len(others)],
        in_specs=[VMEM] * 3,
        out_specs=[VMEM] * (1 + len(others)),
        compiler_params=kernel_params(20),
    )(dest_row, slot, unit)
    parts = dict(zip(numbers + others, made + more))

    def across(part, k):
        return lax.ppermute(part, AXES, [(device(i, h ^ k), device(i, h)) for i, h in planes])

    def inside(part, j):
        return lax.ppermute(part, AXES, [(device(int(held[j, i]), h), device(i, h)) for i, h in planes])

    def after(values, *done):
        return lax.optimization_barrier((values, done))[0]

    own = [parts[0]] + [across(parts[k], k) for k in range(1, min(3, groups))]
    near = inside(own[0], 1)
    rounds = [[near] + [inside(after(own[0], near), j) for j in range(2, count)]]
    rest = after([parts[k] for k in range(3, groups)], near)

    own += [across(part, k) for k, part in zip(range(3, groups), rest)]
    for k in range(1, groups - 1):
        part = after(own[k], *rounds[0]) if k == 1 else after(own[k], rounds[-1][0], *rounds[-2])
        near = after(part, own[k + 1]) if k > 1 else part
        rounds.append([inside(near, 1), *[inside(part, j) for j in range(2, count)]])

    place = after(place, rounds[1][0])

    planes_i = jnp.arange(groups, dtype=jnp.int32)
    swap = (planes_i[:, None] ^ planes_i[None, :]) == plane

    def by_plane(array):
        return jnp.sum(jnp.where(swap[:, :, None], array[None, :, :], 0), axis=1)

    levels = jnp.arange(LEVELS, dtype=jnp.int32)
    counts = jnp.sum((cluster_ids.reshape(1, rows_dev) <= levels[:, None]).astype(jnp.int32), axis=1)
    target_group = dest_pos // group_size
    most = jnp.max(jnp.sum((target_group[None, :] == jnp.arange(groups)[:, None]).astype(jnp.int32), axis=1))
    tail = jnp.concatenate([counts, (most > cap).astype(jnp.int32).reshape(1)])
    length = -(-(cap + LEVELS + 1) // 128) * 128
    facts = jnp.concatenate(
        [
            by_plane(place.reshape(groups, cap)),
            jnp.broadcast_to(tail[None, :], (groups, LEVELS + 1)),
            jnp.zeros((groups, length - cap - LEVELS - 1), jnp.int32),
        ],
        axis=1,
    )
    facts = jnp.broadcast_to(facts[None, :, None, :], (n_row, groups, wide, length)).reshape(devs, length)
    facts = lax.all_to_all(facts, AXES, split_axis=0, concat_axis=0, tiled=True)
    last = after(own[-1], facts, *rounds[-2])
    rounds.append([inside(after(last, rounds[-1][0]), 1), *[inside(last, j) for j in range(2, count)]])
    over = jnp.max(facts[:, cap + LEVELS]) > 0
    facts = facts.reshape(n_row, groups, wide, length)

    in_plane = (jnp.arange(n_row, dtype=jnp.int32) == plane).astype(jnp.int32)
    ends = jnp.sum(facts[..., cap : cap + LEVELS] * in_plane[:, None, None, None], axis=(0, 1, 2))
    places = by_plane(facts[..., :cap].transpose(1, 0, 2, 3).reshape(groups, n_row * wide * cap))
    places = places.reshape(groups, n_row * wide, cap).transpose(1, 0, 2).reshape(n_row * wide, slots)
    mine = jnp.sum(
        jnp.where(jnp.arange(n_row * wide)[None, :] == index, jnp.asarray(held, jnp.int32), 0), axis=1
    )
    mine = (mine[:, None] == jnp.arange(n_row * wide)[None, :]).astype(jnp.int32)
    places = jnp.sum(mine[:, :, None] * places[None, :, :], axis=1)
    labels = jnp.sum((places[:, None, :] >= ends[None, :, None]).astype(jnp.int32), axis=1)
    labels = jnp.where(places < group_size, labels, -1)

    early = (slots - cap) // 256 * 256
    label_cols = labels.T
    facts = places[:, :early], places[:, early:], labels[:, :early], labels[:, early:], label_cols[:early], label_cols
    place, last_place, label, last_label, label_col, label_cols = facts
    blocks = [own] + [[moved[j - 1] for moved in rounds] for j in range(1, count)]
    any_space = pl.BlockSpec(memory_space=pltpu.HBM)
    area = 4 * slots * slots

    def scratch(number):
        return [
            pltpu.VMEM((count, number * cap, width), jnp.bfloat16),
            pltpu.SemaphoreType.DMA((count, number)),
        ]

    limit = 8 + (2 * count * slots * width + 5 * area) // 2**20
    first_best = pl.pallas_call(
        functools.partial(early_kernel, pairs, count, early),
        out_shape=jax.ShapeDtypeStruct((count, early), jnp.float32),
        in_specs=[any_space] * (count * (groups - 1)) + [VMEM] * 2,
        out_specs=VMEM,
        scratch_shapes=scratch(groups - 1),
        compiler_params=kernel_params(limit),
        cost_estimate=pl.CostEstimate(
            flops=2 * len(pairs) * early * early * width, bytes_accessed=2 * count * early * width, transcendentals=0
        ),
    )(*[part for block in blocks for part in block[:-1]], label, label_col)
    best = pl.pallas_call(
        functools.partial(late_kernel, pairs, count, count * groups, group_size),
        out_shape=[jax.ShapeDtypeStruct((rows_dev // 128, 128), jnp.float32)] * n_col,
        in_specs=[pl.BlockSpec(memory_space=pltpu.SMEM)] + [any_space] * (count * groups) + [VMEM] * 6,
        out_specs=[VMEM] * n_col,
        scratch_shapes=[pltpu.VMEM((n_col, rows_dev // 128, 128), jnp.float32), *scratch(groups)],
        compiler_params=kernel_params(limit),
    )(
        index.astype(jnp.int32).reshape(1),
        *itertools.chain(*blocks),
        first_best,
        place,
        last_place,
        label,
        last_label,
        label_cols,
    )

    out = None
    for k, part in enumerate(best):
        moves = [(device(i, h), h * n_col + (i + k) % n_col) for i, h in planes]
        part = lax.ppermute(part, AXES, moves)
        out = part if out is None else jnp.maximum(out, part)
    return out.reshape(1, rows_dev), over


def shards(embeddings, dest_pos, cluster_ids):
    n_row, n_col = lax.axis_size("row"), lax.axis_size("col")
    rows_dev = embeddings.shape[0]
    devs = n_row * n_col
    most = min(rows_dev, n_col * max(4, 2 * rows_dev // devs))
    usual = min(most, -(-(rows_dev // n_row) * 11 // 8 // 16) * 16)
    args = (embeddings, dest_pos, cluster_ids)
    best, over = best_matches(usual, *args)
    if usual == most:
        return best
    return lax.cond(over, lambda: best_matches(most, *args)[0], lambda: best)


def solution(mesh):
    return jax.shard_map(
        shards,
        mesh=mesh,
        in_specs=(P(("row", "col"), None), P(("row", "col")), P("row", "col")),
        out_specs=P("row", "col"),
        check_vma=False,
    )
```

```python
import functools
import itertools

import jax
import jax.numpy as jnp
import numpy as np
from jax import lax
from jax.experimental import pallas as pl
from jax.experimental.pallas import tpu as pltpu
from jax.sharding import PartitionSpec as P

AXES = ("row", "col")
LEVELS = 16
NT = (((1,), (1,)), ((), ()))
VMEM = pl.BlockSpec(memory_space=pltpu.VMEM)


def kernel_params(mebibytes):
    return pltpu.CompilerParams(vmem_limit_bytes=mebibytes * 2**20)


def plane_plan(n_row, wide):
    n = n_row * wide
    if n_row == 4 and wide == 2:
        chips = [(0, 0), (0, 1), (1, 1), (1, 0)]

        def dev(chip, core):
            x, y = chips[chip % 4]
            return (x * 2 + core) * wide + y

        held = np.zeros((4, n), np.int64)
        for chip, core in itertools.product(range(4), range(2)):
            i = dev(chip, core)
            crossed = 1 - core if chip in (1, 2) else core
            held[:, i] = i, dev(chip, 1 - core), dev(chip + 1, core), dev(chip + 3, crossed)
        pairs = [(0, 0), (0, 1), (0, 2), (1, 2), (2, 3)]
    else:
        def covered(cover):
            return {(b - a) % n for a in cover for b in cover}

        size = 1
        while True:
            found = [c for c in itertools.combinations(range(n), size) if c[0] == 0 and len(covered(c)) == n]
            if found:
                break
            size += 1
        cover = found[0]
        held = (np.arange(n)[None, :] + np.array(cover)[:, None]) % n
        pairs, seen = [], set()
        for j, k in itertools.combinations_with_replacement(range(size), 2):
            delta = (cover[k] - cover[j]) % n
            if delta not in seen:
                seen |= {delta, (n - delta) % n}
                pairs.append((j, k))
    met = set()
    for j, k in pairs:
        for i in range(n):
            met |= {(held[j, i], held[k, i]), (held[k, i], held[j, i])}
    assert len(met) == n * n
    return held, pairs


def write_chunks(slot, unit, cap, chunk_refs, numbers):
    for ref, k in zip(chunk_refs, numbers):
        index = lax.broadcasted_iota(jnp.int32, (cap, unit.shape[0]), 0) + k * cap
        pick = (index == slot).astype(jnp.bfloat16)
        ref[...] = jnp.dot(pick, unit, preferred_element_type=jnp.float32).astype(jnp.bfloat16)


def unit_kernel(groups, cap, group_size, numbers, plane_ref, dest_ref, emb_ref, unit_ref, slot_ref, *chunk_refs):
    rows_dev = emb_ref.shape[0]
    dest = dest_ref[...]
    group = jnp.zeros_like(dest)
    for g in range(1, groups):
        group += (dest >= g * group_size).astype(jnp.int32)
    group = jnp.bitwise_xor(group, plane_ref[0])
    pad = -(-groups // 16) * 16
    member = lax.broadcasted_iota(jnp.int32, (pad, rows_dev), 0) == group
    earlier = lax.broadcasted_iota(jnp.int32, (rows_dev, rows_dev), 0) < lax.broadcasted_iota(
        jnp.int32, (rows_dev, rows_dev), 1
    )
    before = jnp.dot(member.astype(jnp.bfloat16), earlier.astype(jnp.bfloat16), preferred_element_type=jnp.float32)
    rank = jnp.sum(jnp.where(member, before, 0.0), axis=0, keepdims=True).astype(jnp.int32)
    slot = jnp.where(rank < cap, group * cap + rank, groups * cap)
    slot_ref[...] = slot
    x = emb_ref[...]
    unit = (x * lax.rsqrt(jnp.sum(x * x, axis=1, keepdims=True) + 1e-06)).astype(jnp.bfloat16)
    unit_ref[...] = unit
    write_chunks(slot, unit, cap, chunk_refs, numbers)


def rest_kernel(groups, cap, group_size, numbers, dest_ref, slot_ref, unit_ref, place_ref, *chunk_refs):
    rows_dev = unit_ref.shape[0]
    slot = slot_ref[...]
    write_chunks(slot, unit_ref[...], cap, chunk_refs, numbers)
    dest = dest_ref[...]
    place = dest
    for g in range(1, groups):
        place -= jnp.where(dest >= g * group_size, group_size, 0)
    high = lax.shift_right_logical(place, 7)
    low = jnp.bitwise_and(place, 127)
    kind = lax.broadcasted_iota(jnp.int32, (16, rows_dev), 0)
    facts = jnp.where(kind == 0, high, jnp.where(kind == 1, low, jnp.where(kind == 2, 1, 0)))
    facts = facts.astype(jnp.float32).astype(jnp.bfloat16)
    pick = (lax.broadcasted_iota(jnp.int32, (groups * cap, rows_dev), 0) == slot).astype(jnp.bfloat16)
    got = lax.dot_general(facts, pick, NT, preferred_element_type=jnp.float32).astype(jnp.int32)
    there = got[2:3, :] > 0
    place_ref[...] = jnp.where(there, got[0:1, :] * 128 + got[1:2, :], group_size)


class Best:
    def __init__(self, start):
        self.row, self.column = start, None

    def add_row(self, row):
        self.row = jnp.maximum(self.row, row)

    def add_column(self, column):
        self.column = column if self.column is None else jnp.maximum(self.column, column)

    def as_row(self):
        if self.column is None:
            return self.row
        n = self.column.shape[0]
        eye = lax.broadcasted_iota(jnp.int32, (n, n), 0) == lax.broadcasted_iota(jnp.int32, (n, n), 1)
        return jnp.maximum(self.row, jnp.max(jnp.where(eye, self.column, -1.0), axis=0, keepdims=True))


def similar(left, right, left_label, right_label, shift=None):
    sims = lax.dot_general(left, right, NT, preferred_element_type=jnp.float32)
    keep = left_label == right_label
    if shift is not None:
        keep &= lax.broadcasted_iota(jnp.int32, sims.shape, 0) != lax.broadcasted_iota(jnp.int32, sims.shape, 1) + shift
    return jnp.where(keep, sims, -1.0)


def row_max(sims):
    return jnp.max(sims, axis=1, keepdims=True)


def column_max(sims):
    return jnp.max(sims, axis=0, keepdims=True)


def loader(chunks, count, blocks, sems):
    number = len(chunks) // count
    cap = chunks[0].shape[0]

    def copy(j, k):
        return pltpu.make_async_copy(chunks[j * number + k], blocks.at[j, pl.ds(k * cap, cap)], sems.at[j, k])

    for j, k in itertools.product(range(count), range(number)):
        copy(j, k).start()
    here = set()

    def need(*wanted):
        for j in sorted(set(wanted) - here):
            for k in range(number):
                copy(j, k).wait()
            here.add(j)

    return need


def early_kernel(pairs, count, early, *refs):
    *chunks, label_ref, label_col_ref, out_ref, blocks, sems = refs
    need = loader(chunks, count, blocks, sems)
    best = [Best(jnp.full((1, early), -1.0, jnp.float32)) for _ in range(count)]
    for j, k in pairs:
        need(j, k)
        sims = similar(
            blocks[j, :early],
            blocks[k, :early],
            label_col_ref[:, j : j + 1],
            label_ref[k : k + 1, :],
            0 if j == k else None,
        )
        best[k].add_row(column_max(sims))
        if j != k:
            best[j].add_column(row_max(sims))
    for j in range(count):
        out_ref[j : j + 1, :] = best[j].as_row()


def late_kernel(pairs, count, group_size, *refs):
    plane_ref, *chunks, best_ref, place_ref, last_place_ref, label_ref, last_label_ref, label_col_ref, out_ref, blocks, sems = refs
    need = loader(chunks, count, blocks, sems)
    first = best_ref.shape[1]
    rest = blocks.shape[1] - first
    early = [Best(best_ref[j : j + 1, :]) for j in range(count)]
    late = [Best(jnp.full((1, rest), -1.0, jnp.float32)) for _ in range(count)]
    for j, k in pairs:
        need(j, k)
        sims = similar(
            blocks[j],
            blocks[k, first:],
            label_col_ref[:, j : j + 1],
            last_label_ref[k : k + 1, :],
            first if j == k else None,
        )
        column = row_max(sims)
        early[j].add_column(column[:first])
        late[k].add_row(column_max(sims))
        if j != k:
            late[j].add_column(column[first:])
            sims = similar(
                blocks[j, first:], blocks[k, :first], label_col_ref[first:, j : j + 1], label_ref[k : k + 1, :]
            )
            early[k].add_row(column_max(sims))
            late[j].add_column(row_max(sims))
    tall = group_size // 128
    pieces = [(early[j], place_ref[j : j + 1, :]) for j in range(count)]
    pieces += [(late[j], last_place_ref[j : j + 1, :]) for j in range(count)]
    spread = jnp.zeros((4 * tall, 128), jnp.float32)
    for best, place in pieces:
        best = best.as_row()
        slots = best.shape[1]
        high = lax.broadcasted_iota(jnp.int32, (tall, slots), 0) == lax.shift_right_logical(place, 7)
        low = lax.broadcasted_iota(jnp.int32, (128, slots), 0) == jnp.bitwise_and(place, 127)
        parts, rest = [], best
        for _ in range(3):
            part = rest.astype(jnp.bfloat16).astype(jnp.float32)
            rest = rest - part
            parts.append(part)
        parts.append(jnp.ones_like(best))
        stack = jnp.concatenate([jnp.where(high, part, 0.0) for part in parts], axis=0).astype(jnp.bfloat16)
        spread += lax.dot_general(stack, low.astype(jnp.bfloat16), NT, preferred_element_type=jnp.float32)
    value = spread[:tall] + spread[tall : 2 * tall] + spread[2 * tall : 3 * tall]
    value = jnp.where(spread[3 * tall :] > 0.5, value, -1.0)
    n_row, n_col, lines, _ = out_ref.shape
    for r in range(n_row):
        here = jnp.where(plane_ref[0] == r, value, -1.0)
        for c in range(n_col):
            out_ref[r, c] = here[c * lines : (c + 1) * lines]


def best_matches(cap, embeddings, dest_pos, cluster_ids):
    n_row, n_col = lax.axis_size("row"), lax.axis_size("col")
    devs = n_row * n_col
    groups, wide = n_row, n_col // n_row
    rows_dev, width = embeddings.shape
    group_size = rows_dev * n_col
    slots = groups * cap
    held, pairs = plane_plan(n_row, wide)
    count = len(held)

    assert groups & (groups - 1) == 0
    row, col = lax.axis_index("row"), lax.axis_index("col")
    plane, index = col // wide, row * wide + col % wide

    def device(i, h):
        return (i // wide) * n_col + h * wide + i % wide

    planes = [(i, h) for h in range(groups) for i in range(n_row * wide)]
    numbers, others = tuple(range(min(3, groups))), tuple(range(3, groups))
    chunk_shape = jax.ShapeDtypeStruct((cap, width), jnp.bfloat16)
    dest_row = dest_pos.reshape(1, rows_dev)
    plane_ref = plane.astype(jnp.int32).reshape(1)
    unit, slot, *made = pl.pallas_call(
        functools.partial(unit_kernel, groups, cap, group_size, numbers),
        out_shape=[
            jax.ShapeDtypeStruct((rows_dev, width), jnp.bfloat16),
            jax.ShapeDtypeStruct((1, rows_dev), jnp.int32),
            *[chunk_shape] * len(numbers),
        ],
        in_specs=[pl.BlockSpec(memory_space=pltpu.SMEM), VMEM, VMEM],
        out_specs=[VMEM] * (2 + len(numbers)),
        compiler_params=kernel_params(20),
    )(plane_ref, dest_row, embeddings)
    place, *more = pl.pallas_call(
        functools.partial(rest_kernel, groups, cap, group_size, others),
        out_shape=[jax.ShapeDtypeStruct((1, slots), jnp.int32), *[chunk_shape] * len(others)],
        in_specs=[VMEM] * 3,
        out_specs=[VMEM] * (1 + len(others)),
        compiler_params=kernel_params(20),
    )(dest_row, slot, unit)
    parts = dict(zip(numbers + others, made + more))

    def across(part, k):
        return lax.ppermute(part, AXES, [(device(i, h ^ k), device(i, h)) for i, h in planes])

    def inside(part, j):
        return lax.ppermute(part, AXES, [(device(int(held[j, i]), h), device(i, h)) for i, h in planes])

    def after(values, *done):
        return lax.optimization_barrier((values, done))[0]

    own = [parts[0]] + [across(parts[k], k) for k in range(1, min(3, groups))]
    near = inside(own[0], 1)
    rounds = [[near] + [inside(after(own[0], near), j) for j in range(2, count)]]
    rest = after([parts[k] for k in range(3, groups)], near)

    own += [across(part, k) for k, part in zip(range(3, groups), rest)]
    for k in range(1, groups - 1):
        part = after(own[k], *rounds[0]) if k == 1 else after(own[k], rounds[-1][0], *rounds[-2])
        near = after(part, own[k + 1]) if k > 1 else part
        rounds.append([inside(near, 1), *[inside(part, j) for j in range(2, count)]])

    place = after(place, *rounds[0])

    planes_i = jnp.arange(groups, dtype=jnp.int32)
    swap = (planes_i[:, None] ^ planes_i[None, :]) == plane

    def by_plane(array):
        return jnp.sum(jnp.where(swap[:, :, None], array[None, :, :], 0), axis=1)

    levels = jnp.arange(LEVELS, dtype=jnp.int32)
    counts = jnp.sum((cluster_ids.reshape(1, rows_dev) <= levels[:, None]).astype(jnp.int32), axis=1)
    target_group = dest_pos // group_size
    most = jnp.max(jnp.sum((target_group[None, :] == jnp.arange(groups)[:, None]).astype(jnp.int32), axis=1))
    tail = jnp.concatenate([counts, (most > cap).astype(jnp.int32).reshape(1)])
    length = -(-(cap + LEVELS + 1) // 128) * 128
    facts = jnp.concatenate(
        [
            by_plane(place.reshape(groups, cap)),
            jnp.broadcast_to(tail[None, :], (groups, LEVELS + 1)),
            jnp.zeros((groups, length - cap - LEVELS - 1), jnp.int32),
        ],
        axis=1,
    )
    facts = jnp.broadcast_to(facts[None, :, None, :], (n_row, groups, wide, length)).reshape(devs, length)
    facts = lax.all_to_all(facts, AXES, split_axis=0, concat_axis=0, tiled=True)
    last = after(own[-1], *rounds[-2], rounds[-1][1])
    rounds.append([inside(after(last, rounds[-1][0], facts), 1), *[inside(last, j) for j in range(2, count)]])
    over = jnp.max(facts[:, cap + LEVELS]) > 0
    facts = facts.reshape(n_row, groups, wide, length)

    in_plane = (jnp.arange(n_row, dtype=jnp.int32) == plane).astype(jnp.int32)
    ends = jnp.sum(facts[..., cap : cap + LEVELS] * in_plane[:, None, None, None], axis=(0, 1, 2))
    places = by_plane(facts[..., :cap].transpose(1, 0, 2, 3).reshape(groups, n_row * wide * cap))
    places = places.reshape(groups, n_row * wide, cap).transpose(1, 0, 2).reshape(n_row * wide, slots)
    mine = jnp.sum(
        jnp.where(jnp.arange(n_row * wide)[None, :] == index, jnp.asarray(held, jnp.int32), 0), axis=1
    )
    mine = (mine[:, None] == jnp.arange(n_row * wide)[None, :]).astype(jnp.int32)
    places = jnp.sum(mine[:, :, None] * places[None, :, :], axis=1)
    labels = jnp.sum((places[:, None, :] >= ends[None, :, None]).astype(jnp.int32), axis=1)
    labels = jnp.where(places < group_size, labels, -1)

    early = (slots - cap) // 256 * 256
    label_cols = labels.T
    facts = places[:, :early], places[:, early:], labels[:, :early], labels[:, early:], label_cols[:early], label_cols
    place, last_place, label, last_label, label_col, label_cols = facts
    blocks = [own] + [[moved[j - 1] for moved in rounds] for j in range(1, count)]
    any_space = pl.BlockSpec(memory_space=pltpu.HBM)
    area = 4 * slots * slots

    def scratch(number):
        return [
            pltpu.VMEM((count, number * cap, width), jnp.bfloat16),
            pltpu.SemaphoreType.DMA((count, number)),
        ]

    limit = 8 + (2 * count * slots * width + 5 * area) // 2**20
    first_best = pl.pallas_call(
        functools.partial(early_kernel, pairs, count, early),
        out_shape=jax.ShapeDtypeStruct((count, early), jnp.float32),
        in_specs=[any_space] * (count * (groups - 1)) + [VMEM] * 2,
        out_specs=VMEM,
        scratch_shapes=scratch(groups - 1),
        compiler_params=kernel_params(limit),
        cost_estimate=pl.CostEstimate(
            flops=2 * len(pairs) * early * early * width, bytes_accessed=2 * count * early * width, transcendentals=0
        ),
    )(*[part for block in blocks for part in block[:-1]], label, label_col)
    best = pl.pallas_call(
        functools.partial(late_kernel, pairs, count, group_size),
        out_shape=jax.ShapeDtypeStruct((n_row, n_col, rows_dev // 128, 128), jnp.float32),
        in_specs=[pl.BlockSpec(memory_space=pltpu.SMEM)] + [any_space] * (count * groups) + [VMEM] * 6,
        out_specs=VMEM,
        scratch_shapes=scratch(groups),
        compiler_params=kernel_params(limit),
    )(
        plane_ref,
        *itertools.chain(*blocks),
        first_best,
        place,
        last_place,
        label,
        last_label,
        label_cols,
    )

    best = lax.all_to_all(best.reshape(devs, -1, 128), AXES, split_axis=0, concat_axis=0, tiled=True)
    return jnp.max(best, axis=0).reshape(1, rows_dev), over


def shards(embeddings, dest_pos, cluster_ids):
    n_row, n_col = lax.axis_size("row"), lax.axis_size("col")
    rows_dev = embeddings.shape[0]
    devs = n_row * n_col
    most = min(rows_dev, n_col * max(4, 2 * rows_dev // devs))
    usual = min(most, -(-(rows_dev // n_row) * 11 // 8 // 16) * 16)
    args = (embeddings, dest_pos, cluster_ids)
    best, over = best_matches(usual, *args)
    if usual == most:
        return best
    return lax.cond(over, lambda: best_matches(most, *args)[0], lambda: best)


def solution(mesh):
    return jax.shard_map(
        shards,
        mesh=mesh,
        in_specs=(P(("row", "col"), None), P(("row", "col")), P("row", "col")),
        out_specs=P("row", "col"),
        check_vma=False,
    )
```

```python
import functools
import itertools

import jax
import jax.numpy as jnp
import numpy as np
from jax import lax
from jax.experimental import pallas as pl
from jax.experimental.pallas import tpu as pltpu
from jax.sharding import PartitionSpec as P

AXES = ("row", "col")
LEVELS = 16
NT = (((1,), (1,)), ((), ()))
VMEM = pl.BlockSpec(memory_space=pltpu.VMEM)


def kernel_params(mebibytes):
    return pltpu.CompilerParams(vmem_limit_bytes=mebibytes * 2**20)


def plane_plan(n_row, wide):
    n = n_row * wide
    if n_row == 4 and wide == 2:
        chips = [(0, 0), (0, 1), (1, 1), (1, 0)]

        def dev(chip, core):
            x, y = chips[chip % 4]
            return (x * 2 + core) * wide + y

        held = np.zeros((4, n), np.int64)
        for chip, core in itertools.product(range(4), range(2)):
            i = dev(chip, core)
            crossed = 1 - core if chip in (1, 2) else core
            held[:, i] = i, dev(chip, 1 - core), dev(chip + 1, core), dev(chip + 3, crossed)
        pairs = [(0, 0), (0, 1), (0, 2), (1, 2), (2, 3)]
    else:
        def covered(cover):
            return {(b - a) % n for a in cover for b in cover}

        size = 1
        while True:
            found = [c for c in itertools.combinations(range(n), size) if c[0] == 0 and len(covered(c)) == n]
            if found:
                break
            size += 1
        cover = found[0]
        held = (np.arange(n)[None, :] + np.array(cover)[:, None]) % n
        pairs, seen = [], set()
        for j, k in itertools.combinations_with_replacement(range(size), 2):
            delta = (cover[k] - cover[j]) % n
            if delta not in seen:
                seen |= {delta, (n - delta) % n}
                pairs.append((j, k))
    met = set()
    for j, k in pairs:
        for i in range(n):
            met |= {(held[j, i], held[k, i]), (held[k, i], held[j, i])}
    assert len(met) == n * n
    return held, pairs


def write_chunks(slot, unit, cap, chunk_refs, numbers):
    for ref, k in zip(chunk_refs, numbers):
        index = lax.broadcasted_iota(jnp.int32, (cap, unit.shape[0]), 0) + k * cap
        pick = (index == slot).astype(jnp.bfloat16)
        ref[...] = jnp.dot(pick, unit, preferred_element_type=jnp.float32).astype(jnp.bfloat16)


def unit_kernel(groups, cap, group_size, numbers, plane_ref, dest_ref, emb_ref, unit_ref, slot_ref, *chunk_refs):
    rows_dev = emb_ref.shape[0]
    dest = dest_ref[...]
    group = jnp.zeros_like(dest)
    for g in range(1, groups):
        group += (dest >= g * group_size).astype(jnp.int32)
    group = jnp.bitwise_xor(group, plane_ref[0])
    pad = -(-groups // 16) * 16
    member = lax.broadcasted_iota(jnp.int32, (pad, rows_dev), 0) == group
    earlier = lax.broadcasted_iota(jnp.int32, (rows_dev, rows_dev), 0) < lax.broadcasted_iota(
        jnp.int32, (rows_dev, rows_dev), 1
    )
    before = jnp.dot(member.astype(jnp.bfloat16), earlier.astype(jnp.bfloat16), preferred_element_type=jnp.float32)
    rank = jnp.sum(jnp.where(member, before, 0.0), axis=0, keepdims=True).astype(jnp.int32)
    slot = jnp.where(rank < cap, group * cap + rank, groups * cap)
    slot_ref[...] = slot
    x = emb_ref[...]
    unit = (x * lax.rsqrt(jnp.sum(x * x, axis=1, keepdims=True) + 1e-06)).astype(jnp.bfloat16)
    unit_ref[...] = unit
    write_chunks(slot, unit, cap, chunk_refs, numbers)


def rest_kernel(groups, cap, group_size, numbers, dest_ref, slot_ref, unit_ref, place_ref, *chunk_refs):
    rows_dev = unit_ref.shape[0]
    slot = slot_ref[...]
    write_chunks(slot, unit_ref[...], cap, chunk_refs, numbers)
    dest = dest_ref[...]
    place = dest
    for g in range(1, groups):
        place -= jnp.where(dest >= g * group_size, group_size, 0)
    high = lax.shift_right_logical(place, 7)
    low = jnp.bitwise_and(place, 127)
    kind = lax.broadcasted_iota(jnp.int32, (16, rows_dev), 0)
    facts = jnp.where(kind == 0, high, jnp.where(kind == 1, low, jnp.where(kind == 2, 1, 0)))
    facts = facts.astype(jnp.float32).astype(jnp.bfloat16)
    pick = (lax.broadcasted_iota(jnp.int32, (groups * cap, rows_dev), 0) == slot).astype(jnp.bfloat16)
    got = lax.dot_general(facts, pick, NT, preferred_element_type=jnp.float32).astype(jnp.int32)
    there = got[2:3, :] > 0
    place_ref[...] = jnp.where(there, got[0:1, :] * 128 + got[1:2, :], group_size)


class Best:
    def __init__(self, start):
        self.row, self.column = start, None

    def add_row(self, row):
        self.row = jnp.maximum(self.row, row)

    def add_column(self, column):
        self.column = column if self.column is None else jnp.maximum(self.column, column)

    def as_row(self):
        if self.column is None:
            return self.row
        n = self.column.shape[0]
        eye = lax.broadcasted_iota(jnp.int32, (n, n), 0) == lax.broadcasted_iota(jnp.int32, (n, n), 1)
        return jnp.maximum(self.row, jnp.max(jnp.where(eye, self.column, -1.0), axis=0, keepdims=True))


def similar(left, right, left_label, right_label, shift=None):
    sims = lax.dot_general(left, right, NT, preferred_element_type=jnp.float32)
    keep = left_label == right_label
    if shift is not None:
        keep &= lax.broadcasted_iota(jnp.int32, sims.shape, 0) != lax.broadcasted_iota(jnp.int32, sims.shape, 1) + shift
    return jnp.where(keep, sims, -1.0)


def row_max(sims):
    return jnp.max(sims, axis=1, keepdims=True)


def column_max(sims):
    return jnp.max(sims, axis=0, keepdims=True)


def loader(chunks, count, blocks, sems):
    number = len(chunks) // count
    cap = chunks[0].shape[0]

    def copy(j, k):
        return pltpu.make_async_copy(chunks[j * number + k], blocks.at[j, pl.ds(k * cap, cap)], sems.at[j, k])

    for j, k in itertools.product(range(count), range(number)):
        copy(j, k).start()
    here = set()

    def need(*wanted):
        for j in sorted(set(wanted) - here):
            for k in range(number):
                copy(j, k).wait()
            here.add(j)

    return need


def early_kernel(pairs, count, early, *refs):
    *chunks, label_ref, label_col_ref, out_ref, blocks, sems = refs
    need = loader(chunks, count, blocks, sems)
    best = [Best(jnp.full((1, early), -1.0, jnp.float32)) for _ in range(count)]
    for j, k in pairs:
        need(j, k)
        sims = similar(
            blocks[j, :early],
            blocks[k, :early],
            label_col_ref[:, j : j + 1],
            label_ref[k : k + 1, :],
            0 if j == k else None,
        )
        best[k].add_row(column_max(sims))
        if j != k:
            best[j].add_column(row_max(sims))
    for j in range(count):
        out_ref[j : j + 1, :] = best[j].as_row()


def late_kernel(pairs, count, group_size, *refs):
    plane_ref, *chunks, best_ref, place_ref, last_place_ref, label_ref, last_label_ref, label_col_ref, out_ref, blocks, sems = refs
    need = loader(chunks, count, blocks, sems)
    first = best_ref.shape[1]
    rest = blocks.shape[1] - first
    early = [Best(best_ref[j : j + 1, :]) for j in range(count)]
    late = [Best(jnp.full((1, rest), -1.0, jnp.float32)) for _ in range(count)]
    for j, k in pairs:
        need(j, k)
        sims = similar(
            blocks[j],
            blocks[k, first:],
            label_col_ref[:, j : j + 1],
            last_label_ref[k : k + 1, :],
            first if j == k else None,
        )
        column = row_max(sims)
        early[j].add_column(column[:first])
        late[k].add_row(column_max(sims))
        if j != k:
            late[j].add_column(column[first:])
            sims = similar(
                blocks[j, first:], blocks[k, :first], label_col_ref[first:, j : j + 1], label_ref[k : k + 1, :]
            )
            early[k].add_row(column_max(sims))
            late[j].add_column(row_max(sims))
    tall = group_size // 128
    pieces = [(early[j], place_ref[j : j + 1, :]) for j in range(count)]
    pieces += [(late[j], last_place_ref[j : j + 1, :]) for j in range(count)]
    spread = jnp.zeros((4 * tall, 128), jnp.float32)
    for best, place in pieces:
        best = best.as_row()
        slots = best.shape[1]
        high = lax.broadcasted_iota(jnp.int32, (tall, slots), 0) == lax.shift_right_logical(place, 7)
        low = lax.broadcasted_iota(jnp.int32, (128, slots), 0) == jnp.bitwise_and(place, 127)
        parts, rest = [], best
        for _ in range(3):
            part = rest.astype(jnp.bfloat16).astype(jnp.float32)
            rest = rest - part
            parts.append(part)
        parts.append(jnp.ones_like(best))
        stack = jnp.concatenate([jnp.where(high, part, 0.0) for part in parts], axis=0).astype(jnp.bfloat16)
        spread += lax.dot_general(stack, low.astype(jnp.bfloat16), NT, preferred_element_type=jnp.float32)
    value = spread[:tall] + spread[tall : 2 * tall] + spread[2 * tall : 3 * tall]
    value = jnp.where(spread[3 * tall :] > 0.5, value, -1.0)
    n_row, n_col, lines, _ = out_ref.shape
    for r in range(n_row):
        here = jnp.where(plane_ref[0] == r, value, -1.0)
        for c in range(n_col):
            out_ref[r, c] = here[c * lines : (c + 1) * lines]


def best_matches(cap, embeddings, dest_pos, cluster_ids):
    n_row, n_col = lax.axis_size("row"), lax.axis_size("col")
    devs = n_row * n_col
    groups, wide = n_row, n_col // n_row
    rows_dev, width = embeddings.shape
    group_size = rows_dev * n_col
    slots = groups * cap
    held, pairs = plane_plan(n_row, wide)
    count = len(held)

    assert groups & (groups - 1) == 0
    row, col = lax.axis_index("row"), lax.axis_index("col")
    plane, index = col // wide, row * wide + col % wide

    def device(i, h):
        return (i // wide) * n_col + h * wide + i % wide

    planes = [(i, h) for h in range(groups) for i in range(n_row * wide)]
    numbers, others = tuple(range(min(3, groups))), tuple(range(3, groups))
    chunk_shape = jax.ShapeDtypeStruct((cap, width), jnp.bfloat16)
    dest_row = dest_pos.reshape(1, rows_dev)
    plane_ref = plane.astype(jnp.int32).reshape(1)
    unit, slot, *made = pl.pallas_call(
        functools.partial(unit_kernel, groups, cap, group_size, numbers),
        out_shape=[
            jax.ShapeDtypeStruct((rows_dev, width), jnp.bfloat16),
            jax.ShapeDtypeStruct((1, rows_dev), jnp.int32),
            *[chunk_shape] * len(numbers),
        ],
        in_specs=[pl.BlockSpec(memory_space=pltpu.SMEM), VMEM, VMEM],
        out_specs=[VMEM] * (2 + len(numbers)),
        compiler_params=kernel_params(20),
    )(plane_ref, dest_row, embeddings)
    place, *more = pl.pallas_call(
        functools.partial(rest_kernel, groups, cap, group_size, others),
        out_shape=[jax.ShapeDtypeStruct((1, slots), jnp.int32), *[chunk_shape] * len(others)],
        in_specs=[VMEM] * 3,
        out_specs=[VMEM] * (1 + len(others)),
        compiler_params=kernel_params(20),
    )(dest_row, slot, unit)
    parts = dict(zip(numbers + others, made + more))

    def across(part, k):
        return lax.ppermute(part, AXES, [(device(i, h ^ k), device(i, h)) for i, h in planes])

    def inside(part, j):
        return lax.ppermute(part, AXES, [(device(int(held[j, i]), h), device(i, h)) for i, h in planes])

    def after(values, *done):
        return lax.optimization_barrier((values, done))[0]

    own = [parts[0]] + [across(parts[k], k) for k in range(1, min(3, groups))]
    near = inside(own[0], 1)
    rounds = [[near] + [inside(after(own[0], near), j) for j in range(2, count)]]
    rest = after([parts[k] for k in range(3, groups)], near)

    own += [across(part, k) for k, part in zip(range(3, groups), rest)]
    for k in range(1, groups - 1):
        part = after(own[k], *rounds[0]) if k == 1 else after(own[k], rounds[-1][0], *rounds[-2])
        near = after(part, own[k + 1]) if k > 1 else part
        rounds.append([inside(near, 1), *[inside(part, j) for j in range(2, count)]])

    last = after(own[-1], *rounds[-2])
    rounds.append([inside(after(last, rounds[-1][0]), 1), *[inside(last, j) for j in range(2, count)]])
    place = after(place, rounds[1][0])

    planes_i = jnp.arange(groups, dtype=jnp.int32)
    swap = (planes_i[:, None] ^ planes_i[None, :]) == plane

    def by_plane(array):
        return jnp.sum(jnp.where(swap[:, :, None], array[None, :, :], 0), axis=1)

    levels = jnp.arange(LEVELS, dtype=jnp.int32)
    counts = jnp.sum((cluster_ids.reshape(1, rows_dev) <= levels[:, None]).astype(jnp.int32), axis=1)
    target_group = dest_pos // group_size
    most = jnp.max(jnp.sum((target_group[None, :] == jnp.arange(groups)[:, None]).astype(jnp.int32), axis=1))
    tail = jnp.concatenate([counts, (most > cap).astype(jnp.int32).reshape(1)])
    length = -(-(cap + LEVELS + 1) // 128) * 128
    facts = jnp.concatenate(
        [
            by_plane(place.reshape(groups, cap)),
            jnp.broadcast_to(tail[None, :], (groups, LEVELS + 1)),
            jnp.zeros((groups, length - cap - LEVELS - 1), jnp.int32),
        ],
        axis=1,
    )
    facts = jnp.broadcast_to(facts[None, :, None, :], (n_row, groups, wide, length)).reshape(devs, length)
    facts = lax.all_to_all(facts, AXES, split_axis=0, concat_axis=0, tiled=True)
    over = jnp.max(facts[:, cap + LEVELS]) > 0
    facts = facts.reshape(n_row, groups, wide, length)

    in_plane = (jnp.arange(n_row, dtype=jnp.int32) == plane).astype(jnp.int32)
    ends = jnp.sum(facts[..., cap : cap + LEVELS] * in_plane[:, None, None, None], axis=(0, 1, 2))
    places = by_plane(facts[..., :cap].transpose(1, 0, 2, 3).reshape(groups, n_row * wide * cap))
    places = places.reshape(groups, n_row * wide, cap).transpose(1, 0, 2).reshape(n_row * wide, slots)
    mine = jnp.sum(
        jnp.where(jnp.arange(n_row * wide)[None, :] == index, jnp.asarray(held, jnp.int32), 0), axis=1
    )
    mine = (mine[:, None] == jnp.arange(n_row * wide)[None, :]).astype(jnp.int32)
    places = jnp.sum(mine[:, :, None] * places[None, :, :], axis=1)
    labels = jnp.sum((places[:, None, :] >= ends[None, :, None]).astype(jnp.int32), axis=1)
    labels = jnp.where(places < group_size, labels, -1)

    early = (slots - cap) // 256 * 256
    label_cols = labels.T
    facts = places[:, :early], places[:, early:], labels[:, :early], labels[:, early:], label_cols[:early], label_cols
    place, last_place, label, last_label, label_col, label_cols = facts
    blocks = [own] + [[moved[j - 1] for moved in rounds] for j in range(1, count)]
    any_space = pl.BlockSpec(memory_space=pltpu.HBM)
    area = 4 * slots * slots

    def scratch(number):
        return [
            pltpu.VMEM((count, number * cap, width), jnp.bfloat16),
            pltpu.SemaphoreType.DMA((count, number)),
        ]

    limit = 8 + (2 * count * slots * width + 5 * area) // 2**20
    first_best = pl.pallas_call(
        functools.partial(early_kernel, pairs, count, early),
        out_shape=jax.ShapeDtypeStruct((count, early), jnp.float32),
        in_specs=[any_space] * (count * (groups - 1)) + [VMEM] * 2,
        out_specs=VMEM,
        scratch_shapes=scratch(groups - 1),
        compiler_params=kernel_params(limit),
        cost_estimate=pl.CostEstimate(
            flops=2 * len(pairs) * early * early * width, bytes_accessed=2 * count * early * width, transcendentals=0
        ),
    )(*[part for block in blocks for part in block[:-1]], label, label_col)
    best = pl.pallas_call(
        functools.partial(late_kernel, pairs, count, group_size),
        out_shape=jax.ShapeDtypeStruct((n_row, n_col, rows_dev // 128, 128), jnp.float32),
        in_specs=[pl.BlockSpec(memory_space=pltpu.SMEM)] + [any_space] * (count * groups) + [VMEM] * 6,
        out_specs=VMEM,
        scratch_shapes=scratch(groups),
        compiler_params=kernel_params(limit),
    )(
        plane_ref,
        *itertools.chain(*blocks),
        first_best,
        place,
        last_place,
        label,
        last_label,
        label_cols,
    )

    best = lax.all_to_all(best.reshape(devs, -1, 128), AXES, split_axis=0, concat_axis=0, tiled=True)
    return jnp.max(best, axis=0).reshape(1, rows_dev), over


def shards(embeddings, dest_pos, cluster_ids):
    n_row, n_col = lax.axis_size("row"), lax.axis_size("col")
    rows_dev = embeddings.shape[0]
    devs = n_row * n_col
    most = min(rows_dev, n_col * max(4, 2 * rows_dev // devs))
    usual = min(most, -(-(rows_dev // n_row) * 11 // 8 // 16) * 16)
    args = (embeddings, dest_pos, cluster_ids)
    best, over = best_matches(usual, *args)
    if usual == most:
        return best
    return lax.cond(over, lambda: best_matches(most, *args)[0], lambda: best)


def solution(mesh):
    return jax.shard_map(
        shards,
        mesh=mesh,
        in_specs=(P(("row", "col"), None), P(("row", "col")), P("row", "col")),
        out_specs=P("row", "col"),
        check_vma=False,
    )
```

```python
import functools
import itertools

import jax
import jax.numpy as jnp
import numpy as np
from jax import lax
from jax.experimental import pallas as pl
from jax.experimental.pallas import tpu as pltpu
from jax.sharding import PartitionSpec as P

AXES = ("row", "col")
LEVELS = 16
NT = (((1,), (1,)), ((), ()))
VMEM = pl.BlockSpec(memory_space=pltpu.VMEM)


def kernel_params(mebibytes):
    return pltpu.CompilerParams(vmem_limit_bytes=mebibytes * 2**20)


def plane_plan(n_row, wide):
    n = n_row * wide
    if n_row == 4 and wide == 2:
        chips = [(0, 0), (0, 1), (1, 1), (1, 0)]

        def dev(chip, core):
            x, y = chips[chip % 4]
            return (x * 2 + core) * wide + y

        held = np.zeros((4, n), np.int64)
        for chip, core in itertools.product(range(4), range(2)):
            i = dev(chip, core)
            crossed = 1 - core if chip in (1, 2) else core
            held[:, i] = i, dev(chip, 1 - core), dev(chip + 1, core), dev(chip + 3, crossed)
        pairs = [(0, 0), (0, 1), (0, 2), (1, 2), (2, 3)]
    else:
        def covered(cover):
            return {(b - a) % n for a in cover for b in cover}

        size = 1
        while True:
            found = [c for c in itertools.combinations(range(n), size) if c[0] == 0 and len(covered(c)) == n]
            if found:
                break
            size += 1
        cover = found[0]
        held = (np.arange(n)[None, :] + np.array(cover)[:, None]) % n
        pairs, seen = [], set()
        for j, k in itertools.combinations_with_replacement(range(size), 2):
            delta = (cover[k] - cover[j]) % n
            if delta not in seen:
                seen |= {delta, (n - delta) % n}
                pairs.append((j, k))
    met = set()
    for j, k in pairs:
        for i in range(n):
            met |= {(held[j, i], held[k, i]), (held[k, i], held[j, i])}
    assert len(met) == n * n
    return held, pairs


def pack_kernel(groups, cap, group_size, plane_ref, dest_ref, emb_ref, place_ref, *chunk_refs):
    rows_dev = emb_ref.shape[0]
    dest = dest_ref[...]
    group, place = jnp.zeros_like(dest), dest
    for g in range(1, groups):
        above = dest >= g * group_size
        group += above.astype(jnp.int32)
        place -= jnp.where(above, group_size, 0)
    group = jnp.bitwise_xor(group, plane_ref[0])
    pad = -(-groups // 16) * 16
    member = lax.broadcasted_iota(jnp.int32, (pad, rows_dev), 0) == group
    earlier = lax.broadcasted_iota(jnp.int32, (rows_dev, rows_dev), 0) < lax.broadcasted_iota(
        jnp.int32, (rows_dev, rows_dev), 1
    )
    before = jnp.dot(member.astype(jnp.bfloat16), earlier.astype(jnp.bfloat16), preferred_element_type=jnp.float32)
    rank = jnp.sum(jnp.where(member, before, 0.0), axis=0, keepdims=True).astype(jnp.int32)
    slot = jnp.where(rank < cap, group * cap + rank, groups * cap)
    pick = (lax.broadcasted_iota(jnp.int32, (groups * cap, rows_dev), 0) == slot).astype(jnp.bfloat16)
    x = emb_ref[...]
    unit = (x * lax.rsqrt(jnp.sum(x * x, axis=1, keepdims=True) + 1e-06)).astype(jnp.bfloat16)
    for k, ref in enumerate(chunk_refs):
        chunk = jnp.dot(pick[k * cap : (k + 1) * cap], unit, preferred_element_type=jnp.float32)
        ref[...] = chunk.astype(jnp.bfloat16)
    high = lax.shift_right_logical(place, 7)
    low = jnp.bitwise_and(place, 127)
    kind = lax.broadcasted_iota(jnp.int32, (16, rows_dev), 0)
    facts = jnp.where(kind == 0, high, jnp.where(kind == 1, low, jnp.where(kind == 2, 1, 0)))
    facts = facts.astype(jnp.float32).astype(jnp.bfloat16)
    got = lax.dot_general(facts, pick, NT, preferred_element_type=jnp.float32).astype(jnp.int32)
    there = got[2:3, :] > 0
    place_ref[...] = jnp.where(there, got[0:1, :] * 128 + got[1:2, :], group_size)


class Best:
    def __init__(self, start):
        self.row, self.column = start, None

    def add_row(self, row):
        self.row = jnp.maximum(self.row, row)

    def add_column(self, column):
        self.column = column if self.column is None else jnp.maximum(self.column, column)

    def as_row(self):
        if self.column is None:
            return self.row
        n = self.column.shape[0]
        eye = lax.broadcasted_iota(jnp.int32, (n, n), 0) == lax.broadcasted_iota(jnp.int32, (n, n), 1)
        return jnp.maximum(self.row, jnp.max(jnp.where(eye, self.column, -1.0), axis=0, keepdims=True))


def similar(left, right, left_label, right_label, shift=None):
    sims = lax.dot_general(left, right, NT, preferred_element_type=jnp.float32)
    keep = left_label == right_label
    if shift is not None:
        keep &= lax.broadcasted_iota(jnp.int32, sims.shape, 0) != lax.broadcasted_iota(jnp.int32, sims.shape, 1) + shift
    return jnp.where(keep, sims, -1.0)


def row_max(sims):
    return jnp.max(sims, axis=1, keepdims=True)


def column_max(sims):
    return jnp.max(sims, axis=0, keepdims=True)


def loader(chunks, count, blocks, sems):
    number = len(chunks) // count
    cap = chunks[0].shape[0]

    def copy(j, k):
        return pltpu.make_async_copy(chunks[j * number + k], blocks.at[j, pl.ds(k * cap, cap)], sems.at[j, k])

    for j, k in itertools.product(range(count), range(number)):
        copy(j, k).start()
    here = set()

    def need(*wanted):
        for j in sorted(set(wanted) - here):
            for k in range(number):
                copy(j, k).wait()
            here.add(j)

    return need


def early_kernel(pairs, count, early, *refs):
    *chunks, label_ref, label_col_ref, out_ref, blocks, sems = refs
    need = loader(chunks, count, blocks, sems)
    best = [Best(jnp.full((1, early), -1.0, jnp.float32)) for _ in range(count)]
    for j, k in pairs:
        need(j, k)
        sims = similar(
            blocks[j, :early],
            blocks[k, :early],
            label_col_ref[:, j : j + 1],
            label_ref[k : k + 1, :],
            0 if j == k else None,
        )
        best[k].add_row(column_max(sims))
        if j != k:
            best[j].add_column(row_max(sims))
    for j in range(count):
        out_ref[j : j + 1, :] = best[j].as_row()


def late_kernel(pairs, count, group_size, *refs):
    plane_ref, *chunks, best_ref, place_ref, last_place_ref, label_ref, last_label_ref, label_col_ref, out_ref, blocks, sems = refs
    need = loader(chunks, count, blocks, sems)
    first = best_ref.shape[1]
    rest = blocks.shape[1] - first
    early = [Best(best_ref[j : j + 1, :]) for j in range(count)]
    late = [Best(jnp.full((1, rest), -1.0, jnp.float32)) for _ in range(count)]
    for j, k in pairs:
        need(j, k)
        sims = similar(
            blocks[j],
            blocks[k, first:],
            label_col_ref[:, j : j + 1],
            last_label_ref[k : k + 1, :],
            first if j == k else None,
        )
        column = row_max(sims)
        early[j].add_column(column[:first])
        late[k].add_row(column_max(sims))
        if j != k:
            late[j].add_column(column[first:])
            sims = similar(
                blocks[j, first:], blocks[k, :first], label_col_ref[first:, j : j + 1], label_ref[k : k + 1, :]
            )
            early[k].add_row(column_max(sims))
            late[j].add_column(row_max(sims))
    tall = group_size // 128
    pieces = [(early[j], place_ref[j : j + 1, :]) for j in range(count)]
    pieces += [(late[j], last_place_ref[j : j + 1, :]) for j in range(count)]
    spread = jnp.zeros((4 * tall, 128), jnp.float32)
    for best, place in pieces:
        best = best.as_row()
        slots = best.shape[1]
        high = lax.broadcasted_iota(jnp.int32, (tall, slots), 0) == lax.shift_right_logical(place, 7)
        low = lax.broadcasted_iota(jnp.int32, (128, slots), 0) == jnp.bitwise_and(place, 127)
        parts, rest = [], best
        for _ in range(3):
            part = rest.astype(jnp.bfloat16).astype(jnp.float32)
            rest = rest - part
            parts.append(part)
        parts.append(jnp.ones_like(best))
        stack = jnp.concatenate([jnp.where(high, part, 0.0) for part in parts], axis=0).astype(jnp.bfloat16)
        spread += lax.dot_general(stack, low.astype(jnp.bfloat16), NT, preferred_element_type=jnp.float32)
    value = spread[:tall] + spread[tall : 2 * tall] + spread[2 * tall : 3 * tall]
    value = jnp.where(spread[3 * tall :] > 0.5, value, -1.0)
    for r in range(out_ref.shape[0]):
        out_ref[r] = jnp.where(plane_ref[0] == r, value, -1.0)


def best_matches(cap, embeddings, dest_pos, cluster_ids):
    n_row, n_col = lax.axis_size("row"), lax.axis_size("col")
    devs = n_row * n_col
    groups, wide = n_row, n_col // n_row
    rows_dev, width = embeddings.shape
    group_size = rows_dev * n_col
    slots = groups * cap
    held, pairs = plane_plan(n_row, wide)
    count = len(held)

    assert groups & (groups - 1) == 0
    row, col = lax.axis_index("row"), lax.axis_index("col")
    plane, index = col // wide, row * wide + col % wide

    def device(i, h):
        return (i // wide) * n_col + h * wide + i % wide

    planes = [(i, h) for h in range(groups) for i in range(n_row * wide)]
    dest_row = dest_pos.reshape(1, rows_dev)
    plane_ref = plane.astype(jnp.int32).reshape(1)
    place, *parts = pl.pallas_call(
        functools.partial(pack_kernel, groups, cap, group_size),
        out_shape=[
            jax.ShapeDtypeStruct((1, slots), jnp.int32),
            *[jax.ShapeDtypeStruct((cap, width), jnp.bfloat16)] * groups,
        ],
        in_specs=[pl.BlockSpec(memory_space=pltpu.SMEM), VMEM, VMEM],
        out_specs=[VMEM] * (1 + groups),
        compiler_params=kernel_params(20),
    )(plane_ref, dest_row, embeddings)

    def across(part, k):
        return lax.ppermute(part, AXES, [(device(i, h ^ k), device(i, h)) for i, h in planes])

    def inside(part, j):
        return lax.ppermute(part, AXES, [(device(int(held[j, i]), h), device(i, h)) for i, h in planes])

    def after(values, *done):
        return lax.optimization_barrier((values, done))[0]

    own = [parts[0]] + [across(parts[k], k) for k in range(1, min(3, groups))]
    near = inside(own[0], 1)
    rounds = [[near] + [inside(after(own[0], near), j) for j in range(2, count)]]
    rest = after([parts[k] for k in range(3, groups)], near)

    own += [across(part, k) for k, part in zip(range(3, groups), rest)]
    for k in range(1, groups - 1):
        part = after(own[k], *rounds[0]) if k == 1 else after(own[k], rounds[-1][0], *rounds[-2])
        near = after(part, own[k + 1]) if k > 1 else part
        rounds.append([inside(near, 1), *[inside(part, j) for j in range(2, count)]])

    last = after(own[-1], *rounds[-2])
    rounds.append([inside(after(last, rounds[-1][0]), 1), *[inside(last, j) for j in range(2, count)]])
    place = after(place, rounds[1][0])

    planes_i = jnp.arange(groups, dtype=jnp.int32)
    swap = (planes_i[:, None] ^ planes_i[None, :]) == plane

    def by_plane(array):
        return jnp.sum(jnp.where(swap[:, :, None], array[None, :, :], 0), axis=1)

    levels = jnp.arange(LEVELS, dtype=jnp.int32)
    counts = jnp.sum((cluster_ids.reshape(1, rows_dev) <= levels[:, None]).astype(jnp.int32), axis=1)
    target_group = dest_pos // group_size
    most = jnp.max(jnp.sum((target_group[None, :] == jnp.arange(groups)[:, None]).astype(jnp.int32), axis=1))
    tail = jnp.concatenate([counts, (most > cap).astype(jnp.int32).reshape(1)])
    length = -(-(cap + LEVELS + 1) // 128) * 128
    facts = jnp.concatenate(
        [
            by_plane(place.reshape(groups, cap)),
            jnp.broadcast_to(tail[None, :], (groups, LEVELS + 1)),
            jnp.zeros((groups, length - cap - LEVELS - 1), jnp.int32),
        ],
        axis=1,
    )
    facts = jnp.broadcast_to(facts[None, :, None, :], (n_row, groups, wide, length)).reshape(devs, length)
    facts = lax.all_to_all(facts, AXES, split_axis=0, concat_axis=0, tiled=True)
    over = jnp.max(facts[:, cap + LEVELS]) > 0
    facts = facts.reshape(n_row, groups, wide, length)

    in_plane = (jnp.arange(n_row, dtype=jnp.int32) == plane).astype(jnp.int32)
    ends = jnp.sum(facts[..., cap : cap + LEVELS] * in_plane[:, None, None, None], axis=(0, 1, 2))
    places = by_plane(facts[..., :cap].transpose(1, 0, 2, 3).reshape(groups, n_row * wide * cap))
    places = places.reshape(groups, n_row * wide, cap).transpose(1, 0, 2).reshape(n_row * wide, slots)
    mine = jnp.sum(
        jnp.where(jnp.arange(n_row * wide)[None, :] == index, jnp.asarray(held, jnp.int32), 0), axis=1
    )
    mine = (mine[:, None] == jnp.arange(n_row * wide)[None, :]).astype(jnp.int32)
    places = jnp.sum(mine[:, :, None] * places[None, :, :], axis=1)
    labels = jnp.sum((places[:, None, :] >= ends[None, :, None]).astype(jnp.int32), axis=1)
    labels = jnp.where(places < group_size, labels, -1)

    early = (slots - cap) // 256 * 256
    label_cols = labels.T
    facts = places[:, :early], places[:, early:], labels[:, :early], labels[:, early:], label_cols[:early], label_cols
    place, last_place, label, last_label, label_col, label_cols = facts
    blocks = [own] + [[moved[j - 1] for moved in rounds] for j in range(1, count)]
    any_space = pl.BlockSpec(memory_space=pltpu.HBM)
    area = 4 * slots * slots

    def scratch(number):
        return [
            pltpu.VMEM((count, number * cap, width), jnp.bfloat16),
            pltpu.SemaphoreType.DMA((count, number)),
        ]

    limit = 8 + (2 * count * slots * width + 5 * area) // 2**20
    first_best = pl.pallas_call(
        functools.partial(early_kernel, pairs, count, early),
        out_shape=jax.ShapeDtypeStruct((count, early), jnp.float32),
        in_specs=[any_space] * (count * (groups - 1)) + [VMEM] * 2,
        out_specs=VMEM,
        scratch_shapes=scratch(groups - 1),
        compiler_params=kernel_params(limit),
        cost_estimate=pl.CostEstimate(
            flops=2 * len(pairs) * early * early * width, bytes_accessed=2 * count * early * width, transcendentals=0
        ),
    )(*[part for block in blocks for part in block[:-1]], label, label_col)
    best = pl.pallas_call(
        functools.partial(late_kernel, pairs, count, group_size),
        out_shape=jax.ShapeDtypeStruct((n_row, group_size // 128, 128), jnp.float32),
        in_specs=[pl.BlockSpec(memory_space=pltpu.SMEM)] + [any_space] * (count * groups) + [VMEM] * 6,
        out_specs=VMEM,
        scratch_shapes=scratch(groups),
        compiler_params=kernel_params(limit),
    )(
        plane_ref,
        *itertools.chain(*blocks),
        first_best,
        place,
        last_place,
        label,
        last_label,
        label_cols,
    )

    best = lax.all_to_all(best.reshape(devs, -1, 128), AXES, split_axis=0, concat_axis=0, tiled=True)
    return jnp.max(best, axis=0).reshape(1, rows_dev), over


def shards(embeddings, dest_pos, cluster_ids):
    n_row, n_col = lax.axis_size("row"), lax.axis_size("col")
    rows_dev = embeddings.shape[0]
    devs = n_row * n_col
    most = min(rows_dev, n_col * max(4, 2 * rows_dev // devs))
    usual = min(most, -(-(rows_dev // n_row) * 11 // 8 // 16) * 16)
    args = (embeddings, dest_pos, cluster_ids)
    best, over = best_matches(usual, *args)
    if usual == most:
        return best
    return lax.cond(over, lambda: best_matches(most, *args)[0], lambda: best)


def solution(mesh):
    return jax.shard_map(
        shards,
        mesh=mesh,
        in_specs=(P(("row", "col"), None), P(("row", "col")), P("row", "col")),
        out_specs=P("row", "col"),
        check_vma=False,
    )
```

```python
import functools
import itertools

import jax
import jax.numpy as jnp
import numpy as np
from jax import lax
from jax.experimental import pallas as pl
from jax.experimental.pallas import tpu as pltpu
from jax.sharding import PartitionSpec as P

AXES = ("row", "col")
LEVELS = 16
NT = (((1,), (1,)), ((), ()))
VMEM = pl.BlockSpec(memory_space=pltpu.VMEM)


def kernel_params(mebibytes):
    return pltpu.CompilerParams(vmem_limit_bytes=mebibytes * 2**20)


def plane_plan(n_row, wide):
    n = n_row * wide
    if n_row == 4 and wide == 2:
        chips = [(0, 0), (0, 1), (1, 1), (1, 0)]

        def dev(chip, core):
            x, y = chips[chip % 4]
            return (x * 2 + core) * wide + y

        held = np.zeros((4, n), np.int64)
        for chip, core in itertools.product(range(4), range(2)):
            i = dev(chip, core)
            crossed = 1 - core if chip in (1, 2) else core
            held[:, i] = i, dev(chip, 1 - core), dev(chip + 1, core), dev(chip + 3, crossed)
        pairs = [(0, 0), (0, 1), (0, 2), (1, 2), (2, 3)]
    else:
        def covered(cover):
            return {(b - a) % n for a in cover for b in cover}

        size = 1
        while True:
            found = [c for c in itertools.combinations(range(n), size) if c[0] == 0 and len(covered(c)) == n]
            if found:
                break
            size += 1
        cover = found[0]
        held = (np.arange(n)[None, :] + np.array(cover)[:, None]) % n
        pairs, seen = [], set()
        for j, k in itertools.combinations_with_replacement(range(size), 2):
            delta = (cover[k] - cover[j]) % n
            if delta not in seen:
                seen |= {delta, (n - delta) % n}
                pairs.append((j, k))
    met = set()
    for j, k in pairs:
        for i in range(n):
            met |= {(held[j, i], held[k, i]), (held[k, i], held[j, i])}
    assert len(met) == n * n
    return held, pairs


def pack_kernel(groups, cap, group_size, plane_ref, dest_ref, emb_ref, place_ref, *chunk_refs):
    rows_dev = emb_ref.shape[0]
    dest = dest_ref[...]
    group, place = jnp.zeros_like(dest), dest
    for g in range(1, groups):
        above = dest >= g * group_size
        group += above.astype(jnp.int32)
        place -= jnp.where(above, group_size, 0)
    group = jnp.bitwise_xor(group, plane_ref[0])
    pad = -(-groups // 16) * 16
    member = lax.broadcasted_iota(jnp.int32, (pad, rows_dev), 0) == group
    earlier = lax.broadcasted_iota(jnp.int32, (rows_dev, rows_dev), 0) < lax.broadcasted_iota(
        jnp.int32, (rows_dev, rows_dev), 1
    )
    before = jnp.dot(member.astype(jnp.bfloat16), earlier.astype(jnp.bfloat16), preferred_element_type=jnp.float32)
    rank = jnp.sum(jnp.where(member, before, 0.0), axis=0, keepdims=True).astype(jnp.int32)
    slot = jnp.where(rank < cap, group * cap + rank, groups * cap)
    pick = (lax.broadcasted_iota(jnp.int32, (groups * cap, rows_dev), 0) == slot).astype(jnp.bfloat16)
    x = emb_ref[...]
    unit = (x * lax.rsqrt(jnp.sum(x * x, axis=1, keepdims=True) + 1e-06)).astype(jnp.bfloat16)
    for k, ref in enumerate(chunk_refs):
        chunk = jnp.dot(pick[k * cap : (k + 1) * cap], unit, preferred_element_type=jnp.float32)
        ref[...] = chunk.astype(jnp.bfloat16)
    high = lax.shift_right_logical(place, 7)
    low = jnp.bitwise_and(place, 127)
    kind = lax.broadcasted_iota(jnp.int32, (16, rows_dev), 0)
    facts = jnp.where(kind == 0, high, jnp.where(kind == 1, low, jnp.where(kind == 2, 1, 0)))
    facts = facts.astype(jnp.float32).astype(jnp.bfloat16)
    got = lax.dot_general(facts, pick, NT, preferred_element_type=jnp.float32).astype(jnp.int32)
    there = got[2:3, :] > 0
    place_ref[...] = jnp.where(there, got[0:1, :] * 128 + got[1:2, :], group_size)


def diagonal(n):
    return lax.broadcasted_iota(jnp.int32, (n, n), 0) == lax.broadcasted_iota(jnp.int32, (n, n), 1)


def as_column(row):
    return jnp.max(jnp.where(diagonal(row.shape[1]), row, -2.0), axis=1, keepdims=True)


class Best:
    def __init__(self, start):
        self.row, self.column = start, None

    def add_row(self, row):
        self.row = jnp.maximum(self.row, row)

    def add_column(self, column):
        self.column = column if self.column is None else jnp.maximum(self.column, column)

    def as_row(self):
        if self.column is None:
            return self.row
        eye = diagonal(self.column.shape[0])
        return jnp.maximum(self.row, jnp.max(jnp.where(eye, self.column, -1.0), axis=0, keepdims=True))


def similar(left, right, left_label, right_label, shift=None):
    sims = lax.dot_general(left, right, NT, preferred_element_type=jnp.float32)
    keep = left_label == right_label
    if shift is not None:
        keep &= lax.broadcasted_iota(jnp.int32, sims.shape, 0) != lax.broadcasted_iota(jnp.int32, sims.shape, 1) + shift
    return jnp.where(keep, sims, -1.0)


def row_max(sims):
    return jnp.max(sims, axis=1, keepdims=True)


def column_max(sims):
    return jnp.max(sims, axis=0, keepdims=True)


def loader(chunks, count, blocks, sems):
    number = len(chunks) // count
    cap = chunks[0].shape[0]

    def copy(j, k):
        return pltpu.make_async_copy(chunks[j * number + k], blocks.at[j, pl.ds(k * cap, cap)], sems.at[j, k])

    for j, k in itertools.product(range(count), range(number)):
        copy(j, k).start()
    here = set()

    def need(*wanted):
        for j in sorted(set(wanted) - here):
            for k in range(number):
                copy(j, k).wait()
            here.add(j)

    return need


def early_kernel(pairs, count, early, *refs):
    *chunks, label_ref, last_label_ref, out_ref, label_col_ref, blocks, sems = refs
    need = loader(chunks, count, blocks, sems)
    for j in sorted({j for j, _ in pairs}):
        label_col_ref[:early, j : j + 1] = as_column(label_ref[j : j + 1, :])
        label_col_ref[early:, j : j + 1] = as_column(last_label_ref[j : j + 1, :])
    best = [Best(jnp.full((1, early), -1.0, jnp.float32)) for _ in range(count)]
    for j, k in pairs:
        need(j, k)
        sims = similar(
            blocks[j, :early],
            blocks[k, :early],
            label_col_ref[:early, j : j + 1],
            label_ref[k : k + 1, :],
            0 if j == k else None,
        )
        best[k].add_row(column_max(sims))
        if j != k:
            best[j].add_column(row_max(sims))
    for j in range(count):
        out_ref[j : j + 1, :] = best[j].as_row()


def late_kernel(pairs, count, group_size, *refs):
    plane_ref, *chunks, best_ref, place_ref, last_place_ref, label_ref, last_label_ref, label_col_ref, out_ref, blocks, sems = refs
    need = loader(chunks, count, blocks, sems)
    first = best_ref.shape[1]
    rest = blocks.shape[1] - first
    early = [Best(best_ref[j : j + 1, :]) for j in range(count)]
    late = [Best(jnp.full((1, rest), -1.0, jnp.float32)) for _ in range(count)]
    for j, k in pairs:
        need(j, k)
        sims = similar(
            blocks[j],
            blocks[k, first:],
            label_col_ref[:, j : j + 1],
            last_label_ref[k : k + 1, :],
            first if j == k else None,
        )
        column = row_max(sims)
        early[j].add_column(column[:first])
        late[k].add_row(column_max(sims))
        if j != k:
            late[j].add_column(column[first:])
            sims = similar(
                blocks[j, first:], blocks[k, :first], label_col_ref[first:, j : j + 1], label_ref[k : k + 1, :]
            )
            early[k].add_row(column_max(sims))
            late[j].add_column(row_max(sims))
    tall = group_size // 128
    pieces = [(early[j], place_ref[j : j + 1, :]) for j in range(count)]
    pieces += [(late[j], last_place_ref[j : j + 1, :]) for j in range(count)]
    spread = jnp.zeros((4 * tall, 128), jnp.float32)
    for best, place in pieces:
        best = best.as_row()
        slots = best.shape[1]
        high = lax.broadcasted_iota(jnp.int32, (tall, slots), 0) == lax.shift_right_logical(place, 7)
        low = lax.broadcasted_iota(jnp.int32, (128, slots), 0) == jnp.bitwise_and(place, 127)
        parts, rest = [], best
        for _ in range(3):
            part = rest.astype(jnp.bfloat16).astype(jnp.float32)
            rest = rest - part
            parts.append(part)
        parts.append(jnp.ones_like(best))
        stack = jnp.concatenate([jnp.where(high, part, 0.0) for part in parts], axis=0).astype(jnp.bfloat16)
        spread += lax.dot_general(stack, low.astype(jnp.bfloat16), NT, preferred_element_type=jnp.float32)
    value = spread[:tall] + spread[tall : 2 * tall] + spread[2 * tall : 3 * tall]
    value = jnp.where(spread[3 * tall :] > 0.5, value, -1.0)
    for r in range(out_ref.shape[0]):
        out_ref[r] = jnp.where(plane_ref[0] == r, value, -1.0)


def best_matches(cap, embeddings, dest_pos, cluster_ids):
    n_row, n_col = lax.axis_size("row"), lax.axis_size("col")
    devs = n_row * n_col
    groups, wide = n_row, n_col // n_row
    rows_dev, width = embeddings.shape
    group_size = rows_dev * n_col
    slots = groups * cap
    held, pairs = plane_plan(n_row, wide)
    count = len(held)

    assert groups & (groups - 1) == 0
    row, col = lax.axis_index("row"), lax.axis_index("col")
    plane, index = col // wide, row * wide + col % wide

    def device(i, h):
        return (i // wide) * n_col + h * wide + i % wide

    planes = [(i, h) for h in range(groups) for i in range(n_row * wide)]
    dest_row = dest_pos.reshape(1, rows_dev)
    plane_ref = plane.astype(jnp.int32).reshape(1)
    place, *parts = pl.pallas_call(
        functools.partial(pack_kernel, groups, cap, group_size),
        out_shape=[
            jax.ShapeDtypeStruct((1, slots), jnp.int32),
            *[jax.ShapeDtypeStruct((cap, width), jnp.bfloat16)] * groups,
        ],
        in_specs=[pl.BlockSpec(memory_space=pltpu.SMEM), VMEM, VMEM],
        out_specs=[VMEM] * (1 + groups),
        compiler_params=kernel_params(20),
    )(plane_ref, dest_row, embeddings)

    def across(part, k):
        return lax.ppermute(part, AXES, [(device(i, h ^ k), device(i, h)) for i, h in planes])

    def inside(part, j):
        return lax.ppermute(part, AXES, [(device(int(held[j, i]), h), device(i, h)) for i, h in planes])

    def after(values, *done):
        return lax.optimization_barrier((values, done))[0]

    own = [parts[0]] + [across(parts[k], k) for k in range(1, min(3, groups))]
    near = inside(own[0], 1)
    rounds = [[near] + [inside(after(own[0], near), j) for j in range(2, count)]]
    rest = after([parts[k] for k in range(3, groups)], near)

    own += [across(part, k) for k, part in zip(range(3, groups), rest)]
    for k in range(1, groups - 1):
        part = after(own[k], *rounds[0]) if k == 1 else after(own[k], rounds[-1][0], *rounds[-2])
        near = after(part, own[k + 1]) if k > 1 else part
        rounds.append([inside(near, 1), *[inside(part, j) for j in range(2, count)]])

    last = after(own[-1], *rounds[-2])
    rounds.append([inside(after(last, rounds[-1][0]), 1), *[inside(last, j) for j in range(2, count)]])
    place = after(place, rounds[1][0])

    planes_i = jnp.arange(groups, dtype=jnp.int32)
    swap = (planes_i[:, None] ^ planes_i[None, :]) == plane

    def by_plane(array):
        return jnp.sum(jnp.where(swap[:, :, None], array[None, :, :], 0), axis=1)

    levels = jnp.arange(LEVELS, dtype=jnp.int32)
    counts = jnp.sum((cluster_ids.reshape(1, rows_dev) <= levels[:, None]).astype(jnp.int32), axis=1)
    target_group = dest_pos // group_size
    most = jnp.max(jnp.sum((target_group[None, :] == jnp.arange(groups)[:, None]).astype(jnp.int32), axis=1))
    tail = jnp.concatenate([counts, (most > cap).astype(jnp.int32).reshape(1)])
    length = -(-(cap + LEVELS + 1) // 128) * 128
    facts = jnp.concatenate(
        [
            by_plane(place.reshape(groups, cap)),
            jnp.broadcast_to(tail[None, :], (groups, LEVELS + 1)),
            jnp.zeros((groups, length - cap - LEVELS - 1), jnp.int32),
        ],
        axis=1,
    )
    facts = jnp.broadcast_to(facts[None, :, None, :], (n_row, groups, wide, length)).reshape(devs, length)
    facts = lax.all_to_all(facts, AXES, split_axis=0, concat_axis=0, tiled=True)
    over = jnp.max(facts[:, cap + LEVELS]) > 0
    facts = facts.reshape(n_row, groups, wide, length)

    in_plane = (jnp.arange(n_row, dtype=jnp.int32) == plane).astype(jnp.int32)
    ends = jnp.sum(facts[..., cap : cap + LEVELS] * in_plane[:, None, None, None], axis=(0, 1, 2))
    places = by_plane(facts[..., :cap].transpose(1, 0, 2, 3).reshape(groups, n_row * wide * cap))
    places = places.reshape(groups, n_row * wide, cap).transpose(1, 0, 2).reshape(n_row * wide, slots)
    mine = jnp.sum(
        jnp.where(jnp.arange(n_row * wide)[None, :] == index, jnp.asarray(held, jnp.int32), 0), axis=1
    )
    mine = (mine[:, None] == jnp.arange(n_row * wide)[None, :]).astype(jnp.int32)
    places = jnp.sum(mine[:, :, None] * places[None, :, :], axis=1)
    labels = jnp.sum((places[:, None, :] >= ends[None, :, None]).astype(jnp.int32), axis=1)
    labels = jnp.where(places < group_size, labels, -1).astype(jnp.float32)

    early = (slots - cap) // 256 * 256
    label, last_label = labels[:, :early], labels[:, early:]
    blocks = [own] + [[moved[j - 1] for moved in rounds] for j in range(1, count)]
    any_space = pl.BlockSpec(memory_space=pltpu.HBM)
    area = 4 * slots * slots

    def scratch(number):
        return [
            pltpu.VMEM((count, number * cap, width), jnp.bfloat16),
            pltpu.SemaphoreType.DMA((count, number)),
        ]

    limit = 8 + (2 * count * slots * width + 5 * area) // 2**20
    first_best, label_cols = pl.pallas_call(
        functools.partial(early_kernel, pairs, count, early),
        out_shape=[
            jax.ShapeDtypeStruct((count, early), jnp.float32),
            jax.ShapeDtypeStruct((slots, count), jnp.float32),
        ],
        in_specs=[any_space] * (count * (groups - 1)) + [VMEM] * 2,
        out_specs=[VMEM] * 2,
        scratch_shapes=scratch(groups - 1),
        compiler_params=kernel_params(limit),
        cost_estimate=pl.CostEstimate(
            flops=2 * len(pairs) * early * early * width, bytes_accessed=2 * count * early * width, transcendentals=0
        ),
    )(*[part for block in blocks for part in block[:-1]], label, last_label)
    best = pl.pallas_call(
        functools.partial(late_kernel, pairs, count, group_size),
        out_shape=jax.ShapeDtypeStruct((n_row, group_size // 128, 128), jnp.float32),
        in_specs=[pl.BlockSpec(memory_space=pltpu.SMEM)] + [any_space] * (count * groups) + [VMEM] * 6,
        out_specs=VMEM,
        scratch_shapes=scratch(groups),
        compiler_params=kernel_params(limit),
    )(
        plane_ref,
        *itertools.chain(*blocks),
        first_best,
        places[:, :early],
        places[:, early:],
        label,
        last_label,
        label_cols,
    )

    best = lax.all_to_all(best.reshape(devs, -1, 128), AXES, split_axis=0, concat_axis=0, tiled=True)
    return jnp.max(best, axis=0).reshape(1, rows_dev), over


def shards(embeddings, dest_pos, cluster_ids):
    n_row, n_col = lax.axis_size("row"), lax.axis_size("col")
    rows_dev = embeddings.shape[0]
    devs = n_row * n_col
    most = min(rows_dev, n_col * max(4, 2 * rows_dev // devs))
    usual = min(most, -(-(rows_dev // n_row) * 11 // 8 // 16) * 16)
    args = (embeddings, dest_pos, cluster_ids)
    best, over = best_matches(usual, *args)
    if usual == most:
        return best
    return lax.cond(over, lambda: best_matches(most, *args)[0], lambda: best)


def solution(mesh):
    return jax.shard_map(
        shards,
        mesh=mesh,
        in_specs=(P(("row", "col"), None), P(("row", "col")), P("row", "col")),
        out_specs=P("row", "col"),
        check_vma=False,
    )
```

```python
import functools
import itertools

import jax
import jax.numpy as jnp
import numpy as np
from jax import lax
from jax.experimental import pallas as pl
from jax.experimental.pallas import tpu as pltpu
from jax.sharding import PartitionSpec as P

AXES = ("row", "col")
LEVELS = 16
NT = (((1,), (1,)), ((), ()))
VMEM = pl.BlockSpec(memory_space=pltpu.VMEM)


def kernel_params(mebibytes):
    return pltpu.CompilerParams(vmem_limit_bytes=mebibytes * 2**20)


def plane_plan(n_row, wide):
    n = n_row * wide
    if n_row == 4 and wide == 2:
        chips = [(0, 0), (0, 1), (1, 1), (1, 0)]

        def dev(chip, core):
            x, y = chips[chip % 4]
            return (x * 2 + core) * wide + y

        held = np.zeros((4, n), np.int64)
        for chip, core in itertools.product(range(4), range(2)):
            i = dev(chip, core)
            crossed = 1 - core if chip in (1, 2) else core
            held[:, i] = i, dev(chip, 1 - core), dev(chip + 1, core), dev(chip + 3, crossed)
        pairs = [(0, 0), (0, 1), (0, 2), (1, 2), (2, 3)]
    else:
        def covered(cover):
            return {(b - a) % n for a in cover for b in cover}

        size = 1
        while True:
            found = [c for c in itertools.combinations(range(n), size) if c[0] == 0 and len(covered(c)) == n]
            if found:
                break
            size += 1
        cover = found[0]
        held = (np.arange(n)[None, :] + np.array(cover)[:, None]) % n
        pairs, seen = [], set()
        for j, k in itertools.combinations_with_replacement(range(size), 2):
            delta = (cover[k] - cover[j]) % n
            if delta not in seen:
                seen |= {delta, (n - delta) % n}
                pairs.append((j, k))
    met = set()
    for j, k in pairs:
        for i in range(n):
            met |= {(held[j, i], held[k, i]), (held[k, i], held[j, i])}
    assert len(met) == n * n
    return held, pairs


def pack_kernel(groups, cap, group_size, plane_ref, dest_ref, emb_ref, place_ref, *chunk_refs):
    rows_dev = emb_ref.shape[0]
    dest = dest_ref[...]
    group, place = jnp.zeros_like(dest), dest
    for g in range(1, groups):
        above = dest >= g * group_size
        group += above.astype(jnp.int32)
        place -= jnp.where(above, group_size, 0)
    group = jnp.bitwise_xor(group, plane_ref[0])
    pad = -(-groups // 16) * 16
    member = lax.broadcasted_iota(jnp.int32, (pad, rows_dev), 0) == group
    earlier = lax.broadcasted_iota(jnp.int32, (rows_dev, rows_dev), 0) < lax.broadcasted_iota(
        jnp.int32, (rows_dev, rows_dev), 1
    )
    before = jnp.dot(member.astype(jnp.bfloat16), earlier.astype(jnp.bfloat16), preferred_element_type=jnp.float32)
    rank = jnp.sum(jnp.where(member, before, 0.0), axis=0, keepdims=True).astype(jnp.int32)
    slot = jnp.where(rank < cap, group * cap + rank, groups * cap)
    pick = (lax.broadcasted_iota(jnp.int32, (groups * cap, rows_dev), 0) == slot).astype(jnp.bfloat16)
    x = emb_ref[...]
    unit = (x * lax.rsqrt(jnp.sum(x * x, axis=1, keepdims=True) + 1e-06)).astype(jnp.bfloat16)
    for k, ref in enumerate(chunk_refs):
        chunk = jnp.dot(pick[k * cap : (k + 1) * cap], unit, preferred_element_type=jnp.float32)
        ref[...] = chunk.astype(jnp.bfloat16)
    high = lax.shift_right_logical(place, 7)
    low = jnp.bitwise_and(place, 127)
    kind = lax.broadcasted_iota(jnp.int32, (16, rows_dev), 0)
    facts = jnp.where(kind == 0, high, jnp.where(kind == 1, low, jnp.where(kind == 2, 1, 0)))
    facts = facts.astype(jnp.float32).astype(jnp.bfloat16)
    got = lax.dot_general(facts, pick, NT, preferred_element_type=jnp.float32).astype(jnp.int32)
    there = got[2:3, :] > 0
    place_ref[...] = jnp.where(there, got[0:1, :] * 128 + got[1:2, :], group_size)


def diagonal(n):
    return lax.broadcasted_iota(jnp.int32, (n, n), 0) == lax.broadcasted_iota(jnp.int32, (n, n), 1)


def as_column(row):
    return jnp.max(jnp.where(diagonal(row.shape[1]), row, -2.0), axis=1, keepdims=True)


class Best:
    def __init__(self, start):
        self.row, self.column = start, None

    def add_row(self, row):
        self.row = jnp.maximum(self.row, row)

    def add_column(self, column):
        self.column = column if self.column is None else jnp.maximum(self.column, column)

    def as_row(self):
        if self.column is None:
            return self.row
        eye = diagonal(self.column.shape[0])
        return jnp.maximum(self.row, jnp.max(jnp.where(eye, self.column, -1.0), axis=0, keepdims=True))


def similar(left, right, left_label, right_label, shift=None):
    sims = lax.dot_general(left, right, NT, preferred_element_type=jnp.float32)
    keep = left_label == right_label
    if shift is not None:
        keep &= lax.broadcasted_iota(jnp.int32, sims.shape, 0) != lax.broadcasted_iota(jnp.int32, sims.shape, 1) + shift
    return jnp.where(keep, sims, -1.0)


def row_max(sims):
    return jnp.max(sims, axis=1, keepdims=True)


def column_max(sims):
    return jnp.max(sims, axis=0, keepdims=True)


def loader(chunks, count, blocks, sems):
    number = len(chunks) // count
    cap = chunks[0].shape[0]

    def copy(j, k):
        return pltpu.make_async_copy(chunks[j * number + k], blocks.at[j, pl.ds(k * cap, cap)], sems.at[j, k])

    for j, k in itertools.product(range(count), range(number)):
        copy(j, k).start()
    here = set()

    def need(*wanted):
        for j in sorted(set(wanted) - here):
            for k in range(number):
                copy(j, k).wait()
            here.add(j)

    return need


def early_kernel(pairs, count, early, *refs):
    *chunks, label_ref, last_label_ref, out_ref, label_col_ref, blocks, sems = refs
    need = loader(chunks, count, blocks, sems)
    for j in sorted({j for j, _ in pairs}):
        label_col_ref[:early, j : j + 1] = as_column(label_ref[j : j + 1, :])
        label_col_ref[early:, j : j + 1] = as_column(last_label_ref[j : j + 1, :])
    best = [Best(jnp.full((1, early), -1.0, jnp.float32)) for _ in range(count)]
    for j, k in pairs:
        need(j, k)
        sims = similar(
            blocks[j, :early],
            blocks[k, :early],
            label_col_ref[:early, j : j + 1],
            label_ref[k : k + 1, :],
            0 if j == k else None,
        )
        best[k].add_row(column_max(sims))
        if j != k:
            best[j].add_column(row_max(sims))
    for j in range(count):
        out_ref[j : j + 1, :] = best[j].as_row()


def meet_last(pairs, blocks, early, late, need, label_ref, last_label_ref, label_col_ref):
    first = label_ref.shape[1]
    for j, k in pairs:
        need(j, k)
        sims = similar(
            blocks[j],
            blocks[k, first:],
            label_col_ref[:, j : j + 1],
            last_label_ref[k : k + 1, :],
            first if j == k else None,
        )
        column = row_max(sims)
        early[j].add_column(column[:first])
        late[k].add_row(column_max(sims))
        if j != k:
            late[j].add_column(column[first:])
            sims = similar(
                blocks[j, first:], blocks[k, :first], label_col_ref[first:, j : j + 1], label_ref[k : k + 1, :]
            )
            early[k].add_row(column_max(sims))
            late[j].add_column(row_max(sims))


def near_kernel(pairs, count, *refs):
    *chunks, best_ref, label_ref, last_label_ref, label_col_ref, early_ref, late_ref, blocks, sems = refs
    need = loader(chunks, count, blocks, sems)
    rest = last_label_ref.shape[1]
    early = [Best(best_ref[j : j + 1, :]) for j in range(best_ref.shape[0])]
    late = [Best(jnp.full((1, rest), -1.0, jnp.float32)) for _ in early]
    meet_last(pairs, blocks, early, late, need, label_ref, last_label_ref, label_col_ref)
    for j, (one, other) in enumerate(zip(early, late)):
        early_ref[j : j + 1, :] = one.as_row()
        late_ref[j : j + 1, :] = other.as_row()


def late_kernel(pairs, count, group_size, *refs):
    plane_ref, *chunks, best_ref, last_best_ref, place_ref, last_place_ref = refs[:-6]
    label_ref, last_label_ref, label_col_ref, out_ref, blocks, sems = refs[-6:]
    need = loader(chunks, count, blocks, sems)
    early = [Best(best_ref[j : j + 1, :]) for j in range(count)]
    late = [Best(last_best_ref[j : j + 1, :]) for j in range(count)]
    meet_last(pairs, blocks, early, late, need, label_ref, last_label_ref, label_col_ref)
    tall = group_size // 128
    pieces = [(early[j], place_ref[j : j + 1, :]) for j in range(count)]
    pieces += [(late[j], last_place_ref[j : j + 1, :]) for j in range(count)]
    spread = jnp.zeros((4 * tall, 128), jnp.float32)
    for best, place in pieces:
        best = best.as_row()
        slots = best.shape[1]
        high = lax.broadcasted_iota(jnp.int32, (tall, slots), 0) == lax.shift_right_logical(place, 7)
        low = lax.broadcasted_iota(jnp.int32, (128, slots), 0) == jnp.bitwise_and(place, 127)
        parts, rest = [], best
        for _ in range(3):
            part = rest.astype(jnp.bfloat16).astype(jnp.float32)
            rest = rest - part
            parts.append(part)
        parts.append(jnp.ones_like(best))
        stack = jnp.concatenate([jnp.where(high, part, 0.0) for part in parts], axis=0).astype(jnp.bfloat16)
        spread += lax.dot_general(stack, low.astype(jnp.bfloat16), NT, preferred_element_type=jnp.float32)
    value = spread[:tall] + spread[tall : 2 * tall] + spread[2 * tall : 3 * tall]
    value = jnp.where(spread[3 * tall :] > 0.5, value, -1.0)
    for r in range(out_ref.shape[0]):
        out_ref[r] = jnp.where(plane_ref[0] == r, value, -1.0)


def best_matches(cap, embeddings, dest_pos, cluster_ids):
    n_row, n_col = lax.axis_size("row"), lax.axis_size("col")
    devs = n_row * n_col
    groups, wide = n_row, n_col // n_row
    rows_dev, width = embeddings.shape
    group_size = rows_dev * n_col
    slots = groups * cap
    held, pairs = plane_plan(n_row, wide)
    count = len(held)

    assert groups & (groups - 1) == 0
    row, col = lax.axis_index("row"), lax.axis_index("col")
    plane, index = col // wide, row * wide + col % wide

    def device(i, h):
        return (i // wide) * n_col + h * wide + i % wide

    planes = [(i, h) for h in range(groups) for i in range(n_row * wide)]
    dest_row = dest_pos.reshape(1, rows_dev)
    plane_ref = plane.astype(jnp.int32).reshape(1)
    place, *parts = pl.pallas_call(
        functools.partial(pack_kernel, groups, cap, group_size),
        out_shape=[
            jax.ShapeDtypeStruct((1, slots), jnp.int32),
            *[jax.ShapeDtypeStruct((cap, width), jnp.bfloat16)] * groups,
        ],
        in_specs=[pl.BlockSpec(memory_space=pltpu.SMEM), VMEM, VMEM],
        out_specs=[VMEM] * (1 + groups),
        compiler_params=kernel_params(20),
    )(plane_ref, dest_row, embeddings)

    def across(part, k):
        return lax.ppermute(part, AXES, [(device(i, h ^ k), device(i, h)) for i, h in planes])

    def inside(part, j):
        return lax.ppermute(part, AXES, [(device(int(held[j, i]), h), device(i, h)) for i, h in planes])

    def after(values, *done):
        return lax.optimization_barrier((values, done))[0]

    own = [parts[0]] + [across(parts[k], k) for k in range(1, min(3, groups))]
    near = inside(own[0], 1)
    rounds = [[near] + [inside(after(own[0], near), j) for j in range(2, count)]]
    rest = after([parts[k] for k in range(3, groups)], near)

    own += [across(part, k) for k, part in zip(range(3, groups), rest)]
    for k in range(1, groups - 1):
        part = after(own[k], *rounds[0]) if k == 1 else after(own[k], rounds[-1][0], *rounds[-2])
        near = after(part, own[k + 1]) if k > 1 else part
        rounds.append([inside(near, 1), *[inside(part, j) for j in range(2, count)]])

    last = after(own[-1], *rounds[-2])
    rounds.append([inside(after(last, rounds[-1][0]), 1), *[inside(last, j) for j in range(2, count)]])
    place = after(place, rounds[1][0])

    planes_i = jnp.arange(groups, dtype=jnp.int32)
    swap = (planes_i[:, None] ^ planes_i[None, :]) == plane

    def by_plane(array):
        return jnp.sum(jnp.where(swap[:, :, None], array[None, :, :], 0), axis=1)

    levels = jnp.arange(LEVELS, dtype=jnp.int32)
    counts = jnp.sum((cluster_ids.reshape(1, rows_dev) <= levels[:, None]).astype(jnp.int32), axis=1)
    target_group = dest_pos // group_size
    most = jnp.max(jnp.sum((target_group[None, :] == jnp.arange(groups)[:, None]).astype(jnp.int32), axis=1))
    tail = jnp.concatenate([counts, (most > cap).astype(jnp.int32).reshape(1)])
    length = -(-(cap + LEVELS + 1) // 128) * 128
    facts = jnp.concatenate(
        [
            by_plane(place.reshape(groups, cap)),
            jnp.broadcast_to(tail[None, :], (groups, LEVELS + 1)),
            jnp.zeros((groups, length - cap - LEVELS - 1), jnp.int32),
        ],
        axis=1,
    )
    facts = jnp.broadcast_to(facts[None, :, None, :], (n_row, groups, wide, length)).reshape(devs, length)
    facts = lax.all_to_all(facts, AXES, split_axis=0, concat_axis=0, tiled=True)
    over = jnp.max(facts[:, cap + LEVELS]) > 0
    facts = facts.reshape(n_row, groups, wide, length)

    in_plane = (jnp.arange(n_row, dtype=jnp.int32) == plane).astype(jnp.int32)
    ends = jnp.sum(facts[..., cap : cap + LEVELS] * in_plane[:, None, None, None], axis=(0, 1, 2))
    places = by_plane(facts[..., :cap].transpose(1, 0, 2, 3).reshape(groups, n_row * wide * cap))
    places = places.reshape(groups, n_row * wide, cap).transpose(1, 0, 2).reshape(n_row * wide, slots)
    mine = jnp.sum(
        jnp.where(jnp.arange(n_row * wide)[None, :] == index, jnp.asarray(held, jnp.int32), 0), axis=1
    )
    mine = (mine[:, None] == jnp.arange(n_row * wide)[None, :]).astype(jnp.int32)
    places = jnp.sum(mine[:, :, None] * places[None, :, :], axis=1)
    labels = jnp.sum((places[:, None, :] >= ends[None, :, None]).astype(jnp.int32), axis=1)
    labels = jnp.where(places < group_size, labels, -1).astype(jnp.float32)

    early = (slots - cap) // 256 * 256
    label, last_label = labels[:, :early], labels[:, early:]
    blocks = [own] + [[moved[j - 1] for moved in rounds] for j in range(1, count)]
    any_space = pl.BlockSpec(memory_space=pltpu.HBM)
    area = 4 * slots * slots

    def scratch(number):
        return [
            pltpu.VMEM((count, number * cap, width), jnp.bfloat16),
            pltpu.SemaphoreType.DMA((count, number)),
        ]

    limit = 8 + (2 * count * slots * width + 5 * area) // 2**20
    first_best, label_cols = pl.pallas_call(
        functools.partial(early_kernel, pairs, count, early),
        out_shape=[
            jax.ShapeDtypeStruct((count, early), jnp.float32),
            jax.ShapeDtypeStruct((slots, count), jnp.float32),
        ],
        in_specs=[any_space] * (count * (groups - 1)) + [VMEM] * 2,
        out_specs=[VMEM] * 2,
        scratch_shapes=scratch(groups - 1),
        compiler_params=kernel_params(limit),
        cost_estimate=pl.CostEstimate(
            flops=2 * len(pairs) * early * early * width, bytes_accessed=2 * count * early * width, transcendentals=0
        ),
    )(*[part for block in blocks for part in block[:-1]], label, last_label)
    near = [pair for pair in pairs if max(pair) < 2]
    first_best, last_best = pl.pallas_call(
        functools.partial(near_kernel, near, 2),
        out_shape=[
            jax.ShapeDtypeStruct((count, early), jnp.float32),
            jax.ShapeDtypeStruct((count, slots - early), jnp.float32),
        ],
        in_specs=[any_space] * (2 * groups) + [VMEM] * 4,
        out_specs=[VMEM] * 2,
        scratch_shapes=[
            pltpu.VMEM((2, slots, width), jnp.bfloat16),
            pltpu.SemaphoreType.DMA((2, groups)),
        ],
        compiler_params=kernel_params(limit),
        cost_estimate=pl.CostEstimate(
            flops=2 * len(near) * (slots * slots - early * early) * width,
            bytes_accessed=4 * slots * width,
            transcendentals=0,
        ),
    )(*blocks[0], *blocks[1], first_best, label, last_label, label_cols)
    best = pl.pallas_call(
        functools.partial(late_kernel, [pair for pair in pairs if pair not in near], count, group_size),
        out_shape=jax.ShapeDtypeStruct((n_row, group_size // 128, 128), jnp.float32),
        in_specs=[pl.BlockSpec(memory_space=pltpu.SMEM)] + [any_space] * (count * groups) + [VMEM] * 7,
        out_specs=VMEM,
        scratch_shapes=scratch(groups),
        compiler_params=kernel_params(limit),
    )(
        plane_ref,
        *itertools.chain(*blocks),
        first_best,
        last_best,
        places[:, :early],
        places[:, early:],
        label,
        last_label,
        label_cols,
    )

    best = lax.all_to_all(best.reshape(devs, -1, 128), AXES, split_axis=0, concat_axis=0, tiled=True)
    return jnp.max(best, axis=0).reshape(1, rows_dev), over


def shards(embeddings, dest_pos, cluster_ids):
    n_row, n_col = lax.axis_size("row"), lax.axis_size("col")
    rows_dev = embeddings.shape[0]
    devs = n_row * n_col
    most = min(rows_dev, n_col * max(4, 2 * rows_dev // devs))
    usual = min(most, -(-(rows_dev // n_row) * 11 // 8 // 16) * 16)
    args = (embeddings, dest_pos, cluster_ids)
    best, over = best_matches(usual, *args)
    if usual == most:
        return best
    return lax.cond(over, lambda: best_matches(most, *args)[0], lambda: best)


def solution(mesh):
    return jax.shard_map(
        shards,
        mesh=mesh,
        in_specs=(P(("row", "col"), None), P(("row", "col")), P("row", "col")),
        out_specs=P("row", "col"),
        check_vma=False,
    )
```

```python
import functools
import itertools

import jax
import jax.numpy as jnp
import numpy as np
from jax import lax
from jax.experimental import pallas as pl
from jax.experimental.pallas import tpu as pltpu
from jax.sharding import PartitionSpec as P

AXES = ("row", "col")
PIECES = 4
LEVELS = 16
NT = (((1,), (1,)), ((), ()))
VMEM = pl.BlockSpec(memory_space=pltpu.VMEM)


def kernel_params(mebibytes):
    return pltpu.CompilerParams(vmem_limit_bytes=mebibytes * 2**20)


def plane_plan(n_row, wide):
    n = n_row * wide
    if n_row == 4 and wide == 2:
        chips = [(0, 0), (0, 1), (1, 1), (1, 0)]

        def dev(chip, core):
            x, y = chips[chip % 4]
            return (x * 2 + core) * wide + y

        held = np.zeros((4, n), np.int64)
        for chip, core in itertools.product(range(4), range(2)):
            i = dev(chip, core)
            crossed = 1 - core if chip in (1, 2) else core
            held[:, i] = i, dev(chip, 1 - core), dev(chip + 1, core), dev(chip + 3, crossed)
        pairs = [(0, 0), (0, 1), (0, 2), (1, 2), (2, 3)]
    else:
        def covered(cover):
            return {(b - a) % n for a in cover for b in cover}

        size = 1
        while True:
            found = [c for c in itertools.combinations(range(n), size) if c[0] == 0 and len(covered(c)) == n]
            if found:
                break
            size += 1
        cover = found[0]
        held = (np.arange(n)[None, :] + np.array(cover)[:, None]) % n
        pairs, seen = [], set()
        for j, k in itertools.combinations_with_replacement(range(size), 2):
            delta = (cover[k] - cover[j]) % n
            if delta not in seen:
                seen |= {delta, (n - delta) % n}
                pairs.append((j, k))
    met = set()
    for j, k in pairs:
        for i in range(n):
            met |= {(held[j, i], held[k, i]), (held[k, i], held[j, i])}
    assert len(met) == n * n
    return held, pairs


def pack_kernel(groups, cap, group_size, plane_ref, dest_ref, emb_ref, place_ref, *refs):
    *chunk_refs, emb, unit, sems = refs
    rows_dev = emb_ref.shape[0]
    pieces = [pl.ds(start, rows_dev // PIECES) for start in range(0, rows_dev, rows_dev // PIECES)]
    loads = [pltpu.make_async_copy(emb_ref.at[piece], emb.at[piece], sems.at[i]) for i, piece in enumerate(pieces)]
    for load in loads:
        load.start()
    dest = dest_ref[...]
    group, place = jnp.zeros_like(dest), dest
    for g in range(1, groups):
        above = dest >= g * group_size
        group += above.astype(jnp.int32)
        place -= jnp.where(above, group_size, 0)
    group = jnp.bitwise_xor(group, plane_ref[0])
    pad = -(-groups // 16) * 16
    member = lax.broadcasted_iota(jnp.int32, (pad, rows_dev), 0) == group
    earlier = lax.broadcasted_iota(jnp.int32, (rows_dev, rows_dev), 0) < lax.broadcasted_iota(
        jnp.int32, (rows_dev, rows_dev), 1
    )
    before = jnp.dot(member.astype(jnp.bfloat16), earlier.astype(jnp.bfloat16), preferred_element_type=jnp.float32)
    rank = jnp.sum(jnp.where(member, before, 0.0), axis=0, keepdims=True).astype(jnp.int32)
    slot = jnp.where(rank < cap, group * cap + rank, groups * cap)
    pick = (lax.broadcasted_iota(jnp.int32, (groups * cap, rows_dev), 0) == slot).astype(jnp.bfloat16)
    for load, piece in zip(loads, pieces):
        load.wait()
        x = emb[piece]
        scale = lax.rsqrt(jnp.sum(x * x, axis=1, keepdims=True) + 1e-06)
        unit[piece] = (x * scale).astype(jnp.bfloat16)
    for k, ref in enumerate(chunk_refs):
        chunk = jnp.dot(pick[k * cap : (k + 1) * cap], unit[...], preferred_element_type=jnp.float32)
        ref[...] = chunk.astype(jnp.bfloat16)
    high = lax.shift_right_logical(place, 7)
    low = jnp.bitwise_and(place, 127)
    kind = lax.broadcasted_iota(jnp.int32, (16, rows_dev), 0)
    facts = jnp.where(kind == 0, high, jnp.where(kind == 1, low, jnp.where(kind == 2, 1, 0)))
    facts = facts.astype(jnp.float32).astype(jnp.bfloat16)
    got = lax.dot_general(facts, pick, NT, preferred_element_type=jnp.float32).astype(jnp.int32)
    there = got[2:3, :] > 0
    place_ref[...] = jnp.where(there, got[0:1, :] * 128 + got[1:2, :], group_size)


def diagonal(n):
    return lax.broadcasted_iota(jnp.int32, (n, n), 0) == lax.broadcasted_iota(jnp.int32, (n, n), 1)


def as_column(row):
    return jnp.max(jnp.where(diagonal(row.shape[1]), row, -2.0), axis=1, keepdims=True)


class Best:
    def __init__(self, start):
        self.row, self.column = start, None

    def add_row(self, row):
        self.row = jnp.maximum(self.row, row)

    def add_column(self, column):
        self.column = column if self.column is None else jnp.maximum(self.column, column)

    def as_row(self):
        if self.column is None:
            return self.row
        eye = diagonal(self.column.shape[0])
        return jnp.maximum(self.row, jnp.max(jnp.where(eye, self.column, -1.0), axis=0, keepdims=True))


def similar(left, right, left_label, right_label, shift=None):
    sims = lax.dot_general(left, right, NT, preferred_element_type=jnp.float32)
    keep = left_label == right_label
    if shift is not None:
        keep &= lax.broadcasted_iota(jnp.int32, sims.shape, 0) != lax.broadcasted_iota(jnp.int32, sims.shape, 1) + shift
    return jnp.where(keep, sims, -1.0)


def row_max(sims):
    return jnp.max(sims, axis=1, keepdims=True)


def column_max(sims):
    return jnp.max(sims, axis=0, keepdims=True)


def loader(chunks, count, blocks, sems):
    number = len(chunks) // count
    cap = chunks[0].shape[0]

    def copy(j, k):
        return pltpu.make_async_copy(chunks[j * number + k], blocks.at[j, pl.ds(k * cap, cap)], sems.at[j, k])

    for j, k in itertools.product(range(count), range(number)):
        copy(j, k).start()
    here = set()

    def need(*wanted):
        for j in sorted(set(wanted) - here):
            for k in range(number):
                copy(j, k).wait()
            here.add(j)

    return need


def early_kernel(pairs, count, early, *refs):
    *chunks, label_ref, last_label_ref, out_ref, label_col_ref, blocks, sems = refs
    need = loader(chunks, count, blocks, sems)
    for j in sorted({j for j, _ in pairs}):
        label_col_ref[:early, j : j + 1] = as_column(label_ref[j : j + 1, :])
        label_col_ref[early:, j : j + 1] = as_column(last_label_ref[j : j + 1, :])
    best = [Best(jnp.full((1, early), -1.0, jnp.float32)) for _ in range(count)]
    for j, k in pairs:
        need(j, k)
        sims = similar(
            blocks[j, :early],
            blocks[k, :early],
            label_col_ref[:early, j : j + 1],
            label_ref[k : k + 1, :],
            0 if j == k else None,
        )
        best[k].add_row(column_max(sims))
        if j != k:
            best[j].add_column(row_max(sims))
    for j in range(count):
        out_ref[j : j + 1, :] = best[j].as_row()


def by_place(best, place, tall):
    slots = best.shape[1]
    high = lax.broadcasted_iota(jnp.int32, (tall, slots), 0) == lax.shift_right_logical(place, 7)
    low = lax.broadcasted_iota(jnp.int32, (128, slots), 0) == jnp.bitwise_and(place, 127)
    parts, rest = [], best
    for _ in range(3):
        part = rest.astype(jnp.bfloat16).astype(jnp.float32)
        rest = rest - part
        parts.append(part)
    parts.append(jnp.ones_like(best))
    stack = jnp.concatenate([jnp.where(high, part, 0.0) for part in parts], axis=0).astype(jnp.bfloat16)
    return lax.dot_general(stack, low.astype(jnp.bfloat16), NT, preferred_element_type=jnp.float32)


def late_kernel(pairs, count, group_size, *refs):
    plane_ref, *chunks, best_ref, place_ref, last_place_ref, label_ref, last_label_ref, label_col_ref, out_ref, blocks, sems = refs
    need = loader(chunks, count, blocks, sems)
    first = best_ref.shape[1]
    rest = blocks.shape[1] - first
    tall = group_size // 128
    early = [Best(best_ref[j : j + 1, :]) for j in range(count)]
    late = [Best(jnp.full((1, rest), -1.0, jnp.float32)) for _ in range(count)]
    spread = jnp.zeros((4 * tall, 128), jnp.float32)
    for number, (j, k) in enumerate(pairs):
        need(j, k)
        sims = similar(
            blocks[j],
            blocks[k, first:],
            label_col_ref[:, j : j + 1],
            last_label_ref[k : k + 1, :],
            first if j == k else None,
        )
        column = row_max(sims)
        early[j].add_column(column[:first])
        late[k].add_row(column_max(sims))
        if j != k:
            late[j].add_column(column[first:])
            sims = similar(
                blocks[j, first:], blocks[k, :first], label_col_ref[first:, j : j + 1], label_ref[k : k + 1, :]
            )
            early[k].add_row(column_max(sims))
            late[j].add_column(row_max(sims))
        ahead = {block for pair in pairs[number + 1 :] for block in pair}
        for block in sorted({j, k} - ahead):
            spread += by_place(early[block].as_row(), place_ref[block : block + 1, :], tall)
            spread += by_place(late[block].as_row(), last_place_ref[block : block + 1, :], tall)
    value = spread[:tall] + spread[tall : 2 * tall] + spread[2 * tall : 3 * tall]
    value = jnp.where(spread[3 * tall :] > 0.5, value, -1.0)
    for r in range(out_ref.shape[0]):
        out_ref[r] = jnp.where(plane_ref[0] == r, value, -1.0)


def best_matches(cap, embeddings, dest_pos, cluster_ids):
    n_row, n_col = lax.axis_size("row"), lax.axis_size("col")
    devs = n_row * n_col
    groups, wide = n_row, n_col // n_row
    rows_dev, width = embeddings.shape
    group_size = rows_dev * n_col
    slots = groups * cap
    held, pairs = plane_plan(n_row, wide)
    count = len(held)

    assert groups & (groups - 1) == 0
    row, col = lax.axis_index("row"), lax.axis_index("col")
    plane, index = col // wide, row * wide + col % wide

    def device(i, h):
        return (i // wide) * n_col + h * wide + i % wide

    planes = [(i, h) for h in range(groups) for i in range(n_row * wide)]
    dest_row = dest_pos.reshape(1, rows_dev)
    plane_ref = plane.astype(jnp.int32).reshape(1)
    place, *parts = pl.pallas_call(
        functools.partial(pack_kernel, groups, cap, group_size),
        out_shape=[
            jax.ShapeDtypeStruct((1, slots), jnp.int32),
            *[jax.ShapeDtypeStruct((cap, width), jnp.bfloat16)] * groups,
        ],
        in_specs=[pl.BlockSpec(memory_space=pltpu.SMEM), VMEM, pl.BlockSpec(memory_space=pltpu.HBM)],
        out_specs=[VMEM] * (1 + groups),
        scratch_shapes=[
            pltpu.VMEM((rows_dev, width), jnp.float32),
            pltpu.VMEM((rows_dev, width), jnp.bfloat16),
            pltpu.SemaphoreType.DMA((PIECES,)),
        ],
        compiler_params=kernel_params(20),
    )(plane_ref, dest_row, embeddings)

    def across(part, k):
        return lax.ppermute(part, AXES, [(device(i, h ^ k), device(i, h)) for i, h in planes])

    def inside(part, j):
        return lax.ppermute(part, AXES, [(device(int(held[j, i]), h), device(i, h)) for i, h in planes])

    def after(values, *done):
        return lax.optimization_barrier((values, done))[0]

    own = [parts[0]] + [across(parts[k], k) for k in range(1, min(3, groups))]
    near = inside(own[0], 1)
    rounds = [[near] + [inside(after(own[0], near), j) for j in range(2, count)]]
    rest = after([parts[k] for k in range(3, groups)], near)

    own += [across(part, k) for k, part in zip(range(3, groups), rest)]
    for k in range(1, groups - 1):
        part = after(own[k], *rounds[0]) if k == 1 else after(own[k], rounds[-1][0], *rounds[-2])
        near = after(part, own[k + 1]) if k > 1 else part
        rounds.append([inside(near, 1), *[inside(part, j) for j in range(2, count)]])

    last = after(own[-1], *rounds[-2])
    rounds.append([inside(after(last, rounds[-1][0]), 1), *[inside(last, j) for j in range(2, count)]])
    place = after(place, rounds[1][0])

    planes_i = jnp.arange(groups, dtype=jnp.int32)
    swap = (planes_i[:, None] ^ planes_i[None, :]) == plane

    def by_plane(array):
        return jnp.sum(jnp.where(swap[:, :, None], array[None, :, :], 0), axis=1)

    levels = jnp.arange(LEVELS, dtype=jnp.int32)
    counts = jnp.sum((cluster_ids.reshape(1, rows_dev) <= levels[:, None]).astype(jnp.int32), axis=1)
    target_group = dest_pos // group_size
    most = jnp.max(jnp.sum((target_group[None, :] == jnp.arange(groups)[:, None]).astype(jnp.int32), axis=1))
    tail = jnp.concatenate([counts, (most > cap).astype(jnp.int32).reshape(1)])
    length = -(-(cap + LEVELS + 1) // 128) * 128
    facts = jnp.concatenate(
        [
            by_plane(place.reshape(groups, cap)),
            jnp.broadcast_to(tail[None, :], (groups, LEVELS + 1)),
            jnp.zeros((groups, length - cap - LEVELS - 1), jnp.int32),
        ],
        axis=1,
    )
    facts = jnp.broadcast_to(facts[None, :, None, :], (n_row, groups, wide, length)).reshape(devs, length)
    facts = lax.all_to_all(facts, AXES, split_axis=0, concat_axis=0, tiled=True)
    over = jnp.max(facts[:, cap + LEVELS]) > 0
    facts = facts.reshape(n_row, groups, wide, length)

    in_plane = (jnp.arange(n_row, dtype=jnp.int32) == plane).astype(jnp.int32)
    ends = jnp.sum(facts[..., cap : cap + LEVELS] * in_plane[:, None, None, None], axis=(0, 1, 2))
    places = by_plane(facts[..., :cap].transpose(1, 0, 2, 3).reshape(groups, n_row * wide * cap))
    places = places.reshape(groups, n_row * wide, cap).transpose(1, 0, 2).reshape(n_row * wide, slots)
    mine = jnp.sum(
        jnp.where(jnp.arange(n_row * wide)[None, :] == index, jnp.asarray(held, jnp.int32), 0), axis=1
    )
    mine = (mine[:, None] == jnp.arange(n_row * wide)[None, :]).astype(jnp.int32)
    places = jnp.sum(mine[:, :, None] * places[None, :, :], axis=1)
    labels = jnp.sum((places[:, None, :] >= ends[None, :, None]).astype(jnp.int32), axis=1)
    labels = jnp.where(places < group_size, labels, -1).astype(jnp.float32)

    early = (slots - cap) // 256 * 256
    label, last_label = labels[:, :early], labels[:, early:]
    blocks = [own] + [[moved[j - 1] for moved in rounds] for j in range(1, count)]
    any_space = pl.BlockSpec(memory_space=pltpu.HBM)
    area = 4 * slots * slots

    def scratch(number):
        return [
            pltpu.VMEM((count, number * cap, width), jnp.bfloat16),
            pltpu.SemaphoreType.DMA((count, number)),
        ]

    limit = 8 + (2 * count * slots * width + 5 * area) // 2**20
    first_best, label_cols = pl.pallas_call(
        functools.partial(early_kernel, pairs, count, early),
        out_shape=[
            jax.ShapeDtypeStruct((count, early), jnp.float32),
            jax.ShapeDtypeStruct((slots, count), jnp.float32),
        ],
        in_specs=[any_space] * (count * (groups - 1)) + [VMEM] * 2,
        out_specs=[VMEM] * 2,
        scratch_shapes=scratch(groups - 1),
        compiler_params=kernel_params(limit),
        cost_estimate=pl.CostEstimate(
            flops=2 * len(pairs) * early * early * width, bytes_accessed=2 * count * early * width, transcendentals=0
        ),
    )(*[part for block in blocks for part in block[:-1]], label, last_label)
    best = pl.pallas_call(
        functools.partial(late_kernel, pairs, count, group_size),
        out_shape=jax.ShapeDtypeStruct((n_row, group_size // 128, 128), jnp.float32),
        in_specs=[pl.BlockSpec(memory_space=pltpu.SMEM)] + [any_space] * (count * groups) + [VMEM] * 6,
        out_specs=VMEM,
        scratch_shapes=scratch(groups),
        compiler_params=kernel_params(limit),
    )(
        plane_ref,
        *itertools.chain(*blocks),
        first_best,
        places[:, :early],
        places[:, early:],
        label,
        last_label,
        label_cols,
    )

    best = lax.all_to_all(best.reshape(devs, -1, 128), AXES, split_axis=0, concat_axis=0, tiled=True)
    return jnp.max(best, axis=0).reshape(1, rows_dev), over


def shards(embeddings, dest_pos, cluster_ids):
    n_row, n_col = lax.axis_size("row"), lax.axis_size("col")
    rows_dev = embeddings.shape[0]
    devs = n_row * n_col
    most = min(rows_dev, n_col * max(4, 2 * rows_dev // devs))
    usual = min(most, -(-(rows_dev // n_row) * 11 // 8 // 16) * 16)
    args = (embeddings, dest_pos, cluster_ids)
    best, over = best_matches(usual, *args)
    if usual == most:
        return best
    return lax.cond(over, lambda: best_matches(most, *args)[0], lambda: best)


def solution(mesh):
    return jax.shard_map(
        shards,
        mesh=mesh,
        in_specs=(P(("row", "col"), None), P(("row", "col")), P("row", "col")),
        out_specs=P("row", "col"),
        check_vma=False,
    )
```

```python
import functools
import itertools

import jax
import jax.numpy as jnp
import numpy as np
from jax import lax
from jax.experimental import pallas as pl
from jax.experimental.pallas import tpu as pltpu
from jax.sharding import PartitionSpec as P

AXES = ("row", "col")
LEVELS = 16
NT = (((1,), (1,)), ((), ()))
VMEM = pl.BlockSpec(memory_space=pltpu.VMEM)


def kernel_params(mebibytes):
    return pltpu.CompilerParams(vmem_limit_bytes=mebibytes * 2**20)


def plane_plan(n_row, wide):
    n = n_row * wide
    if n_row == 4 and wide == 2:
        chips = [(0, 0), (0, 1), (1, 1), (1, 0)]

        def dev(chip, core):
            x, y = chips[chip % 4]
            return (x * 2 + core) * wide + y

        held = np.zeros((4, n), np.int64)
        for chip, core in itertools.product(range(4), range(2)):
            i = dev(chip, core)
            crossed = 1 - core if chip in (1, 2) else core
            held[:, i] = i, dev(chip, 1 - core), dev(chip + 1, core), dev(chip + 3, crossed)
        pairs = [(0, 0), (0, 1), (0, 2), (1, 2), (2, 3)]
    else:
        def covered(cover):
            return {(b - a) % n for a in cover for b in cover}

        size = 1
        while True:
            found = [c for c in itertools.combinations(range(n), size) if c[0] == 0 and len(covered(c)) == n]
            if found:
                break
            size += 1
        cover = found[0]
        held = (np.arange(n)[None, :] + np.array(cover)[:, None]) % n
        pairs, seen = [], set()
        for j, k in itertools.combinations_with_replacement(range(size), 2):
            delta = (cover[k] - cover[j]) % n
            if delta not in seen:
                seen |= {delta, (n - delta) % n}
                pairs.append((j, k))
    met = set()
    for j, k in pairs:
        for i in range(n):
            met |= {(held[j, i], held[k, i]), (held[k, i], held[j, i])}
    assert len(met) == n * n
    return held, pairs


def pack_kernel(groups, cap, group_size, plane_ref, dest_ref, emb_ref, place_ref, *chunk_refs):
    rows_dev = emb_ref.shape[0]
    dest = dest_ref[...]
    group, place = jnp.zeros_like(dest), dest
    for g in range(1, groups):
        above = dest >= g * group_size
        group += above.astype(jnp.int32)
        place -= jnp.where(above, group_size, 0)
    group = jnp.bitwise_xor(group, plane_ref[0])
    pad = -(-groups // 16) * 16
    member = lax.broadcasted_iota(jnp.int32, (pad, rows_dev), 0) == group
    earlier = lax.broadcasted_iota(jnp.int32, (rows_dev, rows_dev), 0) < lax.broadcasted_iota(
        jnp.int32, (rows_dev, rows_dev), 1
    )
    before = jnp.dot(member.astype(jnp.bfloat16), earlier.astype(jnp.bfloat16), preferred_element_type=jnp.float32)
    rank = jnp.sum(jnp.where(member, before, 0.0), axis=0, keepdims=True).astype(jnp.int32)
    slot = jnp.where(rank < cap, group * cap + rank, groups * cap)
    pick = (lax.broadcasted_iota(jnp.int32, (groups * cap, rows_dev), 0) == slot).astype(jnp.bfloat16)
    x = emb_ref[...]
    unit = (x * lax.rsqrt(jnp.sum(x * x, axis=1, keepdims=True) + 1e-06)).astype(jnp.bfloat16)
    for k, ref in enumerate(chunk_refs):
        chunk = jnp.dot(pick[k * cap : (k + 1) * cap], unit, preferred_element_type=jnp.float32)
        ref[...] = chunk.astype(jnp.bfloat16)
    high = lax.shift_right_logical(place, 7)
    low = jnp.bitwise_and(place, 127)
    kind = lax.broadcasted_iota(jnp.int32, (16, rows_dev), 0)
    facts = jnp.where(kind == 0, high, jnp.where(kind == 1, low, jnp.where(kind == 2, 1, 0)))
    facts = facts.astype(jnp.float32).astype(jnp.bfloat16)
    got = lax.dot_general(facts, pick, NT, preferred_element_type=jnp.float32).astype(jnp.int32)
    there = got[2:3, :] > 0
    place_ref[...] = jnp.where(there, got[0:1, :] * 128 + got[1:2, :], group_size)


def diagonal(n):
    return lax.broadcasted_iota(jnp.int32, (n, n), 0) == lax.broadcasted_iota(jnp.int32, (n, n), 1)


def as_column(row):
    return jnp.max(jnp.where(diagonal(row.shape[1]), row, -2.0), axis=1, keepdims=True)


class Best:
    def __init__(self, start):
        self.row, self.column = start, None

    def add_row(self, row):
        self.row = jnp.maximum(self.row, row)

    def add_column(self, column):
        self.column = column if self.column is None else jnp.maximum(self.column, column)

    def as_row(self):
        if self.column is None:
            return self.row
        eye = diagonal(self.column.shape[0])
        return jnp.maximum(self.row, jnp.max(jnp.where(eye, self.column, -1.0), axis=0, keepdims=True))


def similar(left, right, left_label, right_label, shift=None):
    sims = lax.dot_general(left, right, NT, preferred_element_type=jnp.float32)
    keep = left_label == right_label
    if shift is not None:
        keep &= lax.broadcasted_iota(jnp.int32, sims.shape, 0) != lax.broadcasted_iota(jnp.int32, sims.shape, 1) + shift
    return jnp.where(keep, sims, -1.0)


def row_max(sims):
    return jnp.max(sims, axis=1, keepdims=True)


def column_max(sims):
    return jnp.max(sims, axis=0, keepdims=True)


def loader(chunks, count, blocks, sems):
    number = len(chunks) // count
    cap = chunks[0].shape[0]

    def copy(j, k):
        return pltpu.make_async_copy(chunks[j * number + k], blocks.at[j, pl.ds(k * cap, cap)], sems.at[j, k])

    for j, k in itertools.product(range(count), range(number)):
        copy(j, k).start()
    here = set()

    def need(*wanted):
        for j in sorted(set(wanted) - here):
            for k in range(number):
                copy(j, k).wait()
            here.add(j)

    return need


def early_kernel(pairs, count, early, *refs):
    *chunks, label_ref, last_label_ref, out_ref, label_col_ref, blocks, sems = refs
    need = loader(chunks, count, blocks, sems)
    for j in range(count):
        if any(j == left for left, _ in pairs):
            label_col_ref[:early, j : j + 1] = as_column(label_ref[j : j + 1, :])
        label_col_ref[early:, j : j + 1] = as_column(last_label_ref[j : j + 1, :])
    best = [Best(jnp.full((1, early), -1.0, jnp.float32)) for _ in range(count)]
    for j, k in pairs:
        need(j, k)
        sims = similar(
            blocks[j, :early],
            blocks[k, :early],
            label_col_ref[:early, j : j + 1],
            label_ref[k : k + 1, :],
            0 if j == k else None,
        )
        best[k].add_row(column_max(sims))
        if j != k:
            best[j].add_column(row_max(sims))
    for j in range(count):
        out_ref[j : j + 1, :] = best[j].as_row()


def late_kernel(pairs, count, group_size, *refs):
    plane_ref, *chunks, best_ref, place_ref, last_place_ref, label_ref, label_col_ref, out_ref, blocks, sems = refs
    need = loader(chunks, count, blocks, sems)
    first = best_ref.shape[1]
    rest = blocks.shape[1] - first
    early = [Best(best_ref[j : j + 1, :]) for j in range(count)]
    late = [Best(jnp.full((1, rest), -1.0, jnp.float32)) for _ in range(count)]
    for j, k in pairs:
        need(j, k)
        sims = similar(
            blocks[k, first:],
            blocks[j],
            label_col_ref[first:, k : k + 1],
            label_ref[j : j + 1, :],
            -first if j == k else None,
        )
        row = column_max(sims)
        early[j].add_row(row[:, :first])
        late[j].add_row(row[:, first:])
        late[k].add_column(row_max(sims))
        if j != k:
            sims = similar(
                blocks[j, first:],
                blocks[k, :first],
                label_col_ref[first:, j : j + 1],
                label_ref[k : k + 1, :first],
            )
            early[k].add_row(column_max(sims))
            late[j].add_column(row_max(sims))
    tall = group_size // 128
    pieces = [(early[j], place_ref[j : j + 1, :]) for j in range(count)]
    pieces += [(late[j], last_place_ref[j : j + 1, :]) for j in range(count)]
    spread = jnp.zeros((4 * tall, 128), jnp.float32)
    for best, place in pieces:
        best = best.as_row()
        slots = best.shape[1]
        high = lax.broadcasted_iota(jnp.int32, (tall, slots), 0) == lax.shift_right_logical(place, 7)
        low = lax.broadcasted_iota(jnp.int32, (128, slots), 0) == jnp.bitwise_and(place, 127)
        parts, rest = [], best
        for _ in range(3):
            part = rest.astype(jnp.bfloat16).astype(jnp.float32)
            rest = rest - part
            parts.append(part)
        parts.append(jnp.ones_like(best))
        stack = jnp.concatenate([jnp.where(high, part, 0.0) for part in parts], axis=0).astype(jnp.bfloat16)
        spread += lax.dot_general(stack, low.astype(jnp.bfloat16), NT, preferred_element_type=jnp.float32)
    value = spread[:tall] + spread[tall : 2 * tall] + spread[2 * tall : 3 * tall]
    value = jnp.where(spread[3 * tall :] > 0.5, value, -1.0)
    for r in range(out_ref.shape[0]):
        out_ref[r] = jnp.where(plane_ref[0] == r, value, -1.0)


def best_matches(cap, embeddings, dest_pos, cluster_ids):
    n_row, n_col = lax.axis_size("row"), lax.axis_size("col")
    devs = n_row * n_col
    groups, wide = n_row, n_col // n_row
    rows_dev, width = embeddings.shape
    group_size = rows_dev * n_col
    slots = groups * cap
    held, pairs = plane_plan(n_row, wide)
    count = len(held)

    assert groups & (groups - 1) == 0
    row, col = lax.axis_index("row"), lax.axis_index("col")
    plane, index = col // wide, row * wide + col % wide

    def device(i, h):
        return (i // wide) * n_col + h * wide + i % wide

    planes = [(i, h) for h in range(groups) for i in range(n_row * wide)]
    dest_row = dest_pos.reshape(1, rows_dev)
    plane_ref = plane.astype(jnp.int32).reshape(1)
    place, *parts = pl.pallas_call(
        functools.partial(pack_kernel, groups, cap, group_size),
        out_shape=[
            jax.ShapeDtypeStruct((1, slots), jnp.int32),
            *[jax.ShapeDtypeStruct((cap, width), jnp.bfloat16)] * groups,
        ],
        in_specs=[pl.BlockSpec(memory_space=pltpu.SMEM), VMEM, VMEM],
        out_specs=[VMEM] * (1 + groups),
        compiler_params=kernel_params(20),
    )(plane_ref, dest_row, embeddings)

    def across(part, k):
        return lax.ppermute(part, AXES, [(device(i, h ^ k), device(i, h)) for i, h in planes])

    def inside(part, j):
        return lax.ppermute(part, AXES, [(device(int(held[j, i]), h), device(i, h)) for i, h in planes])

    def after(values, *done):
        return lax.optimization_barrier((values, done))[0]

    own = [parts[0]] + [across(parts[k], k) for k in range(1, min(3, groups))]
    near = inside(own[0], 1)
    rounds = [[near] + [inside(after(own[0], near), j) for j in range(2, count)]]
    rest = after([parts[k] for k in range(3, groups)], near)

    own += [across(part, k) for k, part in zip(range(3, groups), rest)]
    for k in range(1, groups - 1):
        part = after(own[k], *rounds[0]) if k == 1 else after(own[k], rounds[-1][0], *rounds[-2])
        near = after(part, own[k + 1]) if k > 1 else part
        rounds.append([inside(near, 1), *[inside(part, j) for j in range(2, count)]])

    last = after(own[-1], *rounds[-2])
    rounds.append([inside(after(last, rounds[-1][0]), 1), *[inside(last, j) for j in range(2, count)]])
    place = after(place, rounds[1][0])

    planes_i = jnp.arange(groups, dtype=jnp.int32)
    swap = (planes_i[:, None] ^ planes_i[None, :]) == plane

    def by_plane(array):
        return jnp.sum(jnp.where(swap[:, :, None], array[None, :, :], 0), axis=1)

    levels = jnp.arange(LEVELS, dtype=jnp.int32)
    counts = jnp.sum((cluster_ids.reshape(1, rows_dev) <= levels[:, None]).astype(jnp.int32), axis=1)
    target_group = dest_pos // group_size
    most = jnp.max(jnp.sum((target_group[None, :] == jnp.arange(groups)[:, None]).astype(jnp.int32), axis=1))
    tail = jnp.concatenate([counts, (most > cap).astype(jnp.int32).reshape(1)])
    length = -(-(cap + LEVELS + 1) // 128) * 128
    facts = jnp.concatenate(
        [
            by_plane(place.reshape(groups, cap)),
            jnp.broadcast_to(tail[None, :], (groups, LEVELS + 1)),
            jnp.zeros((groups, length - cap - LEVELS - 1), jnp.int32),
        ],
        axis=1,
    )
    facts = jnp.broadcast_to(facts[None, :, None, :], (n_row, groups, wide, length)).reshape(devs, length)
    facts = lax.all_to_all(facts, AXES, split_axis=0, concat_axis=0, tiled=True)
    over = jnp.max(facts[:, cap + LEVELS]) > 0
    facts = facts.reshape(n_row, groups, wide, length)

    in_plane = (jnp.arange(n_row, dtype=jnp.int32) == plane).astype(jnp.int32)
    ends = jnp.sum(facts[..., cap : cap + LEVELS] * in_plane[:, None, None, None], axis=(0, 1, 2))
    places = by_plane(facts[..., :cap].transpose(1, 0, 2, 3).reshape(groups, n_row * wide * cap))
    places = places.reshape(groups, n_row * wide, cap).transpose(1, 0, 2).reshape(n_row * wide, slots)
    mine = jnp.sum(
        jnp.where(jnp.arange(n_row * wide)[None, :] == index, jnp.asarray(held, jnp.int32), 0), axis=1
    )
    mine = (mine[:, None] == jnp.arange(n_row * wide)[None, :]).astype(jnp.int32)
    places = jnp.sum(mine[:, :, None] * places[None, :, :], axis=1)
    labels = jnp.sum((places[:, None, :] >= ends[None, :, None]).astype(jnp.int32), axis=1)
    labels = jnp.where(places < group_size, labels, -1).astype(jnp.float32)

    early = (slots - cap) // 256 * 256
    label, last_label = labels[:, :early], labels[:, early:]
    blocks = [own] + [[moved[j - 1] for moved in rounds] for j in range(1, count)]
    any_space = pl.BlockSpec(memory_space=pltpu.HBM)
    area = 4 * slots * slots

    def scratch(number):
        return [
            pltpu.VMEM((count, number * cap, width), jnp.bfloat16),
            pltpu.SemaphoreType.DMA((count, number)),
        ]

    limit = 8 + (2 * count * slots * width + 5 * area) // 2**20
    first_best, label_cols = pl.pallas_call(
        functools.partial(early_kernel, pairs, count, early),
        out_shape=[
            jax.ShapeDtypeStruct((count, early), jnp.float32),
            jax.ShapeDtypeStruct((slots, count), jnp.float32),
        ],
        in_specs=[any_space] * (count * (groups - 1)) + [VMEM] * 2,
        out_specs=[VMEM] * 2,
        scratch_shapes=scratch(groups - 1),
        compiler_params=kernel_params(limit),
        cost_estimate=pl.CostEstimate(
            flops=2 * len(pairs) * early * early * width, bytes_accessed=2 * count * early * width, transcendentals=0
        ),
    )(*[part for block in blocks for part in block[:-1]], label, last_label)
    best = pl.pallas_call(
        functools.partial(late_kernel, pairs, count, group_size),
        out_shape=jax.ShapeDtypeStruct((n_row, group_size // 128, 128), jnp.float32),
        in_specs=[pl.BlockSpec(memory_space=pltpu.SMEM)] + [any_space] * (count * groups) + [VMEM] * 5,
        out_specs=VMEM,
        scratch_shapes=scratch(groups),
        compiler_params=kernel_params(limit),
    )(
        plane_ref,
        *itertools.chain(*blocks),
        first_best,
        places[:, :early],
        places[:, early:],
        labels,
        label_cols,
    )

    best = lax.all_to_all(best.reshape(devs, -1, 128), AXES, split_axis=0, concat_axis=0, tiled=True)
    return jnp.max(best, axis=0).reshape(1, rows_dev), over


def shards(embeddings, dest_pos, cluster_ids):
    n_row, n_col = lax.axis_size("row"), lax.axis_size("col")
    rows_dev = embeddings.shape[0]
    devs = n_row * n_col
    most = min(rows_dev, n_col * max(4, 2 * rows_dev // devs))
    usual = min(most, -(-(rows_dev // n_row) * 11 // 8 // 16) * 16)
    args = (embeddings, dest_pos, cluster_ids)
    best, over = best_matches(usual, *args)
    if usual == most:
        return best
    return lax.cond(over, lambda: best_matches(most, *args)[0], lambda: best)


def solution(mesh):
    return jax.shard_map(
        shards,
        mesh=mesh,
        in_specs=(P(("row", "col"), None), P(("row", "col")), P("row", "col")),
        out_specs=P("row", "col"),
        check_vma=False,
    )
```

```python
import functools
import itertools

import jax
import jax.numpy as jnp
import numpy as np
from jax import lax
from jax.experimental import pallas as pl
from jax.experimental.pallas import tpu as pltpu
from jax.sharding import PartitionSpec as P

AXES = ("row", "col")
LEVELS = 16
NT = (((1,), (1,)), ((), ()))
VMEM = pl.BlockSpec(memory_space=pltpu.VMEM)


def kernel_params(mebibytes):
    return pltpu.CompilerParams(vmem_limit_bytes=mebibytes * 2**20)


def plane_plan(n_row, wide):
    n = n_row * wide
    if n_row == 4 and wide == 2:
        chips = [(0, 0), (0, 1), (1, 1), (1, 0)]

        def dev(chip, core):
            x, y = chips[chip % 4]
            return (x * 2 + core) * wide + y

        held = np.zeros((4, n), np.int64)
        for chip, core in itertools.product(range(4), range(2)):
            i = dev(chip, core)
            crossed = 1 - core if chip in (1, 2) else core
            held[:, i] = i, dev(chip, 1 - core), dev(chip + 1, core), dev(chip + 3, crossed)
        pairs = [(0, 0), (0, 1), (0, 2), (1, 2), (2, 3)]
    else:
        def covered(cover):
            return {(b - a) % n for a in cover for b in cover}

        size = 1
        while True:
            found = [c for c in itertools.combinations(range(n), size) if c[0] == 0 and len(covered(c)) == n]
            if found:
                break
            size += 1
        cover = found[0]
        held = (np.arange(n)[None, :] + np.array(cover)[:, None]) % n
        pairs, seen = [], set()
        for j, k in itertools.combinations_with_replacement(range(size), 2):
            delta = (cover[k] - cover[j]) % n
            if delta not in seen:
                seen |= {delta, (n - delta) % n}
                pairs.append((j, k))
    met = set()
    for j, k in pairs:
        for i in range(n):
            met |= {(held[j, i], held[k, i]), (held[k, i], held[j, i])}
    assert len(met) == n * n
    return held, pairs


def pack_kernel(groups, cap, group_size, plane_ref, dest_ref, emb_ref, place_ref, *chunk_refs):
    rows_dev = emb_ref.shape[0]
    dest = dest_ref[...]
    group, place = jnp.zeros_like(dest), dest
    for g in range(1, groups):
        above = dest >= g * group_size
        group += above.astype(jnp.int32)
        place -= jnp.where(above, group_size, 0)
    group = jnp.bitwise_xor(group, plane_ref[0])
    pad = -(-groups // 16) * 16
    member = lax.broadcasted_iota(jnp.int32, (pad, rows_dev), 0) == group
    earlier = lax.broadcasted_iota(jnp.int32, (rows_dev, rows_dev), 0) < lax.broadcasted_iota(
        jnp.int32, (rows_dev, rows_dev), 1
    )
    before = jnp.dot(member.astype(jnp.bfloat16), earlier.astype(jnp.bfloat16), preferred_element_type=jnp.float32)
    rank = jnp.sum(jnp.where(member, before, 0.0), axis=0, keepdims=True).astype(jnp.int32)
    slot = jnp.where(rank < cap, group * cap + rank, groups * cap)
    pick = (lax.broadcasted_iota(jnp.int32, (groups * cap, rows_dev), 0) == slot).astype(jnp.bfloat16)
    x = emb_ref[...]
    unit = (x * lax.rsqrt(jnp.sum(x * x, axis=1, keepdims=True) + 1e-06)).astype(jnp.bfloat16)
    for k, ref in enumerate(chunk_refs):
        chunk = jnp.dot(pick[k * cap : (k + 1) * cap], unit, preferred_element_type=jnp.float32)
        ref[...] = chunk.astype(jnp.bfloat16)
    high = lax.shift_right_logical(place, 7)
    low = jnp.bitwise_and(place, 127)
    kind = lax.broadcasted_iota(jnp.int32, (16, rows_dev), 0)
    facts = jnp.where(kind == 0, high, jnp.where(kind == 1, low, jnp.where(kind == 2, 1, 0)))
    facts = facts.astype(jnp.float32).astype(jnp.bfloat16)
    got = lax.dot_general(facts, pick, NT, preferred_element_type=jnp.float32).astype(jnp.int32)
    there = got[2:3, :] > 0
    place_ref[...] = jnp.where(there, got[0:1, :] * 128 + got[1:2, :], group_size)


def diagonal(n):
    return lax.broadcasted_iota(jnp.int32, (n, n), 0) == lax.broadcasted_iota(jnp.int32, (n, n), 1)


def as_column(row):
    return jnp.max(jnp.where(diagonal(row.shape[1]), row, -2.0), axis=1, keepdims=True)


class Best:
    def __init__(self, start):
        self.row, self.column = start, None

    def add_row(self, row):
        self.row = jnp.maximum(self.row, row)

    def add_column(self, column):
        self.column = column if self.column is None else jnp.maximum(self.column, column)

    def as_row(self):
        if self.column is None:
            return self.row
        eye = diagonal(self.column.shape[0])
        return jnp.maximum(self.row, jnp.max(jnp.where(eye, self.column, -1.0), axis=0, keepdims=True))


def similar(left, right, left_label, right_label, shift=None):
    sims = lax.dot_general(left, right, NT, preferred_element_type=jnp.float32)
    keep = left_label == right_label
    if shift is not None:
        keep &= lax.broadcasted_iota(jnp.int32, sims.shape, 0) != lax.broadcasted_iota(jnp.int32, sims.shape, 1) + shift
    return jnp.where(keep, sims, -1.0)


def row_max(sims):
    return jnp.max(sims, axis=1, keepdims=True)


def column_max(sims):
    return jnp.max(sims, axis=0, keepdims=True)


def loader(chunks, count, blocks, sems):
    number = len(chunks) // count
    cap = chunks[0].shape[0]

    def copy(j, k):
        return pltpu.make_async_copy(chunks[j * number + k], blocks.at[j, pl.ds(k * cap, cap)], sems.at[j, k])

    for j, k in itertools.product(range(count), range(number)):
        copy(j, k).start()
    here = set()

    def need(*wanted):
        for j in sorted(set(wanted) - here):
            for k in range(number):
                copy(j, k).wait()
            here.add(j)

    return need


def early_kernel(pairs, count, early, *refs):
    *chunks, label_ref, last_label_ref, out_ref, label_col_ref, blocks, sems = refs
    need = loader(chunks, count, blocks, sems)
    for j in range(count):
        if any(j == left for left, _ in pairs):
            label_col_ref[:early, j : j + 1] = as_column(label_ref[j : j + 1, :])
        label_col_ref[early:, j : j + 1] = as_column(last_label_ref[j : j + 1, :])
    best = [Best(jnp.full((1, early), -1.0, jnp.float32)) for _ in range(count)]
    for j, k in pairs:
        need(j, k)
        sims = similar(
            blocks[j, :early],
            blocks[k, :early],
            label_col_ref[:early, j : j + 1],
            label_ref[k : k + 1, :],
            0 if j == k else None,
        )
        best[k].add_row(column_max(sims))
        if j != k:
            best[j].add_column(row_max(sims))
    for j in range(count):
        out_ref[j : j + 1, :] = best[j].as_row()


def late_kernel(pairs, count, group_size, *refs):
    plane_ref, *chunks, best_ref, place_ref, last_place_ref, label_ref, label_col_ref, out_ref, blocks, sems = refs
    need = loader(chunks, count, blocks, sems)
    first = best_ref.shape[1]
    rest = blocks.shape[1] - first
    early = [Best(best_ref[j : j + 1, :]) for j in range(count)]
    late = [Best(jnp.full((1, rest), -1.0, jnp.float32)) for _ in range(count)]
    for j, k in pairs:
        need(j, k)
        sims = similar(
            blocks[k, first:],
            blocks[j],
            label_col_ref[first:, k : k + 1],
            label_ref[j : j + 1, :],
            -first if j == k else None,
        )
        row = column_max(sims)
        early[j].add_row(row[:, :first])
        late[j].add_row(row[:, first:])
        late[k].add_column(row_max(sims))
        if j != k:
            sims = similar(
                blocks[j, first:],
                blocks[k, :first],
                label_col_ref[first:, j : j + 1],
                label_ref[k : k + 1, :first],
            )
            early[k].add_row(column_max(sims))
            late[j].add_column(row_max(sims))
    tall = group_size // 128
    pieces = [(early[j], place_ref[j : j + 1, :]) for j in range(count)]
    pieces += [(late[j], last_place_ref[j : j + 1, :]) for j in range(count)]
    spread = jnp.zeros((4 * tall, 128), jnp.float32)
    for best, place in pieces:
        best = best.as_row()
        slots = best.shape[1]
        high = lax.broadcasted_iota(jnp.int32, (tall, slots), 0) == lax.shift_right_logical(place, 7)
        low = lax.broadcasted_iota(jnp.int32, (128, slots), 0) == jnp.bitwise_and(place, 127)
        parts, rest = [], best
        for _ in range(3):
            part = rest.astype(jnp.bfloat16).astype(jnp.float32)
            rest = rest - part
            parts.append(part)
        parts.append(jnp.ones_like(best))
        stack = jnp.concatenate([jnp.where(high, part, 0.0) for part in parts], axis=0).astype(jnp.bfloat16)
        spread += lax.dot_general(stack, low.astype(jnp.bfloat16), NT, preferred_element_type=jnp.float32)
    value = spread[:tall] + spread[tall : 2 * tall] + spread[2 * tall : 3 * tall]
    value = jnp.where(spread[3 * tall :] > 0.5, value, -1.0)
    for r in range(out_ref.shape[0]):
        out_ref[r] = jnp.where(plane_ref[0] == r, value, -1.0)


def best_matches(cap, embeddings, dest_pos, cluster_ids):
    n_row, n_col = lax.axis_size("row"), lax.axis_size("col")
    devs = n_row * n_col
    groups, wide = n_row, n_col // n_row
    rows_dev, width = embeddings.shape
    group_size = rows_dev * n_col
    slots = groups * cap
    held, pairs = plane_plan(n_row, wide)
    count = len(held)

    assert groups & (groups - 1) == 0
    row, col = lax.axis_index("row"), lax.axis_index("col")
    plane, index = col // wide, row * wide + col % wide

    def device(i, h):
        return (i // wide) * n_col + h * wide + i % wide

    planes = [(i, h) for h in range(groups) for i in range(n_row * wide)]
    dest_row = dest_pos.reshape(1, rows_dev)
    plane_ref = plane.astype(jnp.int32).reshape(1)
    place, *parts = pl.pallas_call(
        functools.partial(pack_kernel, groups, cap, group_size),
        out_shape=[
            jax.ShapeDtypeStruct((1, slots), jnp.int32),
            *[jax.ShapeDtypeStruct((cap, width), jnp.bfloat16)] * groups,
        ],
        in_specs=[pl.BlockSpec(memory_space=pltpu.SMEM), VMEM, VMEM],
        out_specs=[VMEM] * (1 + groups),
        compiler_params=kernel_params(20),
    )(plane_ref, dest_row, embeddings)

    def across(part, k):
        return lax.ppermute(part, AXES, [(device(i, h ^ k), device(i, h)) for i, h in planes])

    def inside(part, j):
        return lax.ppermute(part, AXES, [(device(int(held[j, i]), h), device(i, h)) for i, h in planes])

    def after(values, *done):
        return lax.optimization_barrier((values, done))[0]

    own = [parts[0]] + [across(parts[k], k) for k in range(1, min(3, groups))]
    near = inside(own[0], 1)
    rounds = [[near] + [inside(after(own[0], near), j) for j in range(2, count)]]
    rest = [parts[k] for k in range(3, groups)]

    own += [across(part, k) for k, part in zip(range(3, groups), rest)]
    for k in range(1, groups - 1):
        part = after(own[k], *rounds[0]) if k == 1 else after(own[k], rounds[-1][0], *rounds[-2])
        near = after(part, own[k + 1]) if k > 1 else part
        rounds.append([inside(near, 1), *[inside(part, j) for j in range(2, count)]])

    last = after(own[-1], *rounds[-2])
    rounds.append([inside(after(last, rounds[-1][0]), 1), *[inside(last, j) for j in range(2, count)]])
    place = after(place, rounds[1][0])

    planes_i = jnp.arange(groups, dtype=jnp.int32)
    swap = (planes_i[:, None] ^ planes_i[None, :]) == plane

    def by_plane(array):
        return jnp.sum(jnp.where(swap[:, :, None], array[None, :, :], 0), axis=1)

    levels = jnp.arange(LEVELS, dtype=jnp.int32)
    counts = jnp.sum((cluster_ids.reshape(1, rows_dev) <= levels[:, None]).astype(jnp.int32), axis=1)
    target_group = dest_pos // group_size
    most = jnp.max(jnp.sum((target_group[None, :] == jnp.arange(groups)[:, None]).astype(jnp.int32), axis=1))
    tail = jnp.concatenate([counts, (most > cap).astype(jnp.int32).reshape(1)])
    length = -(-(cap + LEVELS + 1) // 128) * 128
    facts = jnp.concatenate(
        [
            by_plane(place.reshape(groups, cap)),
            jnp.broadcast_to(tail[None, :], (groups, LEVELS + 1)),
            jnp.zeros((groups, length - cap - LEVELS - 1), jnp.int32),
        ],
        axis=1,
    )
    facts = jnp.broadcast_to(facts[None, :, None, :], (n_row, groups, wide, length)).reshape(devs, length)
    facts = lax.all_to_all(facts, AXES, split_axis=0, concat_axis=0, tiled=True)
    over = jnp.max(facts[:, cap + LEVELS]) > 0
    facts = facts.reshape(n_row, groups, wide, length)

    in_plane = (jnp.arange(n_row, dtype=jnp.int32) == plane).astype(jnp.int32)
    ends = jnp.sum(facts[..., cap : cap + LEVELS] * in_plane[:, None, None, None], axis=(0, 1, 2))
    places = by_plane(facts[..., :cap].transpose(1, 0, 2, 3).reshape(groups, n_row * wide * cap))
    places = places.reshape(groups, n_row * wide, cap).transpose(1, 0, 2).reshape(n_row * wide, slots)
    mine = jnp.sum(
        jnp.where(jnp.arange(n_row * wide)[None, :] == index, jnp.asarray(held, jnp.int32), 0), axis=1
    )
    mine = (mine[:, None] == jnp.arange(n_row * wide)[None, :]).astype(jnp.int32)
    places = jnp.sum(mine[:, :, None] * places[None, :, :], axis=1)
    labels = jnp.sum((places[:, None, :] >= ends[None, :, None]).astype(jnp.int32), axis=1)
    labels = jnp.where(places < group_size, labels, -1).astype(jnp.float32)

    early = (slots - cap) // 256 * 256
    label, last_label = labels[:, :early], labels[:, early:]
    blocks = [own] + [[moved[j - 1] for moved in rounds] for j in range(1, count)]
    any_space = pl.BlockSpec(memory_space=pltpu.HBM)
    area = 4 * slots * slots

    def scratch(number):
        return [
            pltpu.VMEM((count, number * cap, width), jnp.bfloat16),
            pltpu.SemaphoreType.DMA((count, number)),
        ]

    limit = 8 + (2 * count * slots * width + 5 * area) // 2**20
    first_best, label_cols = pl.pallas_call(
        functools.partial(early_kernel, pairs, count, early),
        out_shape=[
            jax.ShapeDtypeStruct((count, early), jnp.float32),
            jax.ShapeDtypeStruct((slots, count), jnp.float32),
        ],
        in_specs=[any_space] * (count * (groups - 1)) + [VMEM] * 2,
        out_specs=[VMEM] * 2,
        scratch_shapes=scratch(groups - 1),
        compiler_params=kernel_params(limit),
        cost_estimate=pl.CostEstimate(
            flops=2 * len(pairs) * early * early * width, bytes_accessed=2 * count * early * width, transcendentals=0
        ),
    )(*[part for block in blocks for part in block[:-1]], label, last_label)
    best = pl.pallas_call(
        functools.partial(late_kernel, pairs, count, group_size),
        out_shape=jax.ShapeDtypeStruct((n_row, group_size // 128, 128), jnp.float32),
        in_specs=[pl.BlockSpec(memory_space=pltpu.SMEM)] + [any_space] * (count * groups) + [VMEM] * 5,
        out_specs=VMEM,
        scratch_shapes=scratch(groups),
        compiler_params=kernel_params(limit),
    )(
        plane_ref,
        *itertools.chain(*blocks),
        first_best,
        places[:, :early],
        places[:, early:],
        labels,
        label_cols,
    )

    best = lax.all_to_all(best.reshape(devs, -1, 128), AXES, split_axis=0, concat_axis=0, tiled=True)
    return jnp.max(best, axis=0).reshape(1, rows_dev), over


def shards(embeddings, dest_pos, cluster_ids):
    n_row, n_col = lax.axis_size("row"), lax.axis_size("col")
    rows_dev = embeddings.shape[0]
    devs = n_row * n_col
    most = min(rows_dev, n_col * max(4, 2 * rows_dev // devs))
    usual = min(most, -(-(rows_dev // n_row) * 11 // 8 // 16) * 16)
    args = (embeddings, dest_pos, cluster_ids)
    best, over = best_matches(usual, *args)
    if usual == most:
        return best
    return lax.cond(over, lambda: best_matches(most, *args)[0], lambda: best)


def solution(mesh):
    return jax.shard_map(
        shards,
        mesh=mesh,
        in_specs=(P(("row", "col"), None), P(("row", "col")), P("row", "col")),
        out_specs=P("row", "col"),
        check_vma=False,
    )
```
